128 devices in a mesh: node: 16 (over x_hi, z, core), feat: 8 (over x_lo, y).
Axes of the slice: x: 4 (x_hi: 2, x_lo: 2; x = x_hi * 2 + x_lo), y: 4, z: 4, core: 2. Of those that a mesh axis runs over, the one named last changes fastest.
Arguments:
- features: bfloat16 [128, 98304], P('feat', 'node'), may hold values from -6 to 6
- weight: bfloat16 [128, 256], P('feat'), may hold values from -0.5 to 0.5
- bias: float32 [256], P('feat'), may hold values from -3 to 3
- block_values: bfloat16 [768, 12, 128, 128], P('node'), may hold values from -0.21875 to 0.21875
- block_cols: int32 [768, 12], P('node'), may hold values from 0 to 767
- block_counts: int32 [768], P('node'), may hold values from 1 to 12, as said below
- train_mask: int32 [98304], P('node'), may hold values 0 or 1
- cotangent: bfloat16 [256, 98304], P('feat', 'node'), may hold values from -6 to 6
Outputs:
- activation: bfloat16 [256, 98304], P('feat', 'node')
- grad_features: bfloat16 [128, 98304], P('feat', 'node')
- grad_weight: float32 [128, 256], P('feat')
The draws below stay inside these ranges and needn't reach their ends.
Inputs may be any that keep to these rules, and one draw needn't show every extreme that they name: `block_counts`: block row 0 has all 12 slots live.
All inputs are finite; a program needn't handle non-finite values. No bound on the sum of `train_mask` on one device may be relied on, other than what follows from the above.
Results may differ from the reference program's by a relative error of at most 0.022.
Values may be sent and summed in bfloat16 or wider, within the bound.
No kernel may reach another device: no remote copies, remote signals or barrier semaphores. Data moves between devices by JAX's collectives and lax.ppermute only.
A program may use at most 128 MiB of HBM per device.

```python
import jax
import jax.numpy as jnp
from jax import lax

FIN = 128
FOUT = 256
BLOCK_SIZE = 128
SLOTS = 12
BLOCK_DEV = 48
BLOCKS = 768
NODES = 98304
N_NODE = 16


def draw_block_counts(key, part):
    key = jax.random.fold_in(key, 7)
    key_level, key_rows = jax.random.split(key)
    level = jax.random.randint(key_level, (BLOCKS // BLOCK_DEV,), 3, SLOTS + 1)
    level_rows = jnp.repeat(level, BLOCK_DEV, total_repeat_length=BLOCKS)
    lowest = jnp.maximum(level_rows // 2, 1)
    counts = jax.random.randint(key_rows, (BLOCKS,), lowest, level_rows + 1)
    return counts.at[0].set(SLOTS).astype(jnp.int32)


def plant(array, rng, smallest, largest):
    index_at = [jax.random.randint(jax.random.fold_in(rng, axis), (), 0, length) for axis, length in enumerate(array.shape)]
    longest = array.shape.index(max(array.shape))
    next_to = index_at[:longest] + [(index_at[longest] + 1) % array.shape[longest]] + index_at[longest + 1:]
    return array.at[tuple(index_at)].set(smallest).at[tuple(next_to)].set(largest)


def shard_levels(own_key, extent, cuts, smallest, high):
    gain = 1.0
    for axis_at, parts in cuts:
        heights = jax.random.uniform(jax.random.fold_in(jax.random.fold_in(own_key, 6), axis_at), (parts,), jnp.float32, smallest / len(cuts), high / len(cuts))
        gain = gain * jnp.repeat(jnp.exp(heights), extent[axis_at] // parts).reshape((-1,) + (1,) * (len(extent) - 1 - axis_at))
    return gain


def bell_draw(key, dims, width, most, cuts=(), held_as=jnp.bfloat16):
    entries = jax.random.normal(key, dims, jnp.float32) * width
    if len(cuts) > 0:
        entries = shard_levels(key, dims, cuts, -0.22, 0.18) * entries
    return jnp.clip(entries, min=-most, max=most).astype(held_as)


def setup_inputs(seed: int = 0) -> dict:
    streams_of = jax.random.split(jax.random.key(seed), 9)
    return {
        "features": bell_draw(streams_of[0], (FIN, NODES), 1.0, 6.0, ((0, 8), (1, 16))),
        "weight": bell_draw(streams_of[1], (FIN, FOUT), FIN ** -0.5, 0.5, ((0, 8),)),
        "bias": bell_draw(streams_of[2], (FOUT,), 0.5, 3.0, ((0, 8),), jnp.float32),
        "block_values": bell_draw(streams_of[3], (BLOCKS, SLOTS, BLOCK_SIZE, BLOCK_SIZE), (64 * SLOTS) ** -0.5, 0.21875, ((0, 16),)),
        "block_cols": plant(jax.random.randint(streams_of[4], (BLOCKS, SLOTS), 0, BLOCKS), jax.random.fold_in(streams_of[4], 1), 0, BLOCKS - 1).astype(jnp.int32),
        "block_counts": draw_block_counts(jax.random.fold_in(streams_of[8], 71), 0),
        "train_mask": plant((jax.random.randint(streams_of[6], (NODES,), 0, 2) < 1).astype(jnp.int32), jax.random.fold_in(streams_of[6], 1), 0, 1),
        "cotangent": bell_draw(streams_of[7], (FOUT, NODES), 1.0, 6.0, ((0, 8), (1, 16))),
    }


def silu_slope(preact):
    sigma = jax.nn.sigmoid(preact)
    return sigma * (1.0 + preact * (1.0 - sigma))


def reference(features, weight, bias, block_values, block_cols, block_counts, train_mask, cotangent):
    feature_blocks = features.reshape(FIN, BLOCKS, BLOCK_SIZE)
    living = jnp.arange(SLOTS, dtype=jnp.int32)[None, :] < block_counts[:, None]
    group_values = block_values.reshape(N_NODE, BLOCK_DEV, SLOTS, BLOCK_SIZE, BLOCK_SIZE)
    group_columns = block_cols.reshape(N_NODE, BLOCK_DEV, SLOTS)
    group_living = living.reshape(N_NODE, BLOCK_DEV, SLOTS)

    def forward_group(packed):
        values_group, columns_group, living_group = packed
        picked = jnp.take(feature_blocks, columns_group, axis=1).astype(jnp.float32)
        picked = picked * living_group[None, :, :, None].astype(jnp.float32)
        return jnp.einsum("fnsk,nskm->nfm", picked, values_group.astype(jnp.float32))

    aggregate = lax.map(forward_group, (group_values, group_columns, group_living))
    mixed = aggregate.reshape(BLOCKS, FIN, BLOCK_SIZE).transpose(1, 0, 2).reshape(FIN, NODES).astype(jnp.bfloat16)
    preact = jnp.dot(weight.T, mixed, preferred_element_type=jnp.float32) + bias[:, None]
    activation = jax.nn.silu(preact).astype(jnp.bfloat16)
    grad_pre = (cotangent.astype(jnp.float32) * train_mask.astype(jnp.float32)[None, :] * silu_slope(preact)).astype(jnp.bfloat16)
    grad_weight = jnp.dot(mixed, grad_pre.T, preferred_element_type=jnp.float32)
    grad_mixed = jnp.dot(weight, grad_pre, preferred_element_type=jnp.float32).astype(jnp.bfloat16)
    grad_groups = grad_mixed.reshape(FIN, N_NODE, BLOCK_DEV, BLOCK_SIZE).transpose(1, 0, 2, 3)

    def backward_group(running, packed):
        grads_group, values_group, columns_group, living_group = packed
        contrib = jnp.einsum("fnm,nskm->nsfk", grads_group.astype(jnp.float32), values_group.astype(jnp.float32))
        contrib = contrib * living_group[:, :, None, None].astype(jnp.float32)
        contrib = contrib.reshape(BLOCK_DEV * SLOTS, FIN, BLOCK_SIZE)
        partial_value = jax.ops.segment_sum(contrib, columns_group.reshape(-1), num_segments=BLOCKS)
        return running + partial_value.astype(jnp.bfloat16).astype(jnp.float32), None

    grad_sum, _ = lax.scan(backward_group, jnp.zeros((BLOCKS, FIN, BLOCK_SIZE), jnp.float32),
                           (grad_groups, group_values, group_columns, group_living))
    grad_features = grad_sum.transpose(1, 0, 2).reshape(FIN, NODES).astype(jnp.bfloat16)
    return activation, grad_features, grad_weight
```

```python
import jax
import jax.numpy as jnp
from jax import lax
from jax.experimental import pallas as pl
from jax.experimental.pallas import tpu as pltpu
from jax.sharding import PartitionSpec as P

BF = jnp.bfloat16
F32 = jnp.float32
ANY = pl.BlockSpec(memory_space=pl.ANY)
SMEM = pl.BlockSpec(memory_space=pltpu.SMEM)
VMEM = pl.BlockSpec(memory_space=pltpu.VMEM)
STEPS = ((1, 2), (1, 1), (1, 3), (0, 2), (1, 0), (0, 1), (0, 3))
BLOCK = 128


def node_at(x, z, core):
    return (x * 4 + z) * 2 + core


def node_pairs(dx, dz, dcore=0):
    return [
        (node_at(x, z, c), node_at(x ^ dx, (z + dz) % 4, c ^ dcore))
        for x in range(2)
        for z in range(4)
        for c in range(2)
    ]


def node_near(dx, dz, dcore):
    me = lax.axis_index("node")
    x, z, c = me >> 3, (me >> 1) & 3, me & 1
    return ((x ^ dx) * 4 + ((z + dz) & 3)) * 2 + (c ^ dcore)


def place_of(column):
    group = lax.shift_right_logical(column * 21846, 20)
    return group, pl.multiple_of((column - group * 48) * BLOCK, BLOCK)


def params(mib):
    return pltpu.CompilerParams(vmem_limit_bytes=mib * 2**20)


def mix_kernel(cols, counts, values, cotangent, *rest):
    pieces, (out, held, sems) = rest[:16], rest[16:]
    step = pl.program_id(0)
    rows = values.shape[0]
    slots = values.shape[1]

    @pl.when(step == 0)
    def _():
        copies = []
        for k, (dx, dz) in enumerate(((0, 0),) + STEPS):
            for core in range(2):
                at = 2 * k + core
                copies.append(
                    pltpu.make_async_copy(
                        pieces[at], held.at[node_near(dx, -dz, core)], sems.at[at]
                    )
                )
        for copy in copies:
            copy.start()
        for copy in copies:
            copy.wait()

    for i in range(rows):
        r = step * rows + i
        count = counts[r]
        parts = []
        for s in range(slots):
            group, lane = place_of(cols[r * slots + s])
            block = held[group, :, pl.ds(lane, BLOCK)]
            parts.append(jnp.where(s < count, block, jnp.zeros_like(block)))
        picked = jnp.concatenate(parts, axis=1)
        total = jnp.dot(
            picked, values[i].reshape(slots * BLOCK, BLOCK), preferred_element_type=F32
        )
        out[0, :16, i * BLOCK : (i + 1) * BLOCK] = total.astype(BF)
    out[0, 16:, :] = cotangent[...]


def dense_kernel(both, weight, bias, mask, out):
    width = both.shape[2]
    mixed = both[:, :16, :].reshape(128, width)
    cotangent = both[:, 16:, :].reshape(256, width)
    kept = mask[:, pl.ds(pl.multiple_of(lax.axis_index("feat") * width, BLOCK), width)]
    preact = (
        lax.dot_general(weight[...], mixed, (((0,), (0,)), ((), ())), preferred_element_type=F32)
        + bias[...]
    )
    sigma = jax.nn.sigmoid(preact)
    activation = (preact * sigma).astype(BF).reshape(8, 32, width)
    slope = sigma * (1.0 + preact * (1.0 - sigma))
    grad_pre = (cotangent.astype(F32) * kept.astype(F32) * slope).astype(BF)
    grad_mixed = jnp.dot(weight[...], grad_pre, preferred_element_type=F32)
    grad_weight = lax.dot_general(
        mixed, grad_pre, (((1,), (1,)), ((), ())), preferred_element_type=F32
    )
    out[:, :, :width] = grad_mixed.astype(BF).reshape(8, 16, width)
    out[:, :, width : width + 256] = grad_weight.astype(BF).reshape(8, 16, 256)
    out[:, :, width + 256 : 2 * width + 256] = activation[:, :16]
    out[:, :, 2 * width + 256 :] = activation[:, 16:]


def spread_kernel(cols, counts, values, grads, activation, own, other, total, grad_w):
    step = pl.program_id(0)
    rows = values.shape[0]
    slots = values.shape[1]
    width = rows * BLOCK
    nodes = total.shape[2]

    @pl.when(step == 0)
    def _():
        total[...] = jnp.zeros_like(total)
        grad_w[...] = jnp.zeros_like(grad_w)

    activation[:16, :] = grads[0, :, width + 256 : 2 * width + 256]
    activation[16:, :] = grads[0, :, 2 * width + 256 :]
    grad_w[...] += grads[0, :, width : width + 256].astype(F32)

    for i in range(rows):
        r = step * rows + i
        count = counts[r]
        contrib = lax.dot_general(
            grads[0, :, i * BLOCK : (i + 1) * BLOCK],
            values[i].reshape(slots * BLOCK, BLOCK),
            (((1,), (1,)), ((), ())),
            preferred_element_type=F32,
        )
        for s in range(slots):
            group, lane = place_of(cols[r * slots + s])
            group = jnp.where(s < count, group, 16)
            total[group, :, pl.ds(lane, BLOCK)] += contrib[:, s * BLOCK : (s + 1) * BLOCK]

    @pl.when(step == pl.num_programs(0) - 1)
    def _():
        weight_part = grad_w[...].astype(BF)
        for k, (dx, dz) in enumerate(((0, 0),) + STEPS):
            for core, to in enumerate((own, other)):
                to[k, :, :nodes] = total[node_near(dx, dz, core)].astype(BF)
                to[k, :, nodes:] = weight_part


def pair_kernel(own, other, *outs):
    for k, out in enumerate(outs):
        out[...] = (own[k].astype(F32) + other[k].astype(F32)).astype(BF)


def local(features, weight, bias, block_values, block_cols, block_counts, train_mask, cotangent):
    block_dev, slots = block_values.shape[:2]
    fin, nodes = features.shape
    rows = block_dev // 8
    width = nodes // 8

    def shape(dims, kind=BF):
        return jax.ShapeDtypeStruct(dims, kind)

    whole_weight = lax.all_gather(weight, "feat", axis=0, tiled=True)
    whole_bias = lax.all_gather(bias, "feat", axis=0, tiled=True)[:, None]

    pieces = [features, lax.ppermute(features, "node", node_pairs(0, 0, 1))]
    for dx, dz in STEPS:
        piece = lax.ppermute(features, "node", node_pairs(dx, dz))
        pieces += [piece, lax.ppermute(piece, "node", node_pairs(0, 0, 1))]

    cols = block_cols.reshape(-1)
    values_spec = pl.BlockSpec((rows, slots, BLOCK, BLOCK), lambda i, *_: (i, 0, 0, 0))
    mixed = pl.pallas_call(
        mix_kernel,
        grid_spec=pltpu.PrefetchScalarGridSpec(
            num_scalar_prefetch=2,
            grid=(8,),
            in_specs=[values_spec, pl.BlockSpec((32, width), lambda i, *_: (0, i))] + [ANY] * 16,
            out_specs=pl.BlockSpec((1, 48, width), lambda i, *_: (i, 0, 0)),
            scratch_shapes=[
                pltpu.VMEM((16, fin, nodes), BF),
                pltpu.SemaphoreType.DMA((16,)),
            ],
        ),
        out_shape=shape((8, 48, width)),
        compiler_params=params(24),
        name="mix",
    )(cols, block_counts, block_values, cotangent, *pieces)

    both = lax.all_to_all(mixed, "feat", 0, 0, tiled=True)

    dense = pl.pallas_call(
        dense_kernel,
        in_specs=[VMEM] * 4,
        out_specs=VMEM,
        out_shape=shape((8, 16, 3 * width + 256)),
        compiler_params=params(24),
        name="dense",
    )(both, whole_weight, whole_bias, train_mask[None, :])

    grads = lax.all_to_all(dense, "feat", 0, 0, tiled=True)

    activation, own, other = pl.pallas_call(
        spread_kernel,
        grid_spec=pltpu.PrefetchScalarGridSpec(
            num_scalar_prefetch=2,
            grid=(8,),
            in_specs=[
                values_spec,
                pl.BlockSpec((1, 16, 3 * width + 256), lambda i, *_: (i, 0, 0)),
            ],
            out_specs=[
                pl.BlockSpec((32, width), lambda i, *_: (0, i)),
                pl.BlockSpec((8, 16, nodes + 256), lambda i, *_: (0, 0, 0)),
                pl.BlockSpec((8, 16, nodes + 256), lambda i, *_: (0, 0, 0)),
            ],
            scratch_shapes=[
                pltpu.VMEM((17, fin, nodes), F32),
                pltpu.VMEM((16, 256), F32),
            ],
        ),
        out_shape=[
            shape((32, nodes)),
            shape((8, 16, nodes + 256)),
            shape((8, 16, nodes + 256)),
        ],
        compiler_params=params(32),
        name="spread",
    )(cols, block_counts, block_values, grads)

    other = lax.ppermute(other, "node", node_pairs(0, 0, 1))
    sums = pl.pallas_call(
        pair_kernel,
        in_specs=[VMEM] * 2,
        out_specs=[VMEM] * 8,
        out_shape=[shape((16, nodes + 256))] * 8,
        compiler_params=params(24),
        name="pair",
    )(own, other)
    landed = [sums[0]]
    for (dx, dz), piece in zip(STEPS, sums[1:]):
        landed.append(lax.ppermute(piece, "node", node_pairs(dx, dz)))
    total = sum(piece.astype(F32) for piece in landed)
    return activation, total[:, :nodes].astype(BF), total[:, nodes:]


def solution(mesh):
    placed = (
        P("feat", "node"),
        P("feat", None),
        P("feat"),
        P("node", None, None, None),
        P("node", None),
        P("node"),
        P("node"),
        P("feat", "node"),
    )
    return jax.shard_map(
        local,
        mesh=mesh,
        in_specs=placed,
        out_specs=(P("feat", "node"), P("feat", "node"), P("feat", None)),
        check_vma=False,
    )
```

```python
import jax
import jax.numpy as jnp
from jax import lax
from jax.experimental import pallas as pl
from jax.experimental.pallas import tpu as pltpu
from jax.sharding import PartitionSpec as P

BF = jnp.bfloat16
F32 = jnp.float32
ANY = pl.BlockSpec(memory_space=pl.ANY)
SMEM = pl.BlockSpec(memory_space=pltpu.SMEM)
VMEM = pl.BlockSpec(memory_space=pltpu.VMEM)
STEPS = ((1, 2), (1, 1), (1, 3), (0, 2), (1, 0), (0, 1), (0, 3))
BLOCK = 128


def node_at(x, z, core):
    return (x * 4 + z) * 2 + core


def node_pairs(dx, dz, dcore=0):
    return [
        (node_at(x, z, c), node_at(x ^ dx, (z + dz) % 4, c ^ dcore))
        for x in range(2)
        for z in range(4)
        for c in range(2)
    ]


def node_near(dx, dz, dcore):
    me = lax.axis_index("node")
    x, z, c = me >> 3, (me >> 1) & 3, me & 1
    return ((x ^ dx) * 4 + ((z + dz) & 3)) * 2 + (c ^ dcore)


def place_of(column):
    group = lax.shift_right_logical(column * 21846, 20)
    return group, pl.multiple_of((column - group * 48) * BLOCK, BLOCK)


def params(mib):
    return pltpu.CompilerParams(vmem_limit_bytes=mib * 2**20)


def load_kernel(values, _, out, sems):
    count = sems.shape[0]
    rows = values.shape[0] // count
    copies = [
        pltpu.make_async_copy(
            values.at[pl.ds(i * rows, rows)], out.at[pl.ds(i * rows, rows)], sems.at[i]
        )
        for i in range(count)
    ]
    for copy in copies:
        copy.start()
    for copy in copies:
        copy.wait()


def mix_kernel(cols, counts, values, cotangent, weight, bias_rows, *rest):
    pieces, (out, held, sems) = rest[:16], rest[16:]
    slots = values.shape[1]
    chunks, _, _ = out.shape
    width = cotangent.shape[1] // chunks
    rows = values.shape[0] // chunks

    copies = []
    for k, (dx, dz) in enumerate(((0, 0),) + STEPS):
        for core in range(2):
            at = 2 * k + core
            copies.append(
                pltpu.make_async_copy(pieces[at], held.at[node_near(dx, -dz, core)], sems.at[at])
            )
    for copy in copies:
        copy.start()
    for j in range(chunks):
        out[j, :, width : 2 * width] = cotangent[:16, j * width : (j + 1) * width]
        out[j, :, 2 * width : 3 * width] = cotangent[16:, j * width : (j + 1) * width]
        out[j, :, 3 * width : 3 * width + 256] = weight[...]
        out[j, :, 3 * width + 256 :] = bias_rows[...]
    for copy in copies:
        copy.wait()

    @pl.loop(0, chunks)
    def _(j):
        for i in range(rows):
            r = j * rows + i
            count = counts[r]
            parts = []
            for s in range(slots):
                group, lane = place_of(cols[r, s])
                block = held[group, :, pl.ds(lane, BLOCK)]
                parts.append(jnp.where(s < count, block, jnp.zeros_like(block)))
            total = jnp.dot(
                jnp.concatenate(parts, axis=1),
                values[r].reshape(slots * BLOCK, BLOCK),
                preferred_element_type=F32,
            )
            out[j, :, i * BLOCK : (i + 1) * BLOCK] = total.astype(BF)


def dense_kernel(both, mask, out):
    width = mask.shape[1] // 8
    mixed = both[:, :, :width].reshape(128, width)
    cotangent = jnp.concatenate(
        [both[:, :, width : 2 * width], both[:, :, 2 * width : 3 * width]], axis=1
    ).reshape(256, width)
    weight = both[:, :, 3 * width : 3 * width + 256].reshape(128, 256)
    bias_rows = both[:, :, 3 * width + 256 :].reshape(128, 256)
    kept = mask[:, pl.ds(pl.multiple_of(lax.axis_index("feat") * width, BLOCK), width)]
    preact = lax.dot_general(
        jnp.concatenate([weight, bias_rows], axis=0),
        jnp.concatenate([mixed, jnp.ones_like(mixed)], axis=0),
        (((0,), (0,)), ((), ())),
        preferred_element_type=F32,
    )
    sigma = jax.nn.sigmoid(preact)
    activation = (preact * sigma).astype(BF).reshape(8, 32, width)
    slope = sigma * (1.0 + preact * (1.0 - sigma))
    grad_pre = (cotangent.astype(F32) * kept.astype(F32) * slope).astype(BF)
    grad_mixed = jnp.dot(weight, grad_pre, preferred_element_type=F32)
    grad_weight = lax.dot_general(
        mixed, grad_pre, (((1,), (1,)), ((), ())), preferred_element_type=F32
    )
    out[:, :, :width] = grad_mixed.astype(BF).reshape(8, 16, width)
    out[:, :, width : width + 256] = grad_weight.astype(BF).reshape(8, 16, 256)
    out[:, :, width + 256 : 2 * width + 256] = activation[:, :16]
    out[:, :, 2 * width + 256 :] = activation[:, 16:]


def spread_kernel(cols, counts, values, grads, activation, own, other, total):
    slots = values.shape[1]
    chunks = grads.shape[0]
    rows = values.shape[0] // chunks
    nodes = total.shape[2]
    width = nodes // chunks

    total[...] = jnp.zeros_like(total)
    weight_part = jnp.zeros((16, 256), F32)
    for j in range(chunks):
        at = slice(j * width, (j + 1) * width)
        activation[:16, at] = grads[j, :, width + 256 : 2 * width + 256]
        activation[16:, at] = grads[j, :, 2 * width + 256 :]
        weight_part += grads[j, :, width : width + 256].astype(F32)

    @pl.loop(0, chunks)
    def _(j):
        for i in range(rows):
            r = j * rows + i
            count = counts[r]
            contrib = lax.dot_general(
                grads[j, :, i * BLOCK : (i + 1) * BLOCK],
                values[r].reshape(slots * BLOCK, BLOCK),
                (((1,), (1,)), ((), ())),
                preferred_element_type=F32,
            )
            for s in range(slots):
                group, lane = place_of(cols[r, s])
                group = jnp.where(s < count, group, 16)
                total[group, :, pl.ds(lane, BLOCK)] += contrib[:, s * BLOCK : (s + 1) * BLOCK]

    weight_part = weight_part.astype(BF)
    for k, (dx, dz) in enumerate(((0, 0),) + STEPS):
        for core, to in enumerate((own, other)):
            to[k, :, :nodes] = total[node_near(dx, dz, core)].astype(BF)
            to[k, :, nodes:] = weight_part


def pair_kernel(own, other, *outs):
    for k, out in enumerate(outs):
        out[...] = (own[k].astype(F32) + other[k].astype(F32)).astype(BF)


def local(features, weight, bias, block_values, block_cols, block_counts, train_mask, cotangent):
    fin, nodes = features.shape
    width = nodes // 8

    def shape(dims, kind=BF):
        return jax.ShapeDtypeStruct(dims, kind)

    bias_at = lax.dynamic_update_slice(
        jnp.zeros((1, 256), F32), bias[None, :], (0, lax.axis_index("feat") * bias.shape[0])
    )
    high = lax.reduce_precision(bias_at, 8, 7)
    middle = lax.reduce_precision(bias_at - high, 8, 7)
    bias_rows = jnp.concatenate(
        [high, middle, bias_at - high - middle, jnp.zeros((13, 256), F32)], axis=0
    ).astype(BF)

    pieces = [features, lax.ppermute(features, "node", node_pairs(0, 0, 1))]
    for dx, dz in STEPS:
        piece = lax.ppermute(features, "node", node_pairs(dx, dz))
        pieces += [piece, lax.ppermute(piece, "node", node_pairs(0, 0, 1))]

    values = pl.pallas_call(
        load_kernel,
        in_specs=[ANY, ANY],
        out_specs=VMEM,
        out_shape=pltpu.VMEM(block_values.shape, BF),
        scratch_shapes=[pltpu.SemaphoreType.DMA((8,))],
        compiler_params=params(4),
        cost_estimate=pl.CostEstimate(
            flops=0, bytes_accessed=2 * block_values.size * 2, transcendentals=0
        ),
        name="load",
    )(block_values, pieces[1])

    mixed = pl.pallas_call(
        mix_kernel,
        in_specs=[SMEM, SMEM] + [VMEM] * 4 + [ANY] * 16,
        out_specs=VMEM,
        out_shape=shape((8, 16, 3 * width + 512)),
        scratch_shapes=[pltpu.VMEM((16, fin, nodes), BF), pltpu.SemaphoreType.DMA((16,))],
        compiler_params=params(16),
        name="mix",
    )(block_cols, block_counts, values, cotangent, weight, bias_rows, *pieces)

    both = lax.all_to_all(mixed, "feat", 0, 0, tiled=True)

    dense = pl.pallas_call(
        dense_kernel,
        in_specs=[VMEM] * 2,
        out_specs=VMEM,
        out_shape=shape((8, 16, 3 * width + 256)),
        compiler_params=params(16),
        name="dense",
    )(both, train_mask[None, :])

    grads = lax.all_to_all(dense, "feat", 0, 0, tiled=True)

    activation, own, other = pl.pallas_call(
        spread_kernel,
        in_specs=[SMEM, SMEM] + [VMEM] * 2,
        out_specs=[VMEM] * 3,
        out_shape=[
            shape((32, nodes)),
            shape((8, 16, nodes + 256)),
            shape((8, 16, nodes + 256)),
        ],
        scratch_shapes=[pltpu.VMEM((17, fin, nodes), F32)],
        compiler_params=params(24),
        name="spread",
    )(block_cols, block_counts, values, grads)

    other = lax.ppermute(other, "node", node_pairs(0, 0, 1))
    sums = pl.pallas_call(
        pair_kernel,
        in_specs=[VMEM] * 2,
        out_specs=[VMEM] * 8,
        out_shape=[shape((16, nodes + 256))] * 8,
        compiler_params=params(16),
        name="pair",
    )(own, other)
    landed = [sums[0]]
    for (dx, dz), piece in zip(STEPS, sums[1:]):
        landed.append(lax.ppermute(piece, "node", node_pairs(dx, dz)))
    total = sum(piece.astype(F32) for piece in landed)
    return activation, total[:, :nodes].astype(BF), total[:, nodes:]


def solution(mesh):
    placed = (
        P("feat", "node"),
        P("feat", None),
        P("feat"),
        P("node", None, None, None),
        P("node", None),
        P("node"),
        P("node"),
        P("feat", "node"),
    )
    return jax.shard_map(
        local,
        mesh=mesh,
        in_specs=placed,
        out_specs=(P("feat", "node"), P("feat", "node"), P("feat", None)),
        check_vma=False,
    )
```

```python
import jax
import jax.numpy as jnp
from jax import lax
from jax.experimental import pallas as pl
from jax.experimental.pallas import tpu as pltpu
from jax.sharding import PartitionSpec as P

BF = jnp.bfloat16
F32 = jnp.float32
ANY = pl.BlockSpec(memory_space=pl.ANY)
SMEM = pl.BlockSpec(memory_space=pltpu.SMEM)
VMEM = pl.BlockSpec(memory_space=pltpu.VMEM)
STEPS = ((1, 2), (1, 1), (1, 3), (0, 2), (1, 0), (0, 1), (0, 3))
FAR = (1, 2)
SHARED = (((1, 1), (1, 3)), ((0, 2), (1, 0)), ((0, 1), (0, 3)))
BLOCK = 128


def node_at(x, z, core):
    return (x * 4 + z) * 2 + core


def node_pairs(dx, dz, dcore=0):
    return [
        (node_at(x, z, c), node_at(x ^ dx, (z + dz) % 4, c ^ dcore))
        for x in range(2)
        for z in range(4)
        for c in range(2)
    ]


def node_near(dx, dz, dcore):
    me = lax.axis_index("node")
    x, z, c = me >> 3, (me >> 1) & 3, me & 1
    return ((x ^ dx) * 4 + ((z + dz) & 3)) * 2 + (c ^ dcore)


def shared_pairs(steps):
    return [
        (node_at(x, z, c), node_at(x ^ steps[c][0], (z + steps[c][1]) % 4, c))
        for x in range(2)
        for z in range(4)
        for c in range(2)
    ]


def shared_near(steps, server, sign, dcore):
    core = (lax.axis_index("node") & 1) ^ server
    dx = jnp.where(core == 0, steps[0][0], steps[1][0])
    dz = jnp.where(core == 0, steps[0][1], steps[1][1])
    return node_near(dx, sign * dz, dcore)


def place_of(column):
    group = lax.shift_right_logical(column * 21846, 20)
    return group, pl.multiple_of((column - group * 48) * BLOCK, BLOCK)


def params(mib):
    return pltpu.CompilerParams(vmem_limit_bytes=mib * 2**20)


def load_kernel(values, _, out, loaded, sems):
    count = sems.shape[0]
    rows = values.shape[0] // count
    copies = [
        pltpu.make_async_copy(
            values.at[pl.ds(i * rows, rows)], out.at[pl.ds(i * rows, rows)], sems.at[i]
        )
        for i in range(count)
    ]
    for copy in copies:
        copy.start()
    for copy in copies:
        copy.wait()
    loaded[...] = jnp.zeros_like(loaded)


def mix_kernel(cols, counts, values, cotangent, weight, bias_rows, *rest):
    pieces, (out, held, sems) = rest[:10], rest[10:]
    slots = values.shape[1]
    chunks, _, _ = out.shape
    width = cotangent.shape[1] // chunks
    rows = values.shape[0] // chunks

    sources = []
    for at, (dx, dz) in enumerate(((0, 0), FAR)):
        for server in range(2):
            sources.append((pieces[2 * at + server], node_near(dx, -dz, server)))
    for at, steps in enumerate(SHARED):
        for server in range(2):
            for q in range(2):
                sources.append(
                    (pieces[4 + 2 * at + server].at[q], shared_near(steps, server, -1, server ^ q))
                )
    copies = [
        pltpu.make_async_copy(piece, held.at[group], sems.at[at])
        for at, (piece, group) in enumerate(sources)
    ]
    for copy in copies:
        copy.start()
    for j in range(chunks):
        out[j, :, width : 2 * width] = cotangent[:16, j * width : (j + 1) * width]
        out[j, :, 2 * width : 3 * width] = cotangent[16:, j * width : (j + 1) * width]
        out[j, :, 3 * width : 3 * width + 256] = weight[...]
        out[j, :, 3 * width + 256 :] = bias_rows[...]
    for copy in copies:
        copy.wait()

    @pl.loop(0, chunks)
    def _(j):
        for i in range(rows):
            r = j * rows + i
            count = counts[r]
            parts = []
            for s in range(slots):
                group, lane = place_of(cols[r, s])
                block = held[group, :, pl.ds(lane, BLOCK)]
                parts.append(jnp.where(s < count, block, jnp.zeros_like(block)))
            total = jnp.dot(
                jnp.concatenate(parts, axis=1),
                values[r].reshape(slots * BLOCK, BLOCK),
                preferred_element_type=F32,
            )
            out[j, :, i * BLOCK : (i + 1) * BLOCK] = total.astype(BF)


def dense_kernel(both, mask, out):
    width = mask.shape[1] // 8
    mixed = both[:, :, :width].reshape(128, width)
    cotangent = jnp.concatenate(
        [both[:, :, width : 2 * width], both[:, :, 2 * width : 3 * width]], axis=1
    ).reshape(256, width)
    weight = both[:, :, 3 * width : 3 * width + 256].reshape(128, 256)
    bias_rows = both[:, :, 3 * width + 256 :].reshape(128, 256)
    kept = mask[:, pl.ds(pl.multiple_of(lax.axis_index("feat") * width, BLOCK), width)]
    preact = lax.dot_general(
        jnp.concatenate([weight, bias_rows], axis=0),
        jnp.concatenate([mixed, jnp.ones_like(mixed)], axis=0),
        (((0,), (0,)), ((), ())),
        preferred_element_type=F32,
    )
    sigma = jax.nn.sigmoid(preact)
    activation = (preact * sigma).astype(BF).reshape(8, 32, width)
    slope = sigma * (1.0 + preact * (1.0 - sigma))
    grad_pre = (cotangent.astype(F32) * kept.astype(F32) * slope).astype(BF)
    grad_mixed = jnp.dot(weight, grad_pre, preferred_element_type=F32)
    grad_weight = lax.dot_general(
        mixed, grad_pre, (((1,), (1,)), ((), ())), preferred_element_type=F32
    )
    out[:, :, :width] = grad_mixed.astype(BF).reshape(8, 16, width)
    out[:, :, width : width + 256] = grad_weight.astype(BF).reshape(8, 16, 256)
    out[:, :, width + 256 : 2 * width + 256] = activation[:, :16]
    out[:, :, 2 * width + 256 :] = activation[:, 16:]


def spread_kernel(cols, counts, values, grads, activation, own, other, total):
    slots = values.shape[1]
    chunks = grads.shape[0]
    rows = values.shape[0] // chunks
    nodes = total.shape[2]
    width = nodes // chunks

    total[...] = jnp.zeros_like(total)
    weight_part = jnp.zeros((16, 256), F32)
    for j in range(chunks):
        at = slice(j * width, (j + 1) * width)
        activation[:16, at] = grads[j, :, width + 256 : 2 * width + 256]
        activation[16:, at] = grads[j, :, 2 * width + 256 :]
        weight_part += grads[j, :, width : width + 256].astype(F32)

    @pl.loop(0, chunks)
    def _(j):
        for i in range(rows):
            r = j * rows + i
            count = counts[r]
            contrib = lax.dot_general(
                grads[j, :, i * BLOCK : (i + 1) * BLOCK],
                values[r].reshape(slots * BLOCK, BLOCK),
                (((1,), (1,)), ((), ())),
                preferred_element_type=F32,
            )
            for s in range(slots):
                group, lane = place_of(cols[r, s])
                group = jnp.where(s < count, group, 16)
                total[group, :, pl.ds(lane, BLOCK)] += contrib[:, s * BLOCK : (s + 1) * BLOCK]

    weight_part = weight_part.astype(BF)
    for k, (dx, dz) in enumerate(((0, 0),) + STEPS):
        for core, to in enumerate((own, other)):
            to[k, :, :nodes] = total[node_near(dx, dz, core)].astype(BF)
            to[k, :, nodes:] = weight_part


def pair_kernel(own, other, *outs):
    for k, out in enumerate(outs):
        out[...] = (own[k].astype(F32) + other[k].astype(F32)).astype(BF)


def local(features, weight, bias, block_values, block_cols, block_counts, train_mask, cotangent):
    fin, nodes = features.shape
    width = nodes // 8

    def shape(dims, kind=BF):
        return jax.ShapeDtypeStruct(dims, kind)

    bias_at = lax.dynamic_update_slice(
        jnp.zeros((1, 256), F32), bias[None, :], (0, lax.axis_index("feat") * bias.shape[0])
    )
    high = lax.reduce_precision(bias_at, 8, 7)
    middle = lax.reduce_precision(bias_at - high, 8, 7)
    bias_rows = jnp.concatenate(
        [high, middle, bias_at - high - middle, jnp.zeros((13, 256), F32)], axis=0
    ).astype(BF)

    swap = node_pairs(0, 0, 1)
    pieces = [features, lax.ppermute(features, "node", swap)]
    pair = jnp.stack(pieces)
    arrived = [lax.ppermute(features, "node", node_pairs(*FAR))]
    arrived += [lax.ppermute(pair, "node", shared_pairs(steps)) for steps in SHARED]
    values, loaded = pl.pallas_call(
        load_kernel,
        in_specs=[pl.BlockSpec(memory_space=pltpu.HBM), ANY],
        out_specs=[VMEM, VMEM],
        out_shape=[pltpu.VMEM(block_values.shape, BF), shape((8, 128), F32)],
        scratch_shapes=[pltpu.SemaphoreType.DMA((8,))],
        compiler_params=params(4),
        cost_estimate=pl.CostEstimate(
            flops=0, bytes_accessed=2 * block_values.size * 2, transcendentals=0
        ),
        name="load",
    )(pltpu.with_memory_space_constraint(block_values, pltpu.HBM), pair)

    for piece in arrived:
        piece, _ = lax.optimization_barrier((piece, loaded))
        pieces += [piece, lax.ppermute(piece, "node", swap)]

    mixed = pl.pallas_call(
        mix_kernel,
        in_specs=[SMEM, SMEM] + [VMEM] * 4 + [ANY] * 10,
        out_specs=VMEM,
        out_shape=shape((8, 16, 3 * width + 512)),
        scratch_shapes=[pltpu.VMEM((16, fin, nodes), BF), pltpu.SemaphoreType.DMA((16,))],
        compiler_params=params(16),
        name="mix",
    )(block_cols, block_counts, values, cotangent, weight, bias_rows, *pieces)

    both = lax.all_to_all(mixed, "feat", 0, 0, tiled=True)

    dense = pl.pallas_call(
        dense_kernel,
        in_specs=[VMEM] * 2,
        out_specs=VMEM,
        out_shape=shape((8, 16, 3 * width + 256)),
        compiler_params=params(16),
        name="dense",
    )(both, train_mask[None, :])

    grads = lax.all_to_all(dense, "feat", 0, 0, tiled=True)

    activation, own, other = pl.pallas_call(
        spread_kernel,
        in_specs=[SMEM, SMEM] + [VMEM] * 2,
        out_specs=[VMEM] * 3,
        out_shape=[
            shape((32, nodes)),
            shape((8, 16, nodes + 256)),
            shape((8, 16, nodes + 256)),
        ],
        scratch_shapes=[pltpu.VMEM((17, fin, nodes), F32)],
        compiler_params=params(24),
        name="spread",
    )(block_cols, block_counts, values, grads)

    other = lax.ppermute(other, "node", node_pairs(0, 0, 1))
    sums = pl.pallas_call(
        pair_kernel,
        in_specs=[VMEM] * 2,
        out_specs=[VMEM] * 8,
        out_shape=[shape((16, nodes + 256))] * 8,
        compiler_params=params(16),
        name="pair",
    )(own, other)
    landed = [sums[0]]
    for (dx, dz), piece in zip(STEPS, sums[1:]):
        landed.append(lax.ppermute(piece, "node", node_pairs(dx, dz)))
    total = sum(piece.astype(F32) for piece in landed)
    return activation, total[:, :nodes].astype(BF), total[:, nodes:]


def solution(mesh):
    placed = (
        P("feat", "node"),
        P("feat", None),
        P("feat"),
        P("node", None, None, None),
        P("node", None),
        P("node"),
        P("node"),
        P("feat", "node"),
    )
    return jax.shard_map(
        local,
        mesh=mesh,
        in_specs=placed,
        out_specs=(P("feat", "node"), P("feat", "node"), P("feat", None)),
        check_vma=False,
    )
```

```python
import jax
import jax.numpy as jnp
from jax import lax
from jax.experimental import pallas as pl
from jax.experimental.pallas import tpu as pltpu
from jax.sharding import PartitionSpec as P

BF = jnp.bfloat16
F32 = jnp.float32
ANY = pl.BlockSpec(memory_space=pl.ANY)
SMEM = pl.BlockSpec(memory_space=pltpu.SMEM)
VMEM = pl.BlockSpec(memory_space=pltpu.VMEM)
ALONE = (0, 1)
SHARED = (((1, 2), (1, 1)), ((1, 3), (0, 2)), ((1, 0), (0, 3)))
BLOCK = 128


def node_at(x, z, core):
    return (x * 4 + z) * 2 + core


def node_pairs(dx, dz, dcore=0):
    return [
        (node_at(x, z, c), node_at(x ^ dx, (z + dz) % 4, c ^ dcore))
        for x in range(2)
        for z in range(4)
        for c in range(2)
    ]


def node_near(dx, dz, dcore):
    me = lax.axis_index("node")
    x, z, c = me >> 3, (me >> 1) & 3, me & 1
    return ((x ^ dx) * 4 + ((z + dz) & 3)) * 2 + (c ^ dcore)


def shared_pairs(steps):
    return [
        (node_at(x, z, c), node_at(x ^ steps[c][0], (z + steps[c][1]) % 4, c))
        for x in range(2)
        for z in range(4)
        for c in range(2)
    ]


def shared_near(steps, server, sign, dcore):
    core = (lax.axis_index("node") & 1) ^ server
    dx = jnp.where(core == 0, steps[0][0], steps[1][0])
    dz = jnp.where(core == 0, steps[0][1], steps[1][1])
    return node_near(dx, sign * dz, dcore)


def place_of(column):
    group = lax.shift_right_logical(column * 21846, 20)
    return group, pl.multiple_of((column - group * 48) * BLOCK, BLOCK)


def params(mib):
    return pltpu.CompilerParams(vmem_limit_bytes=mib * 2**20)


def stack_kernel(first, second, out):
    out[0] = first[...]
    out[1] = second[...]


def load_kernel(values, _, out, loaded, sems):
    count = sems.shape[0]
    rows = values.shape[0] // count
    copies = [
        pltpu.make_async_copy(
            values.at[pl.ds(i * rows, rows)], out.at[pl.ds(i * rows, rows)], sems.at[i]
        )
        for i in range(count)
    ]
    for copy in copies:
        copy.start()
    for copy in copies:
        copy.wait()
    loaded[...] = jnp.zeros_like(loaded)


def mix_kernel(cols, counts, values, cotangent, weight, bias_rows, *rest):
    pieces, (out, held) = rest[:10], rest[10:]
    slots = values.shape[1]
    chunks, _, _ = out.shape
    width = cotangent.shape[1] // chunks
    rows = values.shape[0] // chunks

    for at, (dx, dz) in ((0, (0, 0)), (8, ALONE)):
        for server in range(2):
            held[node_near(dx, -dz, server)] = pieces[at + server][...]
    for at, steps in ((2, SHARED[2]), (4, SHARED[1]), (6, SHARED[0])):
        for server in range(2):
            for q in range(2):
                near = shared_near(steps, server, -1, server ^ q)
                held[near] = pieces[at + server][q]
    for j in range(chunks):
        out[j, :, width : 2 * width] = cotangent[:16, j * width : (j + 1) * width]
        out[j, :, 2 * width : 3 * width] = cotangent[16:, j * width : (j + 1) * width]
        out[j, :, 3 * width : 3 * width + 256] = weight[...]
        out[j, :, 3 * width + 256 :] = bias_rows[...]

    for j in range(chunks):
        for i in range(rows):
            r = j * rows + i
            count = counts[r]
            parts = []
            for s in range(slots):
                group, lane = place_of(cols[r, s])
                block = held[group, :, pl.ds(lane, BLOCK)]
                parts.append(jnp.where(s < count, block, jnp.zeros_like(block)))
            total = jnp.dot(
                jnp.concatenate(parts, axis=1),
                values[r].reshape(slots * BLOCK, BLOCK),
                preferred_element_type=F32,
            )
            out[j, :, i * BLOCK : (i + 1) * BLOCK] = total.astype(BF)


def dense_kernel(both, mask, out):
    width = mask.shape[1] // 8
    mixed = both[:, :, :width].reshape(128, width)
    cotangent = jnp.concatenate(
        [both[:, :, width : 2 * width], both[:, :, 2 * width : 3 * width]], axis=1
    ).reshape(256, width)
    weight = both[:, :, 3 * width : 3 * width + 256].reshape(128, 256)
    bias_rows = both[:, :, 3 * width + 256 :].reshape(128, 256)
    kept = mask[:, pl.ds(pl.multiple_of(lax.axis_index("feat") * width, BLOCK), width)]
    preact = lax.dot_general(
        jnp.concatenate([weight, bias_rows], axis=0),
        jnp.concatenate([mixed, jnp.ones_like(mixed)], axis=0),
        (((0,), (0,)), ((), ())),
        preferred_element_type=F32,
    )
    sigma = jax.nn.sigmoid(preact)
    activation = (preact * sigma).astype(BF).reshape(8, 32, width)
    slope = sigma * (1.0 + preact * (1.0 - sigma))
    grad_pre = (cotangent.astype(F32) * kept.astype(F32) * slope).astype(BF)
    grad_mixed = jnp.dot(weight, grad_pre, preferred_element_type=F32)
    grad_weight = lax.dot_general(
        mixed, grad_pre, (((1,), (1,)), ((), ())), preferred_element_type=F32
    )
    out[:, :, :width] = grad_mixed.astype(BF).reshape(8, 16, width)
    out[:, :, width : width + 256] = grad_weight.astype(BF).reshape(8, 16, 256)
    out[:, :, width + 256 : 2 * width + 256] = activation[:, :16]
    out[:, :, 2 * width + 256 :] = activation[:, 16:]


def spread_kernel(cols, counts, values, grads, activation, own, other, total):
    slots = values.shape[1]
    chunks = grads.shape[0]
    rows = values.shape[0] // chunks
    nodes = total.shape[2]
    width = nodes // chunks

    total[...] = jnp.zeros_like(total)
    weight_part = jnp.zeros((16, 256), F32)
    for j in range(chunks):
        at = slice(j * width, (j + 1) * width)
        activation[:16, at] = grads[j, :, width + 256 : 2 * width + 256]
        activation[16:, at] = grads[j, :, 2 * width + 256 :]
        weight_part += grads[j, :, width : width + 256].astype(F32)

    for j in range(chunks):
        for i in range(rows):
            r = j * rows + i
            count = counts[r]
            contrib = lax.dot_general(
                grads[j, :, i * BLOCK : (i + 1) * BLOCK],
                values[r].reshape(slots * BLOCK, BLOCK),
                (((1,), (1,)), ((), ())),
                preferred_element_type=F32,
            )
            for s in range(slots):
                group, lane = place_of(cols[r, s])
                group = jnp.where(s < count, group, 16)
                total[group, :, pl.ds(lane, BLOCK)] += contrib[:, s * BLOCK : (s + 1) * BLOCK]

    weight_part = weight_part.astype(BF)
    for server, to in enumerate((own, other)):
        nears = [node_near(0, 0, server), node_near(*ALONE, server)]
        nears += [shared_near(steps, server, 1, server ^ q) for steps in SHARED for q in range(2)]
        for k, near in enumerate(nears):
            to[k, :, :nodes] = total[near].astype(BF)
            to[k, :, nodes:] = weight_part


def pair_kernel(own, other, stay, alone, *shared):
    def both(k):
        return (own[k].astype(F32) + other[k].astype(F32)).astype(BF)

    stay[...] = both(0)
    alone[...] = both(1)
    for i, out in enumerate(shared):
        for q in range(2):
            out[q] = both(2 + 2 * i + q)


def hand_kernel(first, second, third, out):
    out[...] = (first[1].astype(F32) + second[1].astype(F32) + third[1].astype(F32)).astype(BF)


def last_kernel(stay, alone, handed, first, second, third, grad_features, grad_weight):
    total = stay[...].astype(F32) + alone[...].astype(F32) + handed[...].astype(F32)
    for piece in (first, second, third):
        total += piece[0].astype(F32)
    nodes = grad_features.shape[1]
    grad_features[...] = total[:, :nodes].astype(BF)
    grad_weight[...] = total[:, nodes:]


def local(features, weight, bias, block_values, block_cols, block_counts, train_mask, cotangent):
    fin, nodes = features.shape
    width = nodes // 8

    def shape(dims, kind=BF):
        return jax.ShapeDtypeStruct(dims, kind)

    bias_at = lax.dynamic_update_slice(
        jnp.zeros((1, 256), F32), bias[None, :], (0, lax.axis_index("feat") * bias.shape[0])
    )
    high = lax.reduce_precision(bias_at, 8, 7)
    middle = lax.reduce_precision(bias_at - high, 8, 7)
    bias_rows = jnp.concatenate(
        [high, middle, bias_at - high - middle, jnp.zeros((13, 256), F32)], axis=0
    ).astype(BF)

    swap = node_pairs(0, 0, 1)
    pieces = [features, lax.ppermute(features, "node", swap)]
    pair = pl.pallas_call(
        stack_kernel,
        in_specs=[VMEM] * 2,
        out_specs=VMEM,
        out_shape=shape((2, fin, nodes)),
        compiler_params=params(4),
        name="stack",
    )(*pieces)
    arrived = [lax.ppermute(pair, "node", shared_pairs(steps)) for steps in SHARED[::-1]]
    arrived.append(lax.ppermute(features, "node", node_pairs(*ALONE)))
    values, loaded = pl.pallas_call(
        load_kernel,
        in_specs=[pl.BlockSpec(memory_space=pltpu.HBM), ANY],
        out_specs=[VMEM, VMEM],
        out_shape=[pltpu.VMEM(block_values.shape, BF), shape((8, 128), F32)],
        scratch_shapes=[pltpu.SemaphoreType.DMA((8,))],
        compiler_params=params(4),
        cost_estimate=pl.CostEstimate(
            flops=0, bytes_accessed=2 * block_values.size * 2, transcendentals=0
        ),
        name="load",
    )(pltpu.with_memory_space_constraint(block_values, pltpu.HBM), pair)

    for piece in arrived:
        piece, _ = lax.optimization_barrier((piece, loaded))
        pieces += [piece, lax.ppermute(piece, "node", swap)]

    mixed = pl.pallas_call(
        mix_kernel,
        in_specs=[SMEM, SMEM] + [VMEM] * 14,
        out_specs=VMEM,
        out_shape=shape((8, 16, 3 * width + 512)),
        scratch_shapes=[pltpu.VMEM((16, fin, nodes), BF)],
        compiler_params=params(16),
        name="mix",
    )(block_cols, block_counts, values, cotangent, weight, bias_rows, *pieces)

    both = lax.all_to_all(mixed, "feat", 0, 0, tiled=True)

    dense = pl.pallas_call(
        dense_kernel,
        in_specs=[VMEM] * 2,
        out_specs=VMEM,
        out_shape=shape((8, 16, 3 * width + 256)),
        compiler_params=params(16),
        name="dense",
    )(both, train_mask[None, :])

    grads = lax.all_to_all(dense, "feat", 0, 0, tiled=True)

    activation, own, other = pl.pallas_call(
        spread_kernel,
        in_specs=[SMEM, SMEM] + [VMEM] * 2,
        out_specs=[VMEM] * 3,
        out_shape=[
            shape((32, nodes)),
            shape((8, 16, nodes + 256)),
            shape((8, 16, nodes + 256)),
        ],
        scratch_shapes=[pltpu.VMEM((17, fin, nodes), F32)],
        compiler_params=params(24),
        name="spread",
    )(block_cols, block_counts, values, grads)

    other = lax.ppermute(other, "node", swap)
    stay, alone, *shared = pl.pallas_call(
        pair_kernel,
        in_specs=[VMEM] * 2,
        out_specs=[VMEM] * 5,
        out_shape=[shape((16, nodes + 256))] * 2 + [shape((2, 16, nodes + 256))] * 3,
        compiler_params=params(16),
        name="pair",
    )(own, other)
    alone = lax.ppermute(alone, "node", node_pairs(*ALONE))
    shared = [
        lax.ppermute(piece, "node", shared_pairs(steps)) for piece, steps in zip(shared, SHARED)
    ]
    handed = pl.pallas_call(
        hand_kernel,
        in_specs=[VMEM] * 3,
        out_specs=VMEM,
        out_shape=shape((16, nodes + 256)),
        compiler_params=params(16),
        name="hand",
    )(*shared)
    handed = lax.ppermute(handed, "node", swap)
    grad_features, grad_weight = pl.pallas_call(
        last_kernel,
        in_specs=[VMEM] * 6,
        out_specs=[VMEM] * 2,
        out_shape=[shape((16, nodes)), shape((16, 256), F32)],
        compiler_params=params(16),
        name="last",
    )(stay, alone, handed, *shared)
    return activation, grad_features, grad_weight


def solution(mesh):
    placed = (
        P("feat", "node"),
        P("feat", None),
        P("feat"),
        P("node", None, None, None),
        P("node", None),
        P("node"),
        P("node"),
        P("feat", "node"),
    )
    return jax.shard_map(
        local,
        mesh=mesh,
        in_specs=placed,
        out_specs=(P("feat", "node"), P("feat", "node"), P("feat", None)),
        check_vma=False,
    )
```

```python
import functools

import jax
import jax.numpy as jnp
from jax import lax
from jax.experimental import pallas as pl
from jax.experimental.pallas import tpu as pltpu
from jax.sharding import PartitionSpec as P

BF = jnp.bfloat16
F32 = jnp.float32
ANY = pl.BlockSpec(memory_space=pl.ANY)
SMEM = pl.BlockSpec(memory_space=pltpu.SMEM)
VMEM = pl.BlockSpec(memory_space=pltpu.VMEM)
STEP_A = ((1, 0), (0, 2))
STEP_B = ((0, 1), (0, 3))
STEP_C = ((0, 1), (1, 0))
STEP_D = ((0, 3), (1, 0))
FROM_A = ((1, 0), (0, 2))
FROM_B = ((0, 3), (0, 1))
FROM_C = ((1, 3), (1, 2))
FROM_D = (1, 1)
BLOCK = 128


def node_at(x, z, core):
    return (x * 4 + z) * 2 + core


def node_pairs(dx, dz, dcore=0):
    return [
        (node_at(x, z, c), node_at(x ^ dx, (z + dz) % 4, c ^ dcore))
        for x in range(2)
        for z in range(4)
        for c in range(2)
    ]


def node_near(dx, dz, dcore):
    me = lax.axis_index("node")
    x, z, c = me >> 3, (me >> 1) & 3, me & 1
    return ((x ^ dx) * 4 + ((z + dz) & 3)) * 2 + (c ^ dcore)


def shared_pairs(steps):
    return [
        (node_at(x, z, c), node_at(x ^ steps[c][0], (z + steps[c][1]) % 4, c))
        for x in range(2)
        for z in range(4)
        for c in range(2)
    ]


def back(steps):
    return tuple((dx, -dz % 4) for dx, dz in steps)


def shared_near(steps, server, dcore):
    core = (lax.axis_index("node") & 1) ^ server
    dx = jnp.where(core == 0, steps[0][0], steps[1][0])
    dz = jnp.where(core == 0, steps[0][1], steps[1][1])
    return node_near(dx, dz, dcore)


def pair_near(steps, server):
    return [shared_near(steps, server, server ^ q) for q in range(2)]


def place_of(column):
    group = lax.shift_right_logical(column * 21846, 20)
    return group, pl.multiple_of((column - group * 48) * BLOCK, BLOCK)


def params(mib):
    return pltpu.CompilerParams(vmem_limit_bytes=mib * 2**20)


def stack_kernel(first, second, out):
    out[0] = first[...]
    out[1] = second[...]


def pick_kernel(first, second, _, out):
    core = lax.axis_index("node") & 1

    @pl.when(core == 0)
    def _():
        out[...] = first[0]

    @pl.when(core == 1)
    def _():
        out[...] = second[0]


def bundle_kernel(pair, single, _, out):
    out[:2] = pair[...]
    out[2] = single[...]


def load_kernel(start, values, _, out, loaded, sems):
    count = sems.shape[0]
    rows = out.shape[0] // count
    copies = [
        pltpu.make_async_copy(
            values.at[pl.ds(start + i * rows, rows)], out.at[pl.ds(i * rows, rows)], sems.at[i]
        )
        for i in range(count)
    ]
    for copy in copies:
        copy.start()
    for copy in copies:
        copy.wait()
    loaded[...] = jnp.zeros_like(loaded)


def mix_kernel(cols, counts, upper, lower, cotangent, weight, bias_rows, *rest):
    pieces, (out, held) = rest[:9], rest[9:]
    half, slots = upper.shape[:2]
    chunks, _, _ = out.shape
    width = cotangent.shape[1] // chunks
    rows = 2 * half // chunks

    bundle = pieces[8]
    shards = {(FROM_A, 0): pieces[2], (FROM_A, 1): pieces[3], (FROM_B, 0): pieces[4]}
    shards |= {(FROM_B, 1): pieces[5], (FROM_C, 0): pieces[6], (FROM_C, 1): bundle}
    for server in range(2):
        held[node_near(0, 0, server)] = pieces[server][...]
        for steps in (FROM_A, FROM_B, FROM_C):
            for q, near in enumerate(pair_near(steps, server)):
                held[near] = shards[steps, server][q]
    held[node_near(*FROM_D, 0)] = pieces[7][...]
    held[node_near(*FROM_D, 1)] = bundle[2]
    for j in range(chunks):
        out[j, :, width : 2 * width] = cotangent[:16, j * width : (j + 1) * width]
        out[j, :, 2 * width : 3 * width] = cotangent[16:, j * width : (j + 1) * width]
        out[j, :, 3 * width : 3 * width + 256] = weight[...]
        out[j, :, 3 * width + 256 :] = bias_rows[...]

    for j in range(chunks):
        for i in range(rows):
            r = j * rows + i
            count = counts[r]
            parts = []
            for s in range(slots):
                group, lane = place_of(cols[r, s])
                block = held[group, :, pl.ds(lane, BLOCK)]
                parts.append(jnp.where(s < count, block, jnp.zeros_like(block)))
            total = jnp.dot(
                jnp.concatenate(parts, axis=1),
                (upper if r < half else lower)[r % half].reshape(slots * BLOCK, BLOCK),
                preferred_element_type=F32,
            )
            out[j, :, i * BLOCK : (i + 1) * BLOCK] = total.astype(BF)


def dense_kernel(both, mask, out):
    width = mask.shape[1] // 8
    mixed = both[:, :, :width].reshape(128, width)
    cotangent = jnp.concatenate(
        [both[:, :, width : 2 * width], both[:, :, 2 * width : 3 * width]], axis=1
    ).reshape(256, width)
    weight = both[:, :, 3 * width : 3 * width + 256].reshape(128, 256)
    bias_rows = both[:, :, 3 * width + 256 :].reshape(128, 256)
    kept = mask[:, pl.ds(pl.multiple_of(lax.axis_index("feat") * width, BLOCK), width)]
    preact = lax.dot_general(
        jnp.concatenate([weight, bias_rows], axis=0),
        jnp.concatenate([mixed, jnp.ones_like(mixed)], axis=0),
        (((0,), (0,)), ((), ())),
        preferred_element_type=F32,
    )
    sigma = jax.nn.sigmoid(preact)
    activation = (preact * sigma).astype(BF).reshape(8, 32, width)
    slope = sigma * (1.0 + preact * (1.0 - sigma))
    grad_pre = (cotangent.astype(F32) * kept.astype(F32) * slope).astype(BF)
    grad_mixed = jnp.dot(weight, grad_pre, preferred_element_type=F32)
    grad_weight = lax.dot_general(
        mixed, grad_pre, (((1,), (1,)), ((), ())), preferred_element_type=F32
    )
    out[:, :, :width] = grad_mixed.astype(BF).reshape(8, 16, width)
    out[:, :, width : width + 256] = grad_weight.astype(BF).reshape(8, 16, 256)
    out[:, :, width + 256 : 2 * width + 256] = activation[:, :16]
    out[:, :, 2 * width + 256 :] = activation[:, 16:]


def spread_kernel(
    cols, counts, upper, lower, grads, activation, own1, other1, own2, other2, total
):
    half, slots = upper.shape[:2]
    chunks = grads.shape[0]
    rows = 2 * half // chunks
    nodes = total.shape[2]
    width = nodes // chunks

    total[...] = jnp.zeros_like(total)
    weight_part = jnp.zeros((16, 256), F32)
    for j in range(chunks):
        at = slice(j * width, (j + 1) * width)
        activation[:16, at] = grads[j, :, width + 256 : 2 * width + 256]
        activation[16:, at] = grads[j, :, 2 * width + 256 :]
        weight_part += grads[j, :, width : width + 256].astype(F32)

    for j in range(chunks):
        for i in range(rows):
            r = j * rows + i
            count = counts[r]
            contrib = lax.dot_general(
                grads[j, :, i * BLOCK : (i + 1) * BLOCK],
                (upper if r < half else lower)[r % half].reshape(slots * BLOCK, BLOCK),
                (((1,), (1,)), ((), ())),
                preferred_element_type=F32,
            )
            for s in range(slots):
                group, lane = place_of(cols[r, s])
                group = jnp.where(s < count, group, 16)
                total[group, :, pl.ds(lane, BLOCK)] += contrib[:, s * BLOCK : (s + 1) * BLOCK]

    weight_part = weight_part.astype(BF)
    for server, to1, to2 in ((0, own1, own2), (1, other1, other2)):
        nears1 = pair_near(FROM_C, server) + [node_near(*FROM_D, server)]
        nears2 = pair_near(FROM_A, server) + pair_near(FROM_B, server) + [node_near(0, 0, server)]
        for to, nears in ((to1, nears1), (to2, nears2)):
            for k, near in enumerate(nears):
                to[k, :, :nodes] = total[near].astype(BF)
                to[k, :, nodes:] = weight_part


def pair_kernel(own, other, to_c, to_d):
    def both(k):
        return (own[k].astype(F32) + other[k].astype(F32)).astype(BF)

    to_c[0] = both(0)
    to_c[1] = both(1)
    to_d[...] = both(2)


def merge_kernel(own, other, from_c, from_d, to_a, to_b, stay):
    core = lax.axis_index("node") & 1
    last = from_d[...].astype(F32)

    def both(k):
        return own[k].astype(F32) + other[k].astype(F32)

    for q in range(2):
        total_a = both(q) + from_c[q].astype(F32)
        total_b = both(2 + q)
        if q == 0:
            total_a += jnp.where(core == 0, last, 0.0)
            total_b += jnp.where(core == 1, last, 0.0)
        to_a[q] = total_a.astype(BF)
        to_b[q] = total_b.astype(BF)
    stay[...] = both(4).astype(BF)


def hand_kernel(first, second, out):
    out[...] = (first[1].astype(F32) + second[1].astype(F32)).astype(BF)


def last_kernel(stay, handed, first, second, grad_features, grad_weight):
    total = stay[...].astype(F32) + handed[...].astype(F32)
    total += first[0].astype(F32) + second[0].astype(F32)
    nodes = grad_features.shape[1]
    grad_features[...] = total[:, :nodes].astype(BF)
    grad_weight[...] = total[:, nodes:]


def local(features, weight, bias, block_values, block_cols, block_counts, train_mask, cotangent):
    fin, nodes = features.shape
    width = nodes // 8

    def shape(dims, kind=BF):
        return jax.ShapeDtypeStruct(dims, kind)

    bias_at = lax.dynamic_update_slice(
        jnp.zeros((1, 256), F32), bias[None, :], (0, lax.axis_index("feat") * bias.shape[0])
    )
    high = lax.reduce_precision(bias_at, 8, 7)
    middle = lax.reduce_precision(bias_at - high, 8, 7)
    bias_rows = jnp.concatenate(
        [high, middle, bias_at - high - middle, jnp.zeros((13, 256), F32)], axis=0
    ).astype(BF)

    swap = node_pairs(0, 0, 1)
    pieces = [features, lax.ppermute(features, "node", swap)]
    pair = pl.pallas_call(
        stack_kernel,
        in_specs=[VMEM] * 2,
        out_specs=VMEM,
        out_shape=shape((2, fin, nodes)),
        compiler_params=params(4),
        name="stack",
    )(*pieces)
    half = block_values.shape[0] // 2

    def load(at, after):
        part = (half,) + block_values.shape[1:]
        return pl.pallas_call(
            functools.partial(load_kernel, at * half),
            in_specs=[pl.BlockSpec(memory_space=pltpu.HBM), ANY],
            out_specs=[VMEM, VMEM],
            out_shape=[pltpu.VMEM(part, BF), shape((8, 128), F32)],
            scratch_shapes=[pltpu.SemaphoreType.DMA((4,))],
            compiler_params=params(4),
            cost_estimate=pl.CostEstimate(
                flops=0, bytes_accessed=2 * block_values.size, transcendentals=0
            ),
            name="load",
        )(pltpu.with_memory_space_constraint(block_values, pltpu.HBM), after)

    def send(piece, steps):
        return lax.ppermute(piece, "node", shared_pairs(steps))

    by_a = send(pair, STEP_A)
    by_b = send(pair, STEP_B)
    upper, loaded = load(0, pair)
    by_c = send(by_a, STEP_C)
    picked = pl.pallas_call(
        pick_kernel,
        in_specs=[VMEM] * 2 + [ANY],
        out_specs=VMEM,
        out_shape=shape((fin, nodes)),
        compiler_params=params(4),
        name="pick",
    )(by_a, by_b, loaded)
    by_d = send(picked, STEP_D)
    lower, loaded = load(1, picked)
    bundle = pl.pallas_call(
        bundle_kernel,
        in_specs=[VMEM] * 2 + [ANY],
        out_specs=VMEM,
        out_shape=shape((3, fin, nodes)),
        compiler_params=params(4),
        name="bundle",
    )(by_c, by_d, loaded)
    pieces += [by_a, lax.ppermute(by_a, "node", swap), by_b, lax.ppermute(by_b, "node", swap)]
    pieces += [by_c, by_d, lax.ppermute(bundle, "node", swap)]

    mixed = pl.pallas_call(
        mix_kernel,
        in_specs=[SMEM, SMEM] + [VMEM] * 14,
        out_specs=VMEM,
        out_shape=shape((8, 16, 3 * width + 512)),
        scratch_shapes=[pltpu.VMEM((16, fin, nodes), BF)],
        compiler_params=params(16),
        name="mix",
    )(block_cols, block_counts, upper, lower, cotangent, weight, bias_rows, *pieces)

    both = lax.all_to_all(mixed, "feat", 0, 0, tiled=True)

    dense = pl.pallas_call(
        dense_kernel,
        in_specs=[VMEM] * 2,
        out_specs=VMEM,
        out_shape=shape((8, 16, 3 * width + 256)),
        compiler_params=params(16),
        name="dense",
    )(both, train_mask[None, :])

    grads = lax.all_to_all(dense, "feat", 0, 0, tiled=True)

    wide = nodes + 256
    activation, own1, other1, own2, other2 = pl.pallas_call(
        spread_kernel,
        in_specs=[SMEM, SMEM] + [VMEM] * 3,
        out_specs=[VMEM] * 5,
        out_shape=[shape((32, nodes))]
        + [shape((3, 16, wide))] * 2
        + [shape((5, 16, wide))] * 2,
        scratch_shapes=[pltpu.VMEM((17, fin, nodes), F32)],
        compiler_params=params(24),
        name="spread",
    )(block_cols, block_counts, upper, lower, grads)

    other1 = lax.ppermute(other1, "node", swap)
    other2 = lax.ppermute(other2, "node", swap)
    to_c, to_d = pl.pallas_call(
        pair_kernel,
        in_specs=[VMEM] * 2,
        out_specs=[VMEM] * 2,
        out_shape=[shape((2, 16, wide)), shape((16, wide))],
        compiler_params=params(16),
        name="pair",
    )(own1, other1)
    from_c = send(to_c, back(STEP_C))
    from_d = send(to_d, back(STEP_D))
    to_a, to_b, stay = pl.pallas_call(
        merge_kernel,
        in_specs=[VMEM] * 4,
        out_specs=[VMEM] * 3,
        out_shape=[shape((2, 16, wide))] * 2 + [shape((16, wide))],
        compiler_params=params(16),
        name="merge",
    )(own2, other2, from_c, from_d)
    from_a = send(to_a, back(STEP_A))
    from_b = send(to_b, back(STEP_B))
    handed = pl.pallas_call(
        hand_kernel,
        in_specs=[VMEM] * 2,
        out_specs=VMEM,
        out_shape=shape((16, wide)),
        compiler_params=params(16),
        name="hand",
    )(from_a, from_b)
    handed = lax.ppermute(handed, "node", swap)
    grad_features, grad_weight = pl.pallas_call(
        last_kernel,
        in_specs=[VMEM] * 4,
        out_specs=[VMEM] * 2,
        out_shape=[shape((16, nodes)), shape((16, 256), F32)],
        compiler_params=params(16),
        name="last",
    )(stay, handed, from_a, from_b)
    return activation, grad_features, grad_weight


def solution(mesh):
    placed = (
        P("feat", "node"),
        P("feat", None),
        P("feat"),
        P("node", None, None, None),
        P("node", None),
        P("node"),
        P("node"),
        P("feat", "node"),
    )
    return jax.shard_map(
        local,
        mesh=mesh,
        in_specs=placed,
        out_specs=(P("feat", "node"), P("feat", "node"), P("feat", None)),
        check_vma=False,
    )
```

```python
import functools

import jax
import jax.numpy as jnp
from jax import lax
from jax.experimental import pallas as pl
from jax.experimental.pallas import tpu as pltpu
from jax.sharding import PartitionSpec as P

BF = jnp.bfloat16
F32 = jnp.float32
ANY = pl.BlockSpec(memory_space=pl.ANY)
SMEM = pl.BlockSpec(memory_space=pltpu.SMEM)
VMEM = pl.BlockSpec(memory_space=pltpu.VMEM)
FIRST = ((0, 2), (1, 0))
SECOND = ((1, 1), (1, 3))
THIRD = ((0, 1), (0, 3))
FORWARD = ((1, 0), (0, 2))
FARTHEST = (1, 2)
BLOCK = 128


def node_at(x, z, core):
    return (x * 4 + z) * 2 + core


def node_pairs(dx, dz, dcore=0):
    return [
        (node_at(x, z, c), node_at(x ^ dx, (z + dz) % 4, c ^ dcore))
        for x in range(2)
        for z in range(4)
        for c in range(2)
    ]


def node_near(dx, dz, dcore):
    me = lax.axis_index("node")
    x, z, c = me >> 3, (me >> 1) & 3, me & 1
    return ((x ^ dx) * 4 + ((z + dz) & 3)) * 2 + (c ^ dcore)


def shared_pairs(steps):
    return [
        (node_at(x, z, c), node_at(x ^ steps[c][0], (z + steps[c][1]) % 4, c))
        for x in range(2)
        for z in range(4)
        for c in range(2)
    ]


def back(steps):
    return tuple((dx, -dz % 4) for dx, dz in steps)


def shared_near(steps, server, dcore):
    core = (lax.axis_index("node") & 1) ^ server
    dx = jnp.where(core == 0, steps[0][0], steps[1][0])
    dz = jnp.where(core == 0, steps[0][1], steps[1][1])
    return node_near(dx, dz, dcore)


def pair_near(steps, server):
    return [shared_near(steps, server, server ^ q) for q in range(2)]


def place_of(column):
    group = lax.shift_right_logical(column * 21846, 20)
    return group, pl.multiple_of((column - group * 48) * BLOCK, BLOCK)


def params(mib):
    return pltpu.CompilerParams(vmem_limit_bytes=mib * 2**20)


def stack_kernel(first, second, out):
    out[0] = first[...]
    out[1] = second[...]


def bundle_kernel(_, *refs):
    pieces, out = refs[:-1], refs[-1]
    at = 0
    for piece in pieces:
        if len(piece.shape) == 3:
            out[at : at + 2] = piece[...]
            at += 2
        else:
            out[at] = piece[...]
            at += 1


def pick_kernel(pair, out):
    out[...] = pair[0]


def load_kernel(values, *rest):
    out, loaded, sems = rest[-3:]
    count = sems.shape[0]
    rows = out.shape[0] // count
    copies = [
        pltpu.make_async_copy(
            values.at[pl.ds(i * rows, rows)], out.at[pl.ds(i * rows, rows)], sems.at[i]
        )
        for i in range(count)
    ]
    for copy in copies:
        copy.start()
    for copy in copies:
        copy.wait()
    loaded[...] = jnp.zeros_like(loaded)


def mix_kernel(cols, counts, values, cotangent, weight, bias_rows, *rest):
    pieces, (out, held) = rest[:9], rest[9:]
    slots = values.shape[1]
    chunks, _, _ = out.shape
    width = cotangent.shape[1] // chunks
    rows = values.shape[0] // chunks

    first, second, third = pieces[2:4], pieces[4:6], (pieces[6], pieces[8])
    farthest = (pieces[7], pieces[8].at[2])
    for server in range(2):
        held[node_near(0, 0, server)] = pieces[server][...]
        held[node_near(*FARTHEST, server)] = farthest[server][...]
        for shards, steps in ((first, FIRST), (second, SECOND), (third, THIRD)):
            for q, near in enumerate(pair_near(back(steps), server)):
                held[near] = shards[server][q]
    for j in range(chunks):
        out[j, :, width : 2 * width] = cotangent[:16, j * width : (j + 1) * width]
        out[j, :, 2 * width : 3 * width] = cotangent[16:, j * width : (j + 1) * width]
        out[j, :, 3 * width : 3 * width + 256] = weight[...]
        out[j, :, 3 * width + 256 :] = bias_rows[...]

    for j in range(chunks):
        for i in range(rows):
            r = j * rows + i
            count = counts[r]
            parts = []
            for s in range(slots):
                group, lane = place_of(cols[r, s])
                block = held[group, :, pl.ds(lane, BLOCK)]
                parts.append(jnp.where(s < count, block, jnp.zeros_like(block)))
            total = jnp.dot(
                jnp.concatenate(parts, axis=1),
                values[r].reshape(slots * BLOCK, BLOCK),
                preferred_element_type=F32,
            )
            out[j, :, i * BLOCK : (i + 1) * BLOCK] = total.astype(BF)


def dense_kernel(both, mask, out):
    width = mask.shape[1] // 8
    mixed = both[:, :, :width].reshape(128, width)
    cotangent = jnp.concatenate(
        [both[:, :, width : 2 * width], both[:, :, 2 * width : 3 * width]], axis=1
    ).reshape(256, width)
    weight = both[:, :, 3 * width : 3 * width + 256].reshape(128, 256)
    bias_rows = both[:, :, 3 * width + 256 :].reshape(128, 256)
    kept = mask[:, pl.ds(pl.multiple_of(lax.axis_index("feat") * width, BLOCK), width)]
    preact = lax.dot_general(
        jnp.concatenate([weight, bias_rows], axis=0),
        jnp.concatenate([mixed, jnp.ones_like(mixed)], axis=0),
        (((0,), (0,)), ((), ())),
        preferred_element_type=F32,
    )
    sigma = jax.nn.sigmoid(preact)
    activation = (preact * sigma).astype(BF).reshape(8, 32, width)
    slope = sigma * (1.0 + preact * (1.0 - sigma))
    grad_pre = (cotangent.astype(F32) * kept.astype(F32) * slope).astype(BF)
    grad_mixed = jnp.dot(weight, grad_pre, preferred_element_type=F32)
    grad_weight = lax.dot_general(
        mixed, grad_pre, (((1,), (1,)), ((), ())), preferred_element_type=F32
    )
    out[:, :, :width] = grad_mixed.astype(BF).reshape(8, 16, width)
    out[:, :, width : width + 256] = grad_weight.astype(BF).reshape(8, 16, 256)
    out[:, :, width + 256 : 2 * width + 256] = activation[:, :16]
    out[:, :, 2 * width + 256 :] = activation[:, 16:]


def spread_kernel(
    cols, counts, values, grads, activation, own1, other1, own2, other2, total
):
    slots = values.shape[1]
    chunks = grads.shape[0]
    rows = values.shape[0] // chunks
    nodes = total.shape[2]
    width = nodes // chunks

    total[...] = jnp.zeros_like(total)
    weight_part = jnp.zeros((16, 256), F32)
    for j in range(chunks):
        at = slice(j * width, (j + 1) * width)
        activation[:16, at] = grads[j, :, width + 256 : 2 * width + 256]
        activation[16:, at] = grads[j, :, 2 * width + 256 :]
        weight_part += grads[j, :, width : width + 256].astype(F32)

    for j in range(chunks):
        for i in range(rows):
            r = j * rows + i
            count = counts[r]
            contrib = lax.dot_general(
                grads[j, :, i * BLOCK : (i + 1) * BLOCK],
                values[r].reshape(slots * BLOCK, BLOCK),
                (((1,), (1,)), ((), ())),
                preferred_element_type=F32,
            )
            for s in range(slots):
                group, lane = place_of(cols[r, s])
                group = jnp.where(s < count, group, 16)
                total[group, :, pl.ds(lane, BLOCK)] += contrib[:, s * BLOCK : (s + 1) * BLOCK]

    weight_part = weight_part.astype(BF)
    for server, to1, to2 in ((0, own1, own2), (1, other1, other2)):
        nears1 = [node_near(*FARTHEST, server)]
        nears1 += pair_near(back(SECOND), server) + pair_near(back(THIRD), server)
        nears2 = pair_near(back(FIRST), server) + [node_near(0, 0, server)]
        for to, nears in ((to1, nears1), (to2, nears2)):
            for k, near in enumerate(nears):
                to[k, :, :nodes] = total[near].astype(BF)
                to[k, :, nodes:] = weight_part


def pair_kernel(own, other, farthest, second, third):
    def both(k):
        return (own[k].astype(F32) + other[k].astype(F32)).astype(BF)

    farthest[...] = both(0)
    for q in range(2):
        second[q] = both(1 + q)
        third[q] = both(3 + q)


def merge_kernel(own, other, forwarded, first, stay):
    def both(k):
        return own[k].astype(F32) + other[k].astype(F32)

    first[0] = (both(0) + forwarded[...].astype(F32)).astype(BF)
    first[1] = both(1).astype(BF)
    stay[...] = both(2).astype(BF)


def hand_kernel(first, second, third, out):
    out[...] = (first[1].astype(F32) + second[1].astype(F32) + third[1].astype(F32)).astype(BF)


def last_kernel(stay, handed, first, second, third, grad_features, grad_weight):
    total = stay[...].astype(F32) + handed[...].astype(F32)
    for piece in (first, second, third):
        total += piece[0].astype(F32)
    nodes = grad_features.shape[1]
    grad_features[...] = total[:, :nodes].astype(BF)
    grad_weight[...] = total[:, nodes:]


def local(features, weight, bias, block_values, block_cols, block_counts, train_mask, cotangent):
    fin, nodes = features.shape
    width = nodes // 8

    def shape(dims, kind=BF):
        return jax.ShapeDtypeStruct(dims, kind)

    bias_at = lax.dynamic_update_slice(
        jnp.zeros((1, 256), F32), bias[None, :], (0, lax.axis_index("feat") * bias.shape[0])
    )
    high = lax.reduce_precision(bias_at, 8, 7)
    middle = lax.reduce_precision(bias_at - high, 8, 7)
    bias_rows = jnp.concatenate(
        [high, middle, bias_at - high - middle, jnp.zeros((13, 256), F32)], axis=0
    ).astype(BF)

    swap = node_pairs(0, 0, 1)
    pieces = [features, lax.ppermute(features, "node", swap)]
    pair = pl.pallas_call(
        stack_kernel,
        in_specs=[VMEM] * 2,
        out_specs=VMEM,
        out_shape=shape((2, fin, nodes)),
        compiler_params=params(4),
        name="stack",
    )(*pieces)
    def send(piece, steps):
        return lax.ppermute(piece, "node", shared_pairs(steps))

    first, second, third = (send(pair, steps) for steps in (FIRST, SECOND, THIRD))
    picked = pl.pallas_call(
        pick_kernel,
        in_specs=[VMEM],
        out_specs=VMEM,
        out_shape=shape((fin, nodes)),
        compiler_params=params(4),
        name="pick",
    )(first)
    forwarded = send(picked, FORWARD)
    values, loaded = pl.pallas_call(
        load_kernel,
        in_specs=[pl.BlockSpec(memory_space=pltpu.HBM)] + [ANY] * 3,
        out_specs=[VMEM, VMEM],
        out_shape=[pltpu.VMEM(block_values.shape, BF), shape((8, 128), F32)],
        scratch_shapes=[pltpu.SemaphoreType.DMA((8,))],
        compiler_params=params(4),
        cost_estimate=pl.CostEstimate(
            flops=0, bytes_accessed=2 * block_values.size * 2, transcendentals=0
        ),
        name="load",
    )(
        pltpu.with_memory_space_constraint(block_values, pltpu.HBM),
        picked,
        bias_rows,
        block_cols,
    )

    def bundle(*parts):
        return pl.pallas_call(
            bundle_kernel,
            in_specs=[ANY] + [VMEM] * len(parts),
            out_specs=VMEM,
            out_shape=shape((sum(part.ndim - 1 for part in parts), fin, nodes)),
            compiler_params=params(8),
            name="bundle",
        )(loaded, *parts)

    pieces += [first, lax.ppermute(first, "node", swap)]
    pieces += [second, lax.ppermute(bundle(second), "node", swap)]
    pieces += [third, forwarded, lax.ppermute(bundle(third, forwarded), "node", swap)]

    mixed = pl.pallas_call(
        mix_kernel,
        in_specs=[SMEM, SMEM] + [VMEM] * 13,
        out_specs=VMEM,
        out_shape=shape((8, 16, 3 * width + 512)),
        scratch_shapes=[pltpu.VMEM((16, fin, nodes), BF)],
        compiler_params=params(16),
        name="mix",
    )(block_cols, block_counts, values, cotangent, weight, bias_rows, *pieces)

    both = lax.all_to_all(mixed, "feat", 0, 0, tiled=True)

    dense = pl.pallas_call(
        dense_kernel,
        in_specs=[VMEM] * 2,
        out_specs=VMEM,
        out_shape=shape((8, 16, 3 * width + 256)),
        compiler_params=params(16),
        name="dense",
    )(both, train_mask[None, :])

    grads = lax.all_to_all(dense, "feat", 0, 0, tiled=True)

    wide = nodes + 256
    activation, own1, other1, own2, other2 = pl.pallas_call(
        spread_kernel,
        in_specs=[SMEM, SMEM] + [VMEM] * 2,
        out_specs=[VMEM] * 5,
        out_shape=[shape((32, nodes))]
        + [shape((5, 16, wide))] * 2
        + [shape((3, 16, wide))] * 2,
        scratch_shapes=[pltpu.VMEM((17, fin, nodes), F32)],
        compiler_params=params(24),
        name="spread",
    )(block_cols, block_counts, values, grads)

    other1 = lax.ppermute(other1, "node", swap)
    other2 = lax.ppermute(other2, "node", swap)
    farthest, second, third = pl.pallas_call(
        pair_kernel,
        in_specs=[VMEM] * 2,
        out_specs=[VMEM] * 3,
        out_shape=[shape((16, wide))] + [shape((2, 16, wide))] * 2,
        compiler_params=params(16),
        name="pair",
    )(own1, other1)
    forwarded = send(farthest, back(FORWARD))
    second, third = send(second, back(SECOND)), send(third, back(THIRD))
    first, stay = pl.pallas_call(
        merge_kernel,
        in_specs=[VMEM] * 3,
        out_specs=[VMEM] * 2,
        out_shape=[shape((2, 16, wide)), shape((16, wide))],
        compiler_params=params(16),
        name="merge",
    )(own2, other2, forwarded)
    first = send(first, back(FIRST))
    handed = pl.pallas_call(
        hand_kernel,
        in_specs=[VMEM] * 3,
        out_specs=VMEM,
        out_shape=shape((16, wide)),
        compiler_params=params(16),
        name="hand",
    )(first, second, third)
    handed = lax.ppermute(handed, "node", swap)
    grad_features, grad_weight = pl.pallas_call(
        last_kernel,
        in_specs=[VMEM] * 5,
        out_specs=[VMEM] * 2,
        out_shape=[shape((16, nodes)), shape((16, 256), F32)],
        compiler_params=params(16),
        name="last",
    )(stay, handed, first, second, third)
    return activation, grad_features, grad_weight


def solution(mesh):
    placed = (
        P("feat", "node"),
        P("feat", None),
        P("feat"),
        P("node", None, None, None),
        P("node", None),
        P("node"),
        P("node"),
        P("feat", "node"),
    )
    return jax.shard_map(
        local,
        mesh=mesh,
        in_specs=placed,
        out_specs=(P("feat", "node"), P("feat", "node"), P("feat", None)),
        check_vma=False,
    )
```

```python
import functools

import jax
import jax.numpy as jnp
from jax import lax
from jax.experimental import pallas as pl
from jax.experimental.pallas import tpu as pltpu
from jax.sharding import PartitionSpec as P

BF = jnp.bfloat16
F32 = jnp.float32
ANY = pl.BlockSpec(memory_space=pl.ANY)
SMEM = pl.BlockSpec(memory_space=pltpu.SMEM)
VMEM = pl.BlockSpec(memory_space=pltpu.VMEM)
STEPS = ((1, 2), (1, 1), (1, 3), (0, 2), (1, 0), (0, 1), (0, 3))
NEAREST = ((0, 1), (0, 3), (0, 2), (1, 0), (1, 1), (1, 3), (1, 2))
HAND_OVERS = ((0, 3), (3, 5), (5, 8))
EARLY_SUM = 3
BLOCK = 128


def node_at(x, z, core):
    return (x * 4 + z) * 2 + core


def node_pairs(dx, dz, dcore=0):
    return [
        (node_at(x, z, c), node_at(x ^ dx, (z + dz) % 4, c ^ dcore))
        for x in range(2)
        for z in range(4)
        for c in range(2)
    ]


def node_near(dx, dz, dcore):
    me = lax.axis_index("node")
    x, z, c = me >> 3, (me >> 1) & 3, me & 1
    return ((x ^ dx) * 4 + ((z + dz) & 3)) * 2 + (c ^ dcore)


def place_of(column):
    group = lax.shift_right_logical(column * 21846, 20)
    return group, pl.multiple_of((column - group * 48) * BLOCK, BLOCK)


def params(mib):
    return pltpu.CompilerParams(vmem_limit_bytes=mib * 2**20)


def bundle_kernel(_, *refs):
    pieces, out = refs[:-1], refs[-1]
    for at, piece in enumerate(pieces):
        out[at] = piece[...]


def load_kernel(values, *rest):
    out, loaded, sems = rest[-3:]
    count = sems.shape[0]
    rows = out.shape[0] // count
    copies = [
        pltpu.make_async_copy(
            values.at[pl.ds(i * rows, rows)], out.at[pl.ds(i * rows, rows)], sems.at[i]
        )
        for i in range(count)
    ]
    for copy in copies:
        copy.start()
    for copy in copies:
        copy.wait()
    loaded[...] = jnp.zeros_like(loaded)


def mix_kernel(cols, counts, values, cotangent, weight, bias_rows, *rest):
    pieces, bundles, (out, held) = rest[:8], rest[8:11], rest[11:]
    slots = values.shape[1]
    chunks, _, _ = out.shape
    width = cotangent.shape[1] // chunks
    rows = values.shape[0] // chunks

    for at, (dx, dz) in enumerate(((0, 0),) + NEAREST):
        held[node_near(dx, -dz, 0)] = pieces[at][...]
    for bundle, (start, end) in zip(bundles, HAND_OVERS):
        for at in range(start, end):
            dx, dz = (((0, 0),) + NEAREST)[at]
            held[node_near(dx, -dz, 1)] = bundle[at - start]
    for j in range(chunks):
        out[j, :, width : 2 * width] = cotangent[:16, j * width : (j + 1) * width]
        out[j, :, 2 * width : 3 * width] = cotangent[16:, j * width : (j + 1) * width]
        out[j, :, 3 * width : 3 * width + 256] = weight[...]
        out[j, :, 3 * width + 256 :] = bias_rows[...]

    for j in range(chunks):
        for i in range(rows):
            r = j * rows + i
            count = counts[r]
            parts = []
            for s in range(slots):
                group, lane = place_of(cols[r, s])
                block = held[group, :, pl.ds(lane, BLOCK)]
                parts.append(jnp.where(s < count, block, jnp.zeros_like(block)))
            total = jnp.dot(
                jnp.concatenate(parts, axis=1),
                values[r].reshape(slots * BLOCK, BLOCK),
                preferred_element_type=F32,
            )
            out[j, :, i * BLOCK : (i + 1) * BLOCK] = total.astype(BF)


def dense_kernel(both, mask, out):
    width = mask.shape[1] // 8
    mixed = both[:, :, :width].reshape(128, width)
    cotangent = jnp.concatenate(
        [both[:, :, width : 2 * width], both[:, :, 2 * width : 3 * width]], axis=1
    ).reshape(256, width)
    weight = both[:, :, 3 * width : 3 * width + 256].reshape(128, 256)
    bias_rows = both[:, :, 3 * width + 256 :].reshape(128, 256)
    kept = mask[:, pl.ds(pl.multiple_of(lax.axis_index("feat") * width, BLOCK), width)]
    preact = lax.dot_general(
        jnp.concatenate([weight, bias_rows], axis=0),
        jnp.concatenate([mixed, jnp.ones_like(mixed)], axis=0),
        (((0,), (0,)), ((), ())),
        preferred_element_type=F32,
    )
    sigma = jax.nn.sigmoid(preact)
    activation = (preact * sigma).astype(BF).reshape(8, 32, width)
    slope = sigma * (1.0 + preact * (1.0 - sigma))
    grad_pre = (cotangent.astype(F32) * kept.astype(F32) * slope).astype(BF)
    grad_mixed = jnp.dot(weight, grad_pre, preferred_element_type=F32)
    grad_weight = lax.dot_general(
        mixed, grad_pre, (((1,), (1,)), ((), ())), preferred_element_type=F32
    )
    out[:, :, :width] = grad_mixed.astype(BF).reshape(8, 16, width)
    out[:, :, width : width + 256] = grad_weight.astype(BF).reshape(8, 16, 256)
    out[:, :, width + 256 : 2 * width + 256] = activation[:, :16]
    out[:, :, 2 * width + 256 :] = activation[:, 16:]


def spread_kernel(
    cols, counts, values, grads, activation, own1, other1, own2, other2, total
):
    slots = values.shape[1]
    chunks = grads.shape[0]
    rows = values.shape[0] // chunks
    nodes = total.shape[2]
    width = nodes // chunks

    total[...] = jnp.zeros_like(total)
    weight_part = jnp.zeros((16, 256), F32)
    for j in range(chunks):
        at = slice(j * width, (j + 1) * width)
        activation[:16, at] = grads[j, :, width + 256 : 2 * width + 256]
        activation[16:, at] = grads[j, :, 2 * width + 256 :]
        weight_part += grads[j, :, width : width + 256].astype(F32)

    for j in range(chunks):
        for i in range(rows):
            r = j * rows + i
            count = counts[r]
            contrib = lax.dot_general(
                grads[j, :, i * BLOCK : (i + 1) * BLOCK],
                values[r].reshape(slots * BLOCK, BLOCK),
                (((1,), (1,)), ((), ())),
                preferred_element_type=F32,
            )
            for s in range(slots):
                group, lane = place_of(cols[r, s])
                group = jnp.where(s < count, group, 16)
                total[group, :, pl.ds(lane, BLOCK)] += contrib[:, s * BLOCK : (s + 1) * BLOCK]

    weight_part = weight_part.astype(BF)
    for server, to1, to2 in ((0, own1, own2), (1, other1, other2)):
        nears = [node_near(dx, dz, server) for dx, dz in STEPS + ((0, 0),)]
        nears1, nears2 = nears[:EARLY_SUM], nears[EARLY_SUM:]
        for to, nears in ((to1, nears1), (to2, nears2)):
            for k, near in enumerate(nears):
                to[k, :, :nodes] = total[near].astype(BF)
                to[k, :, nodes:] = weight_part


def pair_kernel(own, other, *outs):
    for k, out in enumerate(outs):
        out[...] = (own[k].astype(F32) + other[k].astype(F32)).astype(BF)


def last_kernel(*refs):
    pieces, grad_features, grad_weight = refs[:8], refs[8], refs[9]
    total = pieces[0][...].astype(F32)
    for piece in pieces[1:]:
        total += piece[...].astype(F32)
    nodes = grad_features.shape[1]
    grad_features[...] = total[:, :nodes].astype(BF)
    grad_weight[...] = total[:, nodes:]


def local(features, weight, bias, block_values, block_cols, block_counts, train_mask, cotangent):
    fin, nodes = features.shape
    width = nodes // 8

    def shape(dims, kind=BF):
        return jax.ShapeDtypeStruct(dims, kind)

    bias_at = lax.dynamic_update_slice(
        jnp.zeros((1, 256), F32), bias[None, :], (0, lax.axis_index("feat") * bias.shape[0])
    )
    high = lax.reduce_precision(bias_at, 8, 7)
    middle = lax.reduce_precision(bias_at - high, 8, 7)
    bias_rows = jnp.concatenate(
        [high, middle, bias_at - high - middle, jnp.zeros((13, 256), F32)], axis=0
    ).astype(BF)

    swap = node_pairs(0, 0, 1)
    pieces = [features]
    pieces += [lax.ppermute(features, "node", node_pairs(*step)) for step in NEAREST]

    values, loaded = pl.pallas_call(
        load_kernel,
        in_specs=[pl.BlockSpec(memory_space=pltpu.HBM)] + [ANY] * 4,
        out_specs=[VMEM, VMEM],
        out_shape=[pltpu.VMEM(block_values.shape, BF), shape((8, 128), F32)],
        scratch_shapes=[pltpu.SemaphoreType.DMA((8,))],
        compiler_params=params(4),
        cost_estimate=pl.CostEstimate(
            flops=0, bytes_accessed=2 * block_values.size * 2, transcendentals=0
        ),
        name="load",
    )(
        pltpu.with_memory_space_constraint(block_values, pltpu.HBM),
        *pieces[1:3],
        bias_rows,
        block_cols,
    )

    bundles = []
    for start, end in HAND_OVERS:
        bundle = pl.pallas_call(
            bundle_kernel,
            in_specs=[ANY] + [VMEM] * (end - start),
            out_specs=VMEM,
            out_shape=shape((end - start, fin, nodes)),
            compiler_params=params(8),
            name="bundle",
        )(loaded if start > 0 else pieces[1], *pieces[start:end])
        bundles.append(lax.ppermute(bundle, "node", swap))

    mixed = pl.pallas_call(
        mix_kernel,
        in_specs=[SMEM, SMEM] + [VMEM] * 15,
        out_specs=VMEM,
        out_shape=shape((8, 16, 3 * width + 512)),
        scratch_shapes=[pltpu.VMEM((16, fin, nodes), BF)],
        compiler_params=params(16),
        name="mix",
    )(block_cols, block_counts, values, cotangent, weight, bias_rows, *pieces, *bundles)

    both = lax.all_to_all(mixed, "feat", 0, 0, tiled=True)

    dense = pl.pallas_call(
        dense_kernel,
        in_specs=[VMEM] * 2,
        out_specs=VMEM,
        out_shape=shape((8, 16, 3 * width + 256)),
        compiler_params=params(16),
        name="dense",
    )(both, train_mask[None, :])

    grads = lax.all_to_all(dense, "feat", 0, 0, tiled=True)

    wide = nodes + 256
    counts = (EARLY_SUM, 8 - EARLY_SUM)
    activation, own1, other1, own2, other2 = pl.pallas_call(
        spread_kernel,
        in_specs=[SMEM, SMEM] + [VMEM] * 2,
        out_specs=[VMEM] * 5,
        out_shape=[shape((32, nodes))]
        + [shape((count, 16, wide)) for count in counts for _ in range(2)],
        scratch_shapes=[pltpu.VMEM((17, fin, nodes), F32)],
        compiler_params=params(24),
        name="spread",
    )(block_cols, block_counts, values, grads)

    sums = []
    for own, other in ((own1, other1), (own2, other2)):
        sums += pl.pallas_call(
            pair_kernel,
            in_specs=[VMEM] * 2,
            out_specs=[VMEM] * own.shape[0],
            out_shape=[shape((16, wide))] * own.shape[0],
            compiler_params=params(16),
            name="pair",
        )(own, lax.ppermute(other, "node", swap))
    landed = [lax.ppermute(part, "node", node_pairs(*step)) for part, step in zip(sums, STEPS)]
    grad_features, grad_weight = pl.pallas_call(
        last_kernel,
        in_specs=[VMEM] * 8,
        out_specs=[VMEM] * 2,
        out_shape=[shape((16, nodes)), shape((16, 256), F32)],
        compiler_params=params(16),
        name="last",
    )(sums[-1], *landed)
    return activation, grad_features, grad_weight


def solution(mesh):
    placed = (
        P("feat", "node"),
        P("feat", None),
        P("feat"),
        P("node", None, None, None),
        P("node", None),
        P("node"),
        P("node"),
        P("feat", "node"),
    )
    return jax.shard_map(
        local,
        mesh=mesh,
        in_specs=placed,
        out_specs=(P("feat", "node"), P("feat", "node"), P("feat", None)),
        check_vma=False,
    )
```

```python
import functools

import jax
import jax.numpy as jnp
from jax import lax
from jax.experimental import pallas as pl
from jax.experimental.pallas import tpu as pltpu
from jax.sharding import PartitionSpec as P

BF = jnp.bfloat16
F32 = jnp.float32
ANY = pl.BlockSpec(memory_space=pl.ANY)
SMEM = pl.BlockSpec(memory_space=pltpu.SMEM)
VMEM = pl.BlockSpec(memory_space=pltpu.VMEM)
STEPS = ((1, 2), (1, 1), (1, 3), (0, 2), (1, 0), (0, 1), (0, 3))
GATHERED = ((0, 1), (1, 0), (0, 2), (1, 3), (1, 1), (1, 2), (0, 3))
EARLY_SUM = 3
BLOCK = 128


def node_at(x, z, core):
    return (x * 4 + z) * 2 + core


def node_pairs(dx, dz, dcore=0):
    return [
        (node_at(x, z, c), node_at(x ^ dx, (z + dz) % 4, c ^ dcore))
        for x in range(2)
        for z in range(4)
        for c in range(2)
    ]


def node_near(dx, dz, dcore):
    me = lax.axis_index("node")
    x, z, c = me >> 3, (me >> 1) & 3, me & 1
    return ((x ^ dx) * 4 + ((z + dz) & 3)) * 2 + (c ^ dcore)


def place_of(column):
    group = lax.shift_right_logical(column * 21846, 20)
    return group, pl.multiple_of((column - group * 48) * BLOCK, BLOCK)


def params(mib):
    return pltpu.CompilerParams(vmem_limit_bytes=mib * 2**20)


def mix_kernel(cols, counts, stored, cotangent, weight, bias_rows, *rest):
    pieces, (out, values, held, sems) = rest[:16], rest[16:]
    slots = values.shape[1]
    chunks, _, _ = out.shape
    width = cotangent.shape[1] // chunks
    rows = values.shape[0] // chunks

    copies = []
    for j in range(chunks):
        part = pl.ds(j * rows, rows)
        copies.append(pltpu.make_async_copy(stored.at[part], values.at[part], sems.at[j]))
        copies[j].start()
    for at, (dx, dz) in enumerate(((0, 0),) + GATHERED):
        for core in range(2):
            held[node_near(dx, -dz, core)] = pieces[2 * at + core][...]
    for j in range(chunks):
        out[j, :, width : 2 * width] = cotangent[:16, j * width : (j + 1) * width]
        out[j, :, 2 * width : 3 * width] = cotangent[16:, j * width : (j + 1) * width]
        out[j, :, 3 * width : 3 * width + 256] = weight[...]
        out[j, :, 3 * width + 256 :] = bias_rows[...]

    for j in range(chunks):
        copies[j].wait()
        for i in range(rows):
            r = j * rows + i
            count = counts[r]
            parts = []
            for s in range(slots):
                group, lane = place_of(cols[r, s])
                block = held[group, :, pl.ds(lane, BLOCK)]
                parts.append(jnp.where(s < count, block, jnp.zeros_like(block)))
            total = jnp.dot(
                jnp.concatenate(parts, axis=1),
                values[r].reshape(slots * BLOCK, BLOCK),
                preferred_element_type=F32,
            )
            out[j, :, i * BLOCK : (i + 1) * BLOCK] = total.astype(BF)


def dense_kernel(both, mask, out):
    width = mask.shape[1] // 8
    mixed = both[:, :, :width].reshape(128, width)
    cotangent = jnp.concatenate(
        [both[:, :, width : 2 * width], both[:, :, 2 * width : 3 * width]], axis=1
    ).reshape(256, width)
    weight = both[:, :, 3 * width : 3 * width + 256].reshape(128, 256)
    bias_rows = both[:, :, 3 * width + 256 :].reshape(128, 256)
    kept = mask[:, pl.ds(pl.multiple_of(lax.axis_index("feat") * width, BLOCK), width)]
    preact = lax.dot_general(
        jnp.concatenate([weight, bias_rows], axis=0),
        jnp.concatenate([mixed, jnp.ones_like(mixed)], axis=0),
        (((0,), (0,)), ((), ())),
        preferred_element_type=F32,
    )
    sigma = jax.nn.sigmoid(preact)
    activation = (preact * sigma).astype(BF).reshape(8, 32, width)
    slope = sigma * (1.0 + preact * (1.0 - sigma))
    grad_pre = (cotangent.astype(F32) * kept.astype(F32) * slope).astype(BF)
    grad_mixed = jnp.dot(weight, grad_pre, preferred_element_type=F32)
    grad_weight = lax.dot_general(
        mixed, grad_pre, (((1,), (1,)), ((), ())), preferred_element_type=F32
    )
    out[:, :, :width] = grad_mixed.astype(BF).reshape(8, 16, width)
    out[:, :, width : width + 256] = grad_weight.astype(BF).reshape(8, 16, 256)
    out[:, :, width + 256 : 2 * width + 256] = activation[:, :16]
    out[:, :, 2 * width + 256 :] = activation[:, 16:]


def spread_kernel(
    cols, counts, values, grads, activation, own1, other1, own2, other2, total
):
    slots = values.shape[1]
    chunks = grads.shape[0]
    rows = values.shape[0] // chunks
    nodes = total.shape[2]
    width = nodes // chunks

    total[...] = jnp.zeros_like(total)
    weight_part = jnp.zeros((16, 256), F32)
    for j in range(chunks):
        at = slice(j * width, (j + 1) * width)
        activation[:16, at] = grads[j, :, width + 256 : 2 * width + 256]
        activation[16:, at] = grads[j, :, 2 * width + 256 :]
        weight_part += grads[j, :, width : width + 256].astype(F32)

    for j in range(chunks):
        for i in range(rows):
            r = j * rows + i
            count = counts[r]
            contrib = lax.dot_general(
                grads[j, :, i * BLOCK : (i + 1) * BLOCK],
                values[r].reshape(slots * BLOCK, BLOCK),
                (((1,), (1,)), ((), ())),
                preferred_element_type=F32,
            )
            for s in range(slots):
                group, lane = place_of(cols[r, s])
                group = jnp.where(s < count, group, 16)
                total[group, :, pl.ds(lane, BLOCK)] += contrib[:, s * BLOCK : (s + 1) * BLOCK]

    weight_part = weight_part.astype(BF)
    for server, to1, to2 in ((0, own1, own2), (1, other1, other2)):
        nears = [node_near(dx, dz, server) for dx, dz in STEPS + ((0, 0),)]
        nears1, nears2 = nears[:EARLY_SUM], nears[EARLY_SUM:]
        for to, nears in ((to1, nears1), (to2, nears2)):
            for k, near in enumerate(nears):
                to[k, :, :nodes] = total[near].astype(BF)
                to[k, :, nodes:] = weight_part


def pair_kernel(own, other, *outs):
    for k, out in enumerate(outs):
        out[...] = (own[k].astype(F32) + other[k].astype(F32)).astype(BF)


def last_kernel(*refs):
    pieces, grad_features, grad_weight = refs[:8], refs[8], refs[9]
    total = pieces[0][...].astype(F32)
    for piece in pieces[1:]:
        total += piece[...].astype(F32)
    nodes = grad_features.shape[1]
    grad_features[...] = total[:, :nodes].astype(BF)
    grad_weight[...] = total[:, nodes:]


def local(features, weight, bias, block_values, block_cols, block_counts, train_mask, cotangent):
    fin, nodes = features.shape
    width = nodes // 8

    def shape(dims, kind=BF):
        return jax.ShapeDtypeStruct(dims, kind)

    bias_at = lax.dynamic_update_slice(
        jnp.zeros((1, 256), F32), bias[None, :], (0, lax.axis_index("feat") * bias.shape[0])
    )
    high = lax.reduce_precision(bias_at, 8, 7)
    middle = lax.reduce_precision(bias_at - high, 8, 7)
    bias_rows = jnp.concatenate(
        [high, middle, bias_at - high - middle, jnp.zeros((13, 256), F32)], axis=0
    ).astype(BF)

    swap = node_pairs(0, 0, 1)
    pieces = [features, lax.ppermute(features, "node", swap)]
    for step in GATHERED:
        piece = lax.ppermute(features, "node", node_pairs(*step))
        pieces += [piece, lax.ppermute(piece, "node", swap)]

    mixed, values = pl.pallas_call(
        mix_kernel,
        in_specs=[SMEM, SMEM, pl.BlockSpec(memory_space=pltpu.HBM)] + [VMEM] * 19,
        out_specs=[VMEM, VMEM],
        out_shape=[shape((8, 16, 3 * width + 512)), pltpu.VMEM(block_values.shape, BF)],
        scratch_shapes=[pltpu.VMEM((16, fin, nodes), BF), pltpu.SemaphoreType.DMA((8,))],
        compiler_params=params(16),
        name="mix",
    )(
        block_cols,
        block_counts,
        pltpu.with_memory_space_constraint(block_values, pltpu.HBM),
        cotangent,
        weight,
        bias_rows,
        *pieces,
    )

    both = lax.all_to_all(mixed, "feat", 0, 0, tiled=True)

    dense = pl.pallas_call(
        dense_kernel,
        in_specs=[VMEM] * 2,
        out_specs=VMEM,
        out_shape=shape((8, 16, 3 * width + 256)),
        compiler_params=params(16),
        name="dense",
    )(both, train_mask[None, :])

    grads = lax.all_to_all(dense, "feat", 0, 0, tiled=True)

    wide = nodes + 256
    counts = (EARLY_SUM, 8 - EARLY_SUM)
    activation, own1, other1, own2, other2 = pl.pallas_call(
        spread_kernel,
        in_specs=[SMEM, SMEM] + [VMEM] * 2,
        out_specs=[VMEM] * 5,
        out_shape=[shape((32, nodes))]
        + [shape((count, 16, wide)) for count in counts for _ in range(2)],
        scratch_shapes=[pltpu.VMEM((17, fin, nodes), F32)],
        compiler_params=params(24),
        name="spread",
    )(block_cols, block_counts, values, grads)

    sums = []
    for own, other in ((own1, other1), (own2, other2)):
        sums += pl.pallas_call(
            pair_kernel,
            in_specs=[VMEM] * 2,
            out_specs=[VMEM] * own.shape[0],
            out_shape=[shape((16, wide))] * own.shape[0],
            compiler_params=params(16),
            name="pair",
        )(own, lax.ppermute(other, "node", swap))
    landed = [lax.ppermute(part, "node", node_pairs(*step)) for part, step in zip(sums, STEPS)]
    grad_features, grad_weight = pl.pallas_call(
        last_kernel,
        in_specs=[VMEM] * 8,
        out_specs=[VMEM] * 2,
        out_shape=[shape((16, nodes)), shape((16, 256), F32)],
        compiler_params=params(16),
        name="last",
    )(sums[-1], *landed)
    return activation, grad_features, grad_weight


def solution(mesh):
    placed = (
        P("feat", "node"),
        P("feat", None),
        P("feat"),
        P("node", None, None, None),
        P("node", None),
        P("node"),
        P("node"),
        P("feat", "node"),
    )
    return jax.shard_map(
        local,
        mesh=mesh,
        in_specs=placed,
        out_specs=(P("feat", "node"), P("feat", "node"), P("feat", None)),
        check_vma=False,
    )
```

```python
import functools

import jax
import jax.numpy as jnp
from jax import lax
from jax.experimental import pallas as pl
from jax.experimental.pallas import tpu as pltpu
from jax.sharding import PartitionSpec as P

BF = jnp.bfloat16
F32 = jnp.float32
ANY = pl.BlockSpec(memory_space=pl.ANY)
SMEM = pl.BlockSpec(memory_space=pltpu.SMEM)
VMEM = pl.BlockSpec(memory_space=pltpu.VMEM)
FIRST = ((1, 0), (0, 2))
SECOND = ((1, 3), (1, 1))
THIRD = ((0, 3), (0, 1))
FORWARD = ((0, 2), (1, 0))
FARTHEST = (1, 2)
BLOCK = 128


def node_at(x, z, core):
    return (x * 4 + z) * 2 + core


def node_pairs(dx, dz, dcore=0):
    return [
        (node_at(x, z, c), node_at(x ^ dx, (z + dz) % 4, c ^ dcore))
        for x in range(2)
        for z in range(4)
        for c in range(2)
    ]


def node_near(dx, dz, dcore):
    me = lax.axis_index("node")
    x, z, c = me >> 3, (me >> 1) & 3, me & 1
    return ((x ^ dx) * 4 + ((z + dz) & 3)) * 2 + (c ^ dcore)


def shared_pairs(steps):
    return [
        (node_at(x, z, c), node_at(x ^ steps[c][0], (z + steps[c][1]) % 4, c))
        for x in range(2)
        for z in range(4)
        for c in range(2)
    ]


def back(steps):
    return tuple((dx, -dz % 4) for dx, dz in steps)


def shared_near(steps, server, dcore):
    core = (lax.axis_index("node") & 1) ^ server
    dx = jnp.where(core == 0, steps[0][0], steps[1][0])
    dz = jnp.where(core == 0, steps[0][1], steps[1][1])
    return node_near(dx, dz, dcore)


def pair_near(steps, server):
    return [shared_near(steps, server, server ^ q) for q in range(2)]


def place_of(column):
    group = lax.shift_right_logical(column * 21846, 20)
    return group, pl.multiple_of((column - group * 48) * BLOCK, BLOCK)


def params(mib):
    return pltpu.CompilerParams(vmem_limit_bytes=mib * 2**20)


def place_kernel(at, shard, *rest):
    out, sem = rest[-2:]
    copy = pltpu.make_async_copy(shard, out.at[at], sem)
    copy.start()
    copy.wait()


def bundle_kernel(_, *refs):
    pieces, out = refs[:-1], refs[-1]
    at = 0
    for piece in pieces:
        if len(piece.shape) == 3:
            out[at : at + 2] = piece[...]
            at += 2
        else:
            out[at] = piece[...]
            at += 1


def pick_kernel(pair, out):
    out[...] = pair[0]


def load_kernel(values, *rest):
    out, loaded, sems = rest[-3:]
    count = sems.shape[0]
    rows = out.shape[0] // count
    copies = [
        pltpu.make_async_copy(
            values.at[pl.ds(i * rows, rows)], out.at[pl.ds(i * rows, rows)], sems.at[i]
        )
        for i in range(count)
    ]
    for copy in copies:
        copy.start()
    for copy in copies:
        copy.wait()
    loaded[...] = jnp.zeros_like(loaded)


def mix_kernel(cols, counts, values, cotangent, weight, bias, *rest):
    pieces, (out, held) = rest[:9], rest[9:]
    slots = values.shape[1]
    chunks, _, _ = out.shape
    width = cotangent.shape[1] // chunks
    rows = values.shape[0] // chunks

    hidden = bias.shape[1]
    high = bias[...].astype(BF).astype(F32)
    middle = (bias[...] - high).astype(BF).astype(F32)
    row = lax.broadcasted_iota(jnp.int32, (16, hidden), 0)
    parts = jnp.where(row == 1, middle, jnp.where(row == 2, bias[...] - high - middle, 0.0))
    parts = jnp.where(row == 0, high, parts).astype(BF)
    place = lax.broadcasted_iota(jnp.int32, (hidden, 256), 1) - lax.axis_index("feat") * hidden
    place = place == lax.broadcasted_iota(jnp.int32, (hidden, 256), 0)
    bias_rows = jnp.dot(
        parts, jnp.where(place, 1.0, 0.0).astype(BF), preferred_element_type=F32
    ).astype(BF)

    first, second, third = pieces[2:4], pieces[4:6], (pieces[6], pieces[8])
    farthest = (pieces[7], pieces[8].at[2])
    for server in range(2):
        held[node_near(0, 0, server)] = pieces[server][...]
        held[node_near(*FARTHEST, server)] = farthest[server][...]
        for shards, steps in ((first, FIRST), (second, SECOND), (third, THIRD)):
            for q, near in enumerate(pair_near(back(steps), server)):
                held[near] = shards[server][q]
    for j in range(chunks):
        out[j, :, width : 2 * width] = cotangent[:16, j * width : (j + 1) * width]
        out[j, :, 2 * width : 3 * width] = cotangent[16:, j * width : (j + 1) * width]
        out[j, :, 3 * width : 3 * width + 256] = weight[...]
        out[j, :, 3 * width + 256 :] = bias_rows

    for j in range(chunks):
        for i in range(rows):
            r = j * rows + i
            count = counts[r]
            parts = []
            for s in range(slots):
                group, lane = place_of(cols[s, r])
                block = held[group, :, pl.ds(lane, BLOCK)]
                parts.append(jnp.where(s < count, block, jnp.zeros_like(block)))
            total = jnp.dot(
                jnp.concatenate(parts, axis=1),
                values[r].reshape(slots * BLOCK, BLOCK),
                preferred_element_type=F32,
            )
            out[j, :, i * BLOCK : (i + 1) * BLOCK] = total.astype(BF)


def dense_kernel(both, mask, out):
    width = mask.shape[1] // 8
    mixed = both[:, :, :width].reshape(128, width)
    cotangent = jnp.concatenate(
        [both[:, :, width : 2 * width], both[:, :, 2 * width : 3 * width]], axis=1
    ).reshape(256, width)
    weight = both[:, :, 3 * width : 3 * width + 256].reshape(128, 256)
    bias_rows = both[:, :, 3 * width + 256 :].reshape(128, 256)
    kept = mask[:, pl.ds(pl.multiple_of(lax.axis_index("feat") * width, BLOCK), width)]
    preact = lax.dot_general(
        jnp.concatenate([weight, bias_rows], axis=0),
        jnp.concatenate([mixed, jnp.ones_like(mixed)], axis=0),
        (((0,), (0,)), ((), ())),
        preferred_element_type=F32,
    )
    sigma = jax.nn.sigmoid(preact)
    activation = (preact * sigma).astype(BF).reshape(8, 32, width)
    slope = sigma * (1.0 + preact * (1.0 - sigma))
    grad_pre = (cotangent.astype(F32) * kept.astype(F32) * slope).astype(BF)
    grad_mixed = jnp.dot(weight, grad_pre, preferred_element_type=F32)
    grad_weight = lax.dot_general(
        mixed, grad_pre, (((1,), (1,)), ((), ())), preferred_element_type=F32
    )
    out[:, :, :width] = grad_mixed.astype(BF).reshape(8, 16, width)
    out[:, :, width : width + 256] = grad_weight.astype(BF).reshape(8, 16, 256)
    out[:, :, width + 256 : 2 * width + 256] = activation[:, :16]
    out[:, :, 2 * width + 256 :] = activation[:, 16:]


def spread_kernel(
    cols, counts, values, grads, activation, *rest
):
    groups, total = rest[:-1], rest[-1]
    slots = values.shape[1]
    chunks = grads.shape[0]
    rows = values.shape[0] // chunks
    nodes = total.shape[2]
    width = nodes // chunks

    total[...] = jnp.zeros_like(total)
    weight_part = jnp.zeros((16, 256), F32)
    for j in range(chunks):
        at = slice(j * width, (j + 1) * width)
        activation[:16, at] = grads[j, :, width + 256 : 2 * width + 256]
        activation[16:, at] = grads[j, :, 2 * width + 256 :]
        weight_part += grads[j, :, width : width + 256].astype(F32)

    for j in range(chunks):
        for i in range(rows):
            r = j * rows + i
            count = counts[r]
            contrib = lax.dot_general(
                grads[j, :, i * BLOCK : (i + 1) * BLOCK],
                values[r].reshape(slots * BLOCK, BLOCK),
                (((1,), (1,)), ((), ())),
                preferred_element_type=F32,
            )
            for s in range(slots):
                group, lane = place_of(cols[s, r])
                group = jnp.where(s < count, group, 16)
                total[group, :, pl.ds(lane, BLOCK)] += contrib[:, s * BLOCK : (s + 1) * BLOCK]

    weight_part = weight_part.astype(BF)
    for server in range(2):
        nears = [node_near(*FARTHEST, server)]
        for steps in (SECOND, THIRD, FIRST):
            nears += pair_near(back(steps), server)
        nears.append(node_near(0, 0, server))
        for group in groups[server::2]:
            for k in range(group.shape[0]):
                near = nears.pop(0)
                group[k, :, :nodes] = total[near].astype(BF)
                group[k, :, nodes:] = weight_part


def both(own, other, k):
    return own[k].astype(F32) + other[k].astype(F32)


def pair_kernel(own, other, _, farthest, second, third, later):
    farthest[...] = both(own, other, 0).astype(BF)
    for q in range(2):
        second[q] = both(own, other, 1 + q).astype(BF)
        third[q] = both(own, other, 3 + q).astype(BF)


def merge_kernel(own, other, forwarded, first, stay):
    first[0] = (both(own, other, 0) + forwarded[...].astype(F32)).astype(BF)
    first[1] = both(own, other, 1).astype(BF)
    stay[...] = both(own, other, 2).astype(BF)


def hand_kernel(first, second, third, out):
    out[...] = (first[1].astype(F32) + second[1].astype(F32) + third[1].astype(F32)).astype(BF)


def last_kernel(stay, handed, first, second, third, grad_features, grad_weight):
    total = stay[...].astype(F32) + handed[...].astype(F32)
    for piece in (first, second, third):
        total += piece[0].astype(F32)
    nodes = grad_features.shape[1]
    grad_features[...] = total[:, :nodes].astype(BF)
    grad_weight[...] = total[:, nodes:]


def local(features, weight, bias, block_values, block_cols, block_counts, train_mask, cotangent):
    fin, nodes = features.shape
    width = nodes // 8

    block_cols = block_cols.T

    def shape(dims, kind=BF):
        return jax.ShapeDtypeStruct(dims, kind)

    swap = node_pairs(0, 0, 1)
    pieces = [features, lax.ppermute(features, "node", swap)]
    pair = features
    for at, shard in enumerate(pieces):
        pair = pl.pallas_call(
            functools.partial(place_kernel, at),
            in_specs=[ANY] * (1 + at),
            out_specs=ANY,
            out_shape=shape((2, fin, nodes)),
            scratch_shapes=[pltpu.SemaphoreType.DMA],
            input_output_aliases={1: 0} if at else {},
            compiler_params=params(4),
            name="place",
        )(*([shard, pair][: 1 + at]))

    def send(piece, steps):
        return lax.ppermute(piece, "node", shared_pairs(steps))

    first, second, third = (send(pair, steps) for steps in (FIRST, SECOND, THIRD))
    picked = pl.pallas_call(
        pick_kernel,
        in_specs=[VMEM],
        out_specs=VMEM,
        out_shape=shape((fin, nodes)),
        compiler_params=params(4),
        name="pick",
    )(first)
    forwarded = send(picked, FORWARD)
    values, loaded = pl.pallas_call(
        load_kernel,
        in_specs=[pl.BlockSpec(memory_space=pltpu.HBM), ANY],
        out_specs=[VMEM, VMEM],
        out_shape=[pltpu.VMEM(block_values.shape, BF), shape((8, 128), F32)],
        scratch_shapes=[pltpu.SemaphoreType.DMA((8,))],
        compiler_params=params(4),
        cost_estimate=pl.CostEstimate(
            flops=0, bytes_accessed=2 * block_values.size * 2, transcendentals=0
        ),
        name="load",
    )(
        pltpu.with_memory_space_constraint(block_values, pltpu.HBM),
        picked,
    )

    def bundle(*parts):
        return pl.pallas_call(
            bundle_kernel,
            in_specs=[ANY] + [VMEM] * len(parts),
            out_specs=VMEM,
            out_shape=shape((sum(part.ndim - 1 for part in parts), fin, nodes)),
            compiler_params=params(8),
            name="bundle",
        )(loaded, *parts)

    pieces += [first, lax.ppermute(first, "node", swap)]
    pieces += [second, lax.ppermute(bundle(second), "node", swap)]
    pieces += [third, forwarded, lax.ppermute(bundle(third, forwarded), "node", swap)]

    mixed = pl.pallas_call(
        mix_kernel,
        in_specs=[SMEM, SMEM] + [VMEM] * 13,
        out_specs=VMEM,
        out_shape=shape((8, 16, 3 * width + 512)),
        scratch_shapes=[pltpu.VMEM((16, fin, nodes), BF)],
        compiler_params=params(16),
        name="mix",
    )(block_cols, block_counts, values, cotangent, weight, bias[None, :], *pieces)

    both = lax.all_to_all(mixed, "feat", 0, 0, tiled=True)

    dense = pl.pallas_call(
        dense_kernel,
        in_specs=[VMEM] * 2,
        out_specs=VMEM,
        out_shape=shape((8, 16, 3 * width + 256)),
        compiler_params=params(16),
        name="dense",
    )(both, train_mask[None, :])

    grads = lax.all_to_all(dense, "feat", 0, 0, tiled=True)

    wide = nodes + 256
    activation, own1, other1, own2, other2 = pl.pallas_call(
        spread_kernel,
        in_specs=[SMEM, SMEM] + [VMEM] * 2,
        out_specs=[VMEM] * 5,
        out_shape=[shape((32, nodes))]
        + [shape((count, 16, wide)) for count in (5, 3) for _ in range(2)],
        scratch_shapes=[pltpu.VMEM((17, fin, nodes), F32)],
        compiler_params=params(24),
        name="spread",
    )(block_cols, block_counts, values, grads)

    other1 = lax.ppermute(other1, "node", swap)
    farthest, second, third, other2 = pl.pallas_call(
        pair_kernel,
        in_specs=[VMEM, VMEM, ANY],
        out_specs=[VMEM, VMEM, VMEM, ANY],
        out_shape=[shape((16, wide))] + [shape((2, 16, wide))] * 2 + [shape((3, 16, wide))],
        input_output_aliases={2: 3},
        compiler_params=params(16),
        name="pair",
    )(own1, other1, other2)
    forwarded = send(farthest, back(FORWARD))
    second, third = send(second, back(SECOND)), send(third, back(THIRD))
    other2 = lax.ppermute(other2, "node", swap)
    first, stay = pl.pallas_call(
        merge_kernel,
        in_specs=[VMEM] * 3,
        out_specs=[VMEM] * 2,
        out_shape=[shape((2, 16, wide)), shape((16, wide))],
        compiler_params=params(16),
        name="merge",
    )(own2, other2, forwarded)
    first = send(first, back(FIRST))
    handed = pl.pallas_call(
        hand_kernel,
        in_specs=[VMEM] * 3,
        out_specs=VMEM,
        out_shape=shape((16, wide)),
        compiler_params=params(16),
        name="hand",
    )(first, second, third)
    handed = lax.ppermute(handed, "node", swap)
    grad_features, grad_weight = pl.pallas_call(
        last_kernel,
        in_specs=[VMEM] * 5,
        out_specs=[VMEM] * 2,
        out_shape=[shape((16, nodes)), shape((16, 256), F32)],
        compiler_params=params(16),
        name="last",
    )(stay, handed, first, second, third)
    return activation, grad_features, grad_weight


def solution(mesh):
    placed = (
        P("feat", "node"),
        P("feat", None),
        P("feat"),
        P("node", None, None, None),
        P("node", None),
        P("node"),
        P("node"),
        P("feat", "node"),
    )
    return jax.shard_map(
        local,
        mesh=mesh,
        in_specs=placed,
        out_specs=(P("feat", "node"), P("feat", "node"), P("feat", None)),
        check_vma=False,
    )
```

```python
import functools

import jax
import jax.numpy as jnp
from jax import lax
from jax.experimental import pallas as pl
from jax.experimental.pallas import tpu as pltpu
from jax.sharding import PartitionSpec as P

BF = jnp.bfloat16
F32 = jnp.float32
ANY = pl.BlockSpec(memory_space=pl.ANY)
HBM = pl.BlockSpec(memory_space=pltpu.HBM)
VMEM = pl.BlockSpec(memory_space=pltpu.VMEM)
FIRST = ((1, 0), (0, 2))
SECOND = ((1, 3), (1, 1))
THIRD = ((0, 3), (0, 1))
FORWARD = ((0, 2), (1, 0))
FARTHEST = (1, 2)
BLOCK = 128


def node_at(x, z, core):
    return (x * 4 + z) * 2 + core


def node_pairs(dx, dz, dcore=0):
    return [
        (node_at(x, z, c), node_at(x ^ dx, (z + dz) % 4, c ^ dcore))
        for x in range(2)
        for z in range(4)
        for c in range(2)
    ]


def node_near(dx, dz, dcore):
    me = lax.axis_index("node")
    x, z, c = me >> 3, (me >> 1) & 3, me & 1
    return ((x ^ dx) * 4 + ((z + dz) & 3)) * 2 + (c ^ dcore)


def shared_pairs(steps):
    return [
        (node_at(x, z, c), node_at(x ^ steps[c][0], (z + steps[c][1]) % 4, c))
        for x in range(2)
        for z in range(4)
        for c in range(2)
    ]


def back(steps):
    return tuple((dx, -dz % 4) for dx, dz in steps)


def shared_near(steps, server, dcore):
    core = (lax.axis_index("node") & 1) ^ server
    dx = jnp.where(core == 0, steps[0][0], steps[1][0])
    dz = jnp.where(core == 0, steps[0][1], steps[1][1])
    return node_near(dx, dz, dcore)


def pair_near(steps, server):
    return [shared_near(steps, server, server ^ q) for q in range(2)]


def place_of(column):
    group = lax.shift_right_logical(column * 21846, 20)
    return group, pl.multiple_of((column - group * 48) * BLOCK, BLOCK)


def params(mib):
    return pltpu.CompilerParams(vmem_limit_bytes=mib * 2**20)


def place_kernel(at, shard, *rest):
    out, sem = rest[-2:]
    copy = pltpu.make_async_copy(shard, out.at[at], sem)
    copy.start()
    copy.wait()


def pick_kernel(pair, _, out):
    out[...] = pair[0]


def load_kernel(values, *rest):
    out, loaded, sems = rest[-3:]
    count = sems.shape[0]
    rows = out.shape[0] // count
    copies = [
        pltpu.make_async_copy(
            values.at[pl.ds(i * rows, rows)], out.at[pl.ds(i * rows, rows)], sems.at[i]
        )
        for i in range(count)
    ]
    for copy in copies:
        copy.start()
    for copy in copies:
        copy.wait()
    loaded[...] = jnp.zeros_like(loaded)


def start_small(sources, places, sems):
    copies = [
        pltpu.make_async_copy(source, place, sems.at[at])
        for at, (source, place) in enumerate(zip(sources, places))
    ]
    for copy in copies:
        copy.start()
    return copies


def mix_kernel(cols_in, counts_in, values, cotangent, weight, bias, *rest):
    pieces, (out, held, cols, counts, sems) = rest[:10], rest[10:]
    small = start_small((cols_in, counts_in), (cols, counts), sems)
    slots = values.shape[1]
    chunks, _, _ = out.shape
    width = cotangent.shape[1] // chunks
    rows = values.shape[0] // chunks

    hidden = bias.shape[1]
    high = bias[...].astype(BF).astype(F32)
    middle = (bias[...] - high).astype(BF).astype(F32)
    row = lax.broadcasted_iota(jnp.int32, (16, hidden), 0)
    parts = jnp.where(row == 1, middle, jnp.where(row == 2, bias[...] - high - middle, 0.0))
    parts = jnp.where(row == 0, high, parts).astype(BF)
    place = lax.broadcasted_iota(jnp.int32, (hidden, 256), 1) - lax.axis_index("feat") * hidden
    place = place == lax.broadcasted_iota(jnp.int32, (hidden, 256), 0)
    bias_rows = jnp.dot(
        parts, jnp.where(place, 1.0, 0.0).astype(BF), preferred_element_type=F32
    ).astype(BF)

    first, second, third, farthest = (pieces[at : at + 2] for at in (2, 4, 6, 8))
    for server in range(2):
        held[node_near(0, 0, server)] = pieces[server][...]
        held[node_near(*FARTHEST, server)] = farthest[server][...]
        for shards, steps in ((first, FIRST), (second, SECOND), (third, THIRD)):
            for q, near in enumerate(pair_near(back(steps), server)):
                held[near] = shards[server][q]
    for j in range(chunks):
        out[j, :, width : 2 * width] = cotangent[:16, j * width : (j + 1) * width]
        out[j, :, 2 * width : 3 * width] = cotangent[16:, j * width : (j + 1) * width]
        out[j, :, 3 * width : 3 * width + 256] = weight[...]
        out[j, :, 3 * width + 256 :] = bias_rows

    for copy in small:
        copy.wait()
    for j in range(chunks):
        for i in range(rows):
            r = j * rows + i
            count = counts[r]
            parts = []
            for s in range(slots):
                group, lane = place_of(cols[s, r])
                block = held[group, :, pl.ds(lane, BLOCK)]
                parts.append(jnp.where(s < count, block, jnp.zeros_like(block)))
            total = jnp.dot(
                jnp.concatenate(parts, axis=1),
                values[r].reshape(slots * BLOCK, BLOCK),
                preferred_element_type=F32,
            )
            out[j, :, i * BLOCK : (i + 1) * BLOCK] = total.astype(BF)


def dense_kernel(both, mask, out):
    width = mask.shape[1] // 8
    mixed = both[:, :, :width].reshape(128, width)
    cotangent = jnp.concatenate(
        [both[:, :, width : 2 * width], both[:, :, 2 * width : 3 * width]], axis=1
    ).reshape(256, width)
    weight = both[:, :, 3 * width : 3 * width + 256].reshape(128, 256)
    bias_rows = both[:, :, 3 * width + 256 :].reshape(128, 256)
    kept = mask[:, pl.ds(pl.multiple_of(lax.axis_index("feat") * width, BLOCK), width)]
    preact = lax.dot_general(
        jnp.concatenate([weight, bias_rows], axis=0),
        jnp.concatenate([mixed, jnp.ones_like(mixed)], axis=0),
        (((0,), (0,)), ((), ())),
        preferred_element_type=F32,
    )
    sigma = jax.nn.sigmoid(preact)
    activation = (preact * sigma).astype(BF).reshape(8, 32, width)
    slope = sigma * (1.0 + preact * (1.0 - sigma))
    grad_pre = (cotangent.astype(F32) * kept.astype(F32) * slope).astype(BF)
    grad_mixed = jnp.dot(weight, grad_pre, preferred_element_type=F32)
    grad_weight = lax.dot_general(
        mixed, grad_pre, (((1,), (1,)), ((), ())), preferred_element_type=F32
    )
    out[:, :, :width] = grad_mixed.astype(BF).reshape(8, 16, width)
    out[:, :, width : width + 256] = grad_weight.astype(BF).reshape(8, 16, 256)
    out[:, :, width + 256 : 2 * width + 256] = activation[:, :16]
    out[:, :, 2 * width + 256 :] = activation[:, 16:]


def spread_kernel(
    cols_in, counts_in, values, grads, activation, *rest
):
    groups, (total, cols, counts, sems) = rest[:-4], rest[-4:]
    small = start_small((cols_in, counts_in), (cols, counts), sems)
    slots = values.shape[1]
    chunks = grads.shape[0]
    rows = values.shape[0] // chunks
    nodes = total.shape[2]
    width = nodes // chunks

    total[...] = jnp.zeros_like(total)
    weight_part = jnp.zeros((16, 256), F32)
    for j in range(chunks):
        at = slice(j * width, (j + 1) * width)
        activation[:16, at] = grads[j, :, width + 256 : 2 * width + 256]
        activation[16:, at] = grads[j, :, 2 * width + 256 :]
        weight_part += grads[j, :, width : width + 256].astype(F32)

    for copy in small:
        copy.wait()
    for j in range(chunks):
        for i in range(rows):
            r = j * rows + i
            count = counts[r]
            contrib = lax.dot_general(
                grads[j, :, i * BLOCK : (i + 1) * BLOCK],
                values[r].reshape(slots * BLOCK, BLOCK),
                (((1,), (1,)), ((), ())),
                preferred_element_type=F32,
            )
            for s in range(slots):
                group, lane = place_of(cols[s, r])
                group = jnp.where(s < count, group, 16)
                total[group, :, pl.ds(lane, BLOCK)] += contrib[:, s * BLOCK : (s + 1) * BLOCK]

    weight_part = weight_part.astype(BF)
    for server in range(2):
        nears = [node_near(*FARTHEST, server)]
        for steps in (SECOND, THIRD, FIRST):
            nears += pair_near(back(steps), server)
        nears.append(node_near(0, 0, server))
        for group in groups[server::2]:
            for k in range(group.shape[0]):
                near = nears.pop(0)
                group[k, :, :nodes] = total[near].astype(BF)
                group[k, :, nodes:] = weight_part


def both(own, other, k):
    return own[k].astype(F32) + other[k].astype(F32)


def pair_kernel(own, other, _, farthest, second, later):
    farthest[...] = both(own, other, 0).astype(BF)
    for q in range(2):
        second[q] = both(own, other, 1 + q).astype(BF)


def third_kernel(own, other, third):
    for q in range(2):
        third[q] = both(own, other, q).astype(BF)


def merge_kernel(own, other, forwarded, first, stay):
    first[0] = (both(own, other, 2) + forwarded[...].astype(F32)).astype(BF)
    first[1] = both(own, other, 3).astype(BF)
    stay[...] = both(own, other, 4).astype(BF)


def hand_kernel(first, second, third, out):
    out[...] = (first[1].astype(F32) + second[1].astype(F32) + third[1].astype(F32)).astype(BF)


def last_kernel(stay, handed, first, second, third, grad_features, grad_weight):
    total = stay[...].astype(F32) + handed[...].astype(F32)
    for piece in (first, second, third):
        total += piece[0].astype(F32)
    nodes = grad_features.shape[1]
    grad_features[...] = total[:, :nodes].astype(BF)
    grad_weight[...] = total[:, nodes:]


def local(features, weight, bias, block_values, block_cols, block_counts, train_mask, cotangent):
    fin, nodes = features.shape
    width = nodes // 8

    block_cols = pltpu.with_memory_space_constraint(block_cols.T, pltpu.HBM)
    block_counts = pltpu.with_memory_space_constraint(block_counts, pltpu.HBM)

    def shape(dims, kind=BF):
        return jax.ShapeDtypeStruct(dims, kind)

    swap = node_pairs(0, 0, 1)
    pieces = [features, lax.ppermute(features, "node", swap)]
    pair = features
    for at, shard in enumerate(pieces):
        pair = pl.pallas_call(
            functools.partial(place_kernel, at),
            in_specs=[ANY] * (1 + at),
            out_specs=ANY,
            out_shape=shape((2, fin, nodes)),
            scratch_shapes=[pltpu.SemaphoreType.DMA],
            input_output_aliases={1: 0} if at else {},
            compiler_params=params(4),
            name="place",
        )(*([shard, pair][: 1 + at]))

    def send(piece, steps):
        return lax.ppermute(piece, "node", shared_pairs(steps))

    first, second, third = (send(pair, steps) for steps in (FIRST, SECOND, THIRD))
    values, loaded = pl.pallas_call(
        load_kernel,
        in_specs=[pl.BlockSpec(memory_space=pltpu.HBM), ANY],
        out_specs=[VMEM, VMEM],
        out_shape=[pltpu.VMEM(block_values.shape, BF), shape((8, 128), F32)],
        scratch_shapes=[pltpu.SemaphoreType.DMA((8,))],
        compiler_params=params(4),
        cost_estimate=pl.CostEstimate(
            flops=0, bytes_accessed=2 * block_values.size * 2, transcendentals=0
        ),
        name="load",
    )(pltpu.with_memory_space_constraint(block_values, pltpu.HBM), pair)
    picked = pl.pallas_call(
        pick_kernel,
        in_specs=[VMEM, ANY],
        out_specs=VMEM,
        out_shape=shape((fin, nodes)),
        compiler_params=params(4),
        name="pick",
    )(first, loaded)
    forwarded = send(picked, FORWARD)
    for piece in (first, second, third, forwarded):
        pieces += [piece, lax.ppermute(piece, "node", swap)]

    index_scratch = [
        pltpu.SMEM(block_cols.shape, jnp.int32),
        pltpu.SMEM(block_counts.shape, jnp.int32),
        pltpu.SemaphoreType.DMA((2,)),
    ]
    mixed = pl.pallas_call(
        mix_kernel,
        in_specs=[HBM, HBM] + [VMEM] * 14,
        out_specs=VMEM,
        out_shape=shape((8, 16, 3 * width + 512)),
        scratch_shapes=[pltpu.VMEM((16, fin, nodes), BF)] + index_scratch,
        compiler_params=params(16),
        name="mix",
    )(block_cols, block_counts, values, cotangent, weight, bias[None, :], *pieces)

    both = lax.all_to_all(mixed, "feat", 0, 0, tiled=True)

    dense = pl.pallas_call(
        dense_kernel,
        in_specs=[VMEM] * 2,
        out_specs=VMEM,
        out_shape=shape((8, 16, 3 * width + 256)),
        compiler_params=params(16),
        name="dense",
    )(both, train_mask[None, :])

    grads = lax.all_to_all(dense, "feat", 0, 0, tiled=True)

    wide = nodes + 256
    activation, own1, other1, own2, other2 = pl.pallas_call(
        spread_kernel,
        in_specs=[HBM, HBM] + [VMEM] * 2,
        out_specs=[VMEM] * 5,
        out_shape=[shape((32, nodes))]
        + [shape((count, 16, wide)) for count in (3, 5) for _ in range(2)],
        scratch_shapes=[pltpu.VMEM((17, fin, nodes), F32)] + index_scratch,
        compiler_params=params(24),
        name="spread",
    )(block_cols, block_counts, values, grads)

    other1 = lax.ppermute(other1, "node", swap)
    farthest, second, other2 = pl.pallas_call(
        pair_kernel,
        in_specs=[VMEM, VMEM, ANY],
        out_specs=[VMEM, VMEM, ANY],
        out_shape=[shape((16, wide)), shape((2, 16, wide)), shape((5, 16, wide))],
        input_output_aliases={2: 2},
        compiler_params=params(16),
        name="pair",
    )(own1, other1, other2)
    forwarded = send(farthest, back(FORWARD))
    second = send(second, back(SECOND))
    other2 = lax.ppermute(other2, "node", swap)
    third = pl.pallas_call(
        third_kernel,
        in_specs=[VMEM] * 2,
        out_specs=VMEM,
        out_shape=shape((2, 16, wide)),
        compiler_params=params(16),
        name="third",
    )(own2, other2)
    third = send(third, back(THIRD))
    first, stay = pl.pallas_call(
        merge_kernel,
        in_specs=[VMEM] * 3,
        out_specs=[VMEM] * 2,
        out_shape=[shape((2, 16, wide)), shape((16, wide))],
        compiler_params=params(16),
        name="merge",
    )(own2, other2, forwarded)
    first = send(first, back(FIRST))
    handed = pl.pallas_call(
        hand_kernel,
        in_specs=[VMEM] * 3,
        out_specs=VMEM,
        out_shape=shape((16, wide)),
        compiler_params=params(16),
        name="hand",
    )(first, second, third)
    handed = lax.ppermute(handed, "node", swap)
    grad_features, grad_weight = pl.pallas_call(
        last_kernel,
        in_specs=[VMEM] * 5,
        out_specs=[VMEM] * 2,
        out_shape=[shape((16, nodes)), shape((16, 256), F32)],
        compiler_params=params(16),
        name="last",
    )(stay, handed, first, second, third)
    return activation, grad_features, grad_weight


def solution(mesh):
    placed = (
        P("feat", "node"),
        P("feat", None),
        P("feat"),
        P("node", None, None, None),
        P("node", None),
        P("node"),
        P("node"),
        P("feat", "node"),
    )
    return jax.shard_map(
        local,
        mesh=mesh,
        in_specs=placed,
        out_specs=(P("feat", "node"), P("feat", "node"), P("feat", None)),
        check_vma=False,
    )
```

```python
import functools

import jax
import jax.numpy as jnp
from jax import lax
from jax.experimental import pallas as pl
from jax.experimental.pallas import tpu as pltpu
from jax.sharding import PartitionSpec as P

BF = jnp.bfloat16
F32 = jnp.float32
ANY = pl.BlockSpec(memory_space=pl.ANY)
HBM = pl.BlockSpec(memory_space=pltpu.HBM)
VMEM = pl.BlockSpec(memory_space=pltpu.VMEM)
FIRST = ((1, 0), (0, 2))
SECOND = ((1, 3), (1, 1))
THIRD = ((0, 3), (0, 1))
FORWARD = ((0, 2), (1, 0))
FARTHEST = (1, 2)
BLOCK = 128


def node_at(x, z, core):
    return (x * 4 + z) * 2 + core


def node_pairs(dx, dz, dcore=0):
    return [
        (node_at(x, z, c), node_at(x ^ dx, (z + dz) % 4, c ^ dcore))
        for x in range(2)
        for z in range(4)
        for c in range(2)
    ]


def node_near(dx, dz, dcore):
    me = lax.axis_index("node")
    x, z, c = me >> 3, (me >> 1) & 3, me & 1
    return ((x ^ dx) * 4 + ((z + dz) & 3)) * 2 + (c ^ dcore)


def shared_pairs(steps):
    return [
        (node_at(x, z, c), node_at(x ^ steps[c][0], (z + steps[c][1]) % 4, c))
        for x in range(2)
        for z in range(4)
        for c in range(2)
    ]


def back(steps):
    return tuple((dx, -dz % 4) for dx, dz in steps)


def shared_near(steps, server, dcore):
    core = (lax.axis_index("node") & 1) ^ server
    dx = jnp.where(core == 0, steps[0][0], steps[1][0])
    dz = jnp.where(core == 0, steps[0][1], steps[1][1])
    return node_near(dx, dz, dcore)


def pair_near(steps, server):
    return [shared_near(steps, server, server ^ q) for q in range(2)]


def place_of(column):
    group = lax.shift_right_logical(column * 21846, 20)
    return group, pl.multiple_of((column - group * 48) * BLOCK, BLOCK)


def params(mib):
    return pltpu.CompilerParams(vmem_limit_bytes=mib * 2**20)


def place_kernel(at, shard, *rest):
    out, sem = rest[-2:]
    copy = pltpu.make_async_copy(shard, out.at[at], sem)
    copy.start()
    copy.wait()


def gate_kernel(*refs):
    pass


def load_kernel(values, *rest):
    out, loaded, sems = rest[-3:]
    count = sems.shape[0]
    rows = out.shape[0] // count
    copies = [
        pltpu.make_async_copy(
            values.at[pl.ds(i * rows, rows)], out.at[pl.ds(i * rows, rows)], sems.at[i]
        )
        for i in range(count)
    ]
    for copy in copies:
        copy.start()
    for copy in copies:
        copy.wait()
    loaded[...] = jnp.zeros_like(loaded)


def start_small(sources, places, sems):
    copies = [
        pltpu.make_async_copy(source, place, sems.at[at])
        for at, (source, place) in enumerate(zip(sources, places))
    ]
    for copy in copies:
        copy.start()
    return copies


def mix_kernel(cols_in, counts_in, values, cotangent, weight, bias, *rest):
    pieces, (out, held, cols, counts, sems) = rest[:12], rest[12:]
    small = start_small((cols_in, counts_in), (cols, counts), sems)
    slots = values.shape[1]
    chunks, _, _ = out.shape
    width = cotangent.shape[1] // chunks
    rows = values.shape[0] // chunks

    hidden = bias.shape[1]
    high = bias[...].astype(BF).astype(F32)
    middle = (bias[...] - high).astype(BF).astype(F32)
    row = lax.broadcasted_iota(jnp.int32, (16, hidden), 0)
    parts = jnp.where(row == 1, middle, jnp.where(row == 2, bias[...] - high - middle, 0.0))
    parts = jnp.where(row == 0, high, parts).astype(BF)
    place = lax.broadcasted_iota(jnp.int32, (hidden, 256), 1) - lax.axis_index("feat") * hidden
    place = place == lax.broadcasted_iota(jnp.int32, (hidden, 256), 0)
    bias_rows = jnp.dot(
        parts, jnp.where(place, 1.0, 0.0).astype(BF), preferred_element_type=F32
    ).astype(BF)

    def shard(server, steps, q):
        if steps is FIRST:
            return pieces[2 + 2 * q + server][...]
        return pieces[(6 if steps is SECOND else 8) + server][q]

    for server in range(2):
        held[node_near(0, 0, server)] = pieces[server][...]
        held[node_near(*FARTHEST, server)] = pieces[10 + server][...]
        for steps in (FIRST, SECOND, THIRD):
            for q, near in enumerate(pair_near(back(steps), server)):
                held[near] = shard(server, steps, q)
    for j in range(chunks):
        out[j, :, width : 2 * width] = cotangent[:16, j * width : (j + 1) * width]
        out[j, :, 2 * width : 3 * width] = cotangent[16:, j * width : (j + 1) * width]
        out[j, :, 3 * width : 3 * width + 256] = weight[...]
        out[j, :, 3 * width + 256 :] = bias_rows

    for copy in small:
        copy.wait()
    for j in range(chunks):
        for i in range(rows):
            r = j * rows + i
            count = counts[r]
            parts = []
            for s in range(slots):
                group, lane = place_of(cols[s, r])
                block = held[group, :, pl.ds(lane, BLOCK)]
                parts.append(jnp.where(s < count, block, jnp.zeros_like(block)))
            total = jnp.dot(
                jnp.concatenate(parts, axis=1),
                values[r].reshape(slots * BLOCK, BLOCK),
                preferred_element_type=F32,
            )
            out[j, :, i * BLOCK : (i + 1) * BLOCK] = total.astype(BF)


def dense_kernel(both, mask, out):
    width = mask.shape[1] // 8
    mixed = both[:, :, :width].reshape(128, width)
    cotangent = jnp.concatenate(
        [both[:, :, width : 2 * width], both[:, :, 2 * width : 3 * width]], axis=1
    ).reshape(256, width)
    weight = both[:, :, 3 * width : 3 * width + 256].reshape(128, 256)
    bias_rows = both[:, :, 3 * width + 256 :].reshape(128, 256)
    kept = mask[:, pl.ds(pl.multiple_of(lax.axis_index("feat") * width, BLOCK), width)]
    preact = lax.dot_general(
        jnp.concatenate([weight, bias_rows], axis=0),
        jnp.concatenate([mixed, jnp.ones_like(mixed)], axis=0),
        (((0,), (0,)), ((), ())),
        preferred_element_type=F32,
    )
    sigma = jax.nn.sigmoid(preact)
    activation = (preact * sigma).astype(BF).reshape(8, 32, width)
    slope = sigma * (1.0 + preact * (1.0 - sigma))
    grad_pre = (cotangent.astype(F32) * kept.astype(F32) * slope).astype(BF)
    grad_mixed = jnp.dot(weight, grad_pre, preferred_element_type=F32)
    grad_weight = lax.dot_general(
        mixed, grad_pre, (((1,), (1,)), ((), ())), preferred_element_type=F32
    )
    out[:, :, :width] = grad_mixed.astype(BF).reshape(8, 16, width)
    out[:, :, width : width + 256] = grad_weight.astype(BF).reshape(8, 16, 256)
    out[:, :, width + 256 : 2 * width + 256] = activation[:, :16]
    out[:, :, 2 * width + 256 :] = activation[:, 16:]


def spread_kernel(
    cols_in, counts_in, values, grads, activation, *rest
):
    groups, (total, cols, counts, sems) = rest[:-4], rest[-4:]
    small = start_small((cols_in, counts_in), (cols, counts), sems)
    slots = values.shape[1]
    chunks = grads.shape[0]
    rows = values.shape[0] // chunks
    nodes = total.shape[2]
    width = nodes // chunks

    total[...] = jnp.zeros_like(total)
    weight_part = jnp.zeros((16, 256), F32)
    for j in range(chunks):
        at = slice(j * width, (j + 1) * width)
        activation[:16, at] = grads[j, :, width + 256 : 2 * width + 256]
        activation[16:, at] = grads[j, :, 2 * width + 256 :]
        weight_part += grads[j, :, width : width + 256].astype(F32)

    for copy in small:
        copy.wait()
    for j in range(chunks):
        for i in range(rows):
            r = j * rows + i
            count = counts[r]
            contrib = lax.dot_general(
                grads[j, :, i * BLOCK : (i + 1) * BLOCK],
                values[r].reshape(slots * BLOCK, BLOCK),
                (((1,), (1,)), ((), ())),
                preferred_element_type=F32,
            )
            for s in range(slots):
                group, lane = place_of(cols[s, r])
                group = jnp.where(s < count, group, 16)
                total[group, :, pl.ds(lane, BLOCK)] += contrib[:, s * BLOCK : (s + 1) * BLOCK]

    weight_part = weight_part.astype(BF)
    for server in range(2):
        nears = [node_near(*FARTHEST, server)]
        for steps in (SECOND, THIRD, FIRST):
            nears += pair_near(back(steps), server)
        nears.append(node_near(0, 0, server))
        for group in groups[server::2]:
            for k in range(group.shape[0]):
                near = nears.pop(0)
                group[k, :, :nodes] = total[near].astype(BF)
                group[k, :, nodes:] = weight_part


def both(own, other, k):
    return own[k].astype(F32) + other[k].astype(F32)


def pair_kernel(own, other, _, farthest, second, third, later):
    farthest[...] = both(own, other, 0).astype(BF)
    for q in range(2):
        second[q] = both(own, other, 1 + q).astype(BF)
        third[q] = both(own, other, 3 + q).astype(BF)


def merge_kernel(own, other, forwarded, first, stay):
    first[0] = (both(own, other, 0) + forwarded[...].astype(F32)).astype(BF)
    first[1] = both(own, other, 1).astype(BF)
    stay[...] = both(own, other, 2).astype(BF)


def hand_kernel(first, second, third, out):
    out[...] = (first[1].astype(F32) + second[1].astype(F32) + third[1].astype(F32)).astype(BF)


def last_kernel(stay, handed, first, second, third, grad_features, grad_weight):
    total = stay[...].astype(F32) + handed[...].astype(F32)
    for piece in (first, second, third):
        total += piece[0].astype(F32)
    nodes = grad_features.shape[1]
    grad_features[...] = total[:, :nodes].astype(BF)
    grad_weight[...] = total[:, nodes:]


def local(features, weight, bias, block_values, block_cols, block_counts, train_mask, cotangent):
    fin, nodes = features.shape
    width = nodes // 8

    block_cols = pltpu.with_memory_space_constraint(block_cols.T, pltpu.HBM)
    block_counts = pltpu.with_memory_space_constraint(block_counts, pltpu.HBM)

    def shape(dims, kind=BF):
        return jax.ShapeDtypeStruct(dims, kind)

    swap = node_pairs(0, 0, 1)
    pieces = [features, lax.ppermute(features, "node", swap)]

    def send(piece, steps):
        return lax.ppermute(piece, "node", shared_pairs(steps))

    first = [send(shard, FIRST) for shard in pieces]
    pair = features
    for at, shard in enumerate(pieces):
        pair = pl.pallas_call(
            functools.partial(place_kernel, at),
            in_specs=[ANY] * (1 + 2 * at),
            out_specs=ANY,
            out_shape=shape((2, fin, nodes)),
            scratch_shapes=[pltpu.SemaphoreType.DMA],
            input_output_aliases={1: 0} if at else {},
            compiler_params=params(4),
            name="place",
        )(*([shard, pair, first[0]][: 1 + 2 * at]))

    forwarded = send(first[0], FORWARD)
    second, third = send(pair, SECOND), send(pair, THIRD)
    values, loaded = pl.pallas_call(
        load_kernel,
        in_specs=[pl.BlockSpec(memory_space=pltpu.HBM), ANY],
        out_specs=[VMEM, VMEM],
        out_shape=[pltpu.VMEM(block_values.shape, BF), shape((8, 128), F32)],
        scratch_shapes=[pltpu.SemaphoreType.DMA((8,))],
        compiler_params=params(4),
        cost_estimate=pl.CostEstimate(
            flops=0, bytes_accessed=2 * block_values.size * 2, transcendentals=0
        ),
        name="load",
    )(pltpu.with_memory_space_constraint(block_values, pltpu.HBM), pair)
    def gate(*parts):
        return pl.pallas_call(
            gate_kernel,
            in_specs=[ANY] * (len(parts) + 1),
            out_specs=[ANY] * len(parts),
            out_shape=[shape(part.shape) for part in parts],
            input_output_aliases={at: at for at in range(len(parts))},
            compiler_params=params(4),
            name="gate",
        )(*parts, loaded)

    first[1], third = gate(first[1], third)
    second, forwarded = gate(second, forwarded)
    for piece in (*first, second, third, forwarded):
        pieces += [piece, lax.ppermute(piece, "node", swap)]

    index_scratch = [
        pltpu.SMEM(block_cols.shape, jnp.int32),
        pltpu.SMEM(block_counts.shape, jnp.int32),
        pltpu.SemaphoreType.DMA((2,)),
    ]
    mixed = pl.pallas_call(
        mix_kernel,
        in_specs=[HBM, HBM] + [VMEM] * 16,
        out_specs=VMEM,
        out_shape=shape((8, 16, 3 * width + 512)),
        scratch_shapes=[pltpu.VMEM((16, fin, nodes), BF)] + index_scratch,
        compiler_params=params(16),
        name="mix",
    )(block_cols, block_counts, values, cotangent, weight, bias[None, :], *pieces)

    both = lax.all_to_all(mixed, "feat", 0, 0, tiled=True)

    dense = pl.pallas_call(
        dense_kernel,
        in_specs=[VMEM] * 2,
        out_specs=VMEM,
        out_shape=shape((8, 16, 3 * width + 256)),
        compiler_params=params(16),
        name="dense",
    )(both, train_mask[None, :])

    grads = lax.all_to_all(dense, "feat", 0, 0, tiled=True)

    wide = nodes + 256
    activation, own1, other1, own2, other2 = pl.pallas_call(
        spread_kernel,
        in_specs=[HBM, HBM] + [VMEM] * 2,
        out_specs=[VMEM] * 5,
        out_shape=[shape((32, nodes))]
        + [shape((count, 16, wide)) for count in (5, 3) for _ in range(2)],
        scratch_shapes=[pltpu.VMEM((17, fin, nodes), F32)] + index_scratch,
        compiler_params=params(24),
        name="spread",
    )(block_cols, block_counts, values, grads)

    other1 = lax.ppermute(other1, "node", swap)
    farthest, second, third, other2 = pl.pallas_call(
        pair_kernel,
        in_specs=[VMEM, VMEM, ANY],
        out_specs=[VMEM, VMEM, VMEM, ANY],
        out_shape=[shape((16, wide))] + [shape((2, 16, wide))] * 2 + [shape((3, 16, wide))],
        input_output_aliases={2: 3},
        compiler_params=params(16),
        name="pair",
    )(own1, other1, other2)
    forwarded = send(farthest, back(FORWARD))
    second, third = send(second, back(SECOND)), send(third, back(THIRD))
    other2 = lax.ppermute(other2, "node", swap)
    first, stay = pl.pallas_call(
        merge_kernel,
        in_specs=[VMEM] * 3,
        out_specs=[VMEM] * 2,
        out_shape=[shape((2, 16, wide)), shape((16, wide))],
        compiler_params=params(16),
        name="merge",
    )(own2, other2, forwarded)
    first = send(first, back(FIRST))
    handed = pl.pallas_call(
        hand_kernel,
        in_specs=[VMEM] * 3,
        out_specs=VMEM,
        out_shape=shape((16, wide)),
        compiler_params=params(16),
        name="hand",
    )(first, second, third)
    handed = lax.ppermute(handed, "node", swap)
    grad_features, grad_weight = pl.pallas_call(
        last_kernel,
        in_specs=[VMEM] * 5,
        out_specs=[VMEM] * 2,
        out_shape=[shape((16, nodes)), shape((16, 256), F32)],
        compiler_params=params(16),
        name="last",
    )(stay, handed, first, second, third)
    return activation, grad_features, grad_weight


def solution(mesh):
    placed = (
        P("feat", "node"),
        P("feat", None),
        P("feat"),
        P("node", None, None, None),
        P("node", None),
        P("node"),
        P("node"),
        P("feat", "node"),
    )
    return jax.shard_map(
        local,
        mesh=mesh,
        in_specs=placed,
        out_specs=(P("feat", "node"), P("feat", "node"), P("feat", None)),
        check_vma=False,
    )
```

```python
import functools

import jax
import jax.numpy as jnp
from jax import lax
from jax.experimental import pallas as pl
from jax.experimental.pallas import tpu as pltpu
from jax.sharding import PartitionSpec as P

BF = jnp.bfloat16
F32 = jnp.float32
ANY = pl.BlockSpec(memory_space=pl.ANY)
HBM = pl.BlockSpec(memory_space=pltpu.HBM)
VMEM = pl.BlockSpec(memory_space=pltpu.VMEM)
FIRST = ((1, 0), (0, 2))
SECOND = ((1, 3), (1, 1))
THIRD = ((0, 3), (0, 1))
FORWARD = ((0, 2), (1, 0))
FARTHEST = (1, 2)
BLOCK = 128


def node_at(x, z, core):
    return (x * 4 + z) * 2 + core


def node_pairs(dx, dz, dcore=0):
    return [
        (node_at(x, z, c), node_at(x ^ dx, (z + dz) % 4, c ^ dcore))
        for x in range(2)
        for z in range(4)
        for c in range(2)
    ]


def node_near(dx, dz, dcore):
    me = lax.axis_index("node")
    x, z, c = me >> 3, (me >> 1) & 3, me & 1
    return ((x ^ dx) * 4 + ((z + dz) & 3)) * 2 + (c ^ dcore)


def shared_pairs(steps):
    return [
        (node_at(x, z, c), node_at(x ^ steps[c][0], (z + steps[c][1]) % 4, c))
        for x in range(2)
        for z in range(4)
        for c in range(2)
    ]


def back(steps):
    return tuple((dx, -dz % 4) for dx, dz in steps)


def shared_near(steps, server, dcore):
    core = (lax.axis_index("node") & 1) ^ server
    dx = jnp.where(core == 0, steps[0][0], steps[1][0])
    dz = jnp.where(core == 0, steps[0][1], steps[1][1])
    return node_near(dx, dz, dcore)


def pair_near(steps, server):
    return [shared_near(steps, server, server ^ q) for q in range(2)]


def place_of(column):
    group = lax.shift_right_logical(column * 21846, 20)
    return group, pl.multiple_of((column - group * 48) * BLOCK, BLOCK)


def params(mib):
    return pltpu.CompilerParams(vmem_limit_bytes=mib * 2**20)


def place_kernel(at, shard, *rest):
    out, sem = rest[-2:]
    copy = pltpu.make_async_copy(shard, out.at[at], sem)
    copy.start()
    copy.wait()


def pick_kernel(pair, _, out):
    out[...] = pair[0]


def load_kernel(values, *rest):
    out, loaded, sems = rest[-3:]
    count = sems.shape[0]
    rows = out.shape[0] // count
    copies = [
        pltpu.make_async_copy(
            values.at[pl.ds(i * rows, rows)], out.at[pl.ds(i * rows, rows)], sems.at[i]
        )
        for i in range(count)
    ]
    for copy in copies:
        copy.start()
    for copy in copies:
        copy.wait()
    loaded[...] = jnp.zeros_like(loaded)


def start_small(sources, places, sems):
    copies = [
        pltpu.make_async_copy(source, place, sems.at[at])
        for at, (source, place) in enumerate(zip(sources, places))
    ]
    for copy in copies:
        copy.start()
    return copies


def mix_kernel(cols_in, counts_in, values, cotangent, weight, bias, *rest):
    pieces, (out, held, cols, counts, sems) = rest[:10], rest[10:]
    small = start_small((cols_in, counts_in), (cols, counts), sems)
    slots = values.shape[1]
    chunks, _, _ = out.shape
    width = cotangent.shape[1] // chunks
    rows = values.shape[0] // chunks

    hidden = bias.shape[1]
    high = bias[...].astype(BF).astype(F32)
    middle = (bias[...] - high).astype(BF).astype(F32)
    row = lax.broadcasted_iota(jnp.int32, (16, hidden), 0)
    parts = jnp.where(row == 1, middle, jnp.where(row == 2, bias[...] - high - middle, 0.0))
    parts = jnp.where(row == 0, high, parts).astype(BF)
    place = lax.broadcasted_iota(jnp.int32, (hidden, 256), 1) - lax.axis_index("feat") * hidden
    place = place == lax.broadcasted_iota(jnp.int32, (hidden, 256), 0)
    bias_rows = jnp.dot(
        parts, jnp.where(place, 1.0, 0.0).astype(BF), preferred_element_type=F32
    ).astype(BF)

    first, second, third, farthest = (pieces[at : at + 2] for at in (2, 4, 6, 8))
    for server in range(2):
        held[node_near(0, 0, server)] = pieces[server][...]
        held[node_near(*FARTHEST, server)] = farthest[server][...]
        for shards, steps in ((first, FIRST), (second, SECOND), (third, THIRD)):
            for q, near in enumerate(pair_near(back(steps), server)):
                held[near] = shards[server][q]
    for j in range(chunks):
        out[j, :, width : 2 * width] = cotangent[:16, j * width : (j + 1) * width]
        out[j, :, 2 * width : 3 * width] = cotangent[16:, j * width : (j + 1) * width]
        out[j, :, 3 * width : 3 * width + 256] = weight[...]
        out[j, :, 3 * width + 256 :] = bias_rows

    for copy in small:
        copy.wait()
    for j in range(chunks):
        for i in range(rows):
            r = j * rows + i
            count = counts[r]
            parts = []
            for s in range(slots):
                group, lane = place_of(cols[s, r])
                block = held[group, :, pl.ds(lane, BLOCK)]
                parts.append(jnp.where(s < count, block, jnp.zeros_like(block)))
            total = jnp.dot(
                jnp.concatenate(parts, axis=1),
                values[r].reshape(slots * BLOCK, BLOCK),
                preferred_element_type=F32,
            )
            out[j, :, i * BLOCK : (i + 1) * BLOCK] = total.astype(BF)


def dense_kernel(both, mask, out):
    width = mask.shape[1] // 8
    mixed = both[:, :, :width].reshape(128, width)
    cotangent = jnp.concatenate(
        [both[:, :, width : 2 * width], both[:, :, 2 * width : 3 * width]], axis=1
    ).reshape(256, width)
    weight = both[:, :, 3 * width : 3 * width + 256].reshape(128, 256)
    bias_rows = both[:, :, 3 * width + 256 :].reshape(128, 256)
    kept = mask[:, pl.ds(pl.multiple_of(lax.axis_index("feat") * width, BLOCK), width)]
    preact = lax.dot_general(
        jnp.concatenate([weight, bias_rows], axis=0),
        jnp.concatenate([mixed, jnp.ones_like(mixed)], axis=0),
        (((0,), (0,)), ((), ())),
        preferred_element_type=F32,
    )
    sigma = jax.nn.sigmoid(preact)
    activation = (preact * sigma).astype(BF).reshape(8, 32, width)
    slope = sigma * (1.0 + preact * (1.0 - sigma))
    grad_pre = (cotangent.astype(F32) * kept.astype(F32) * slope).astype(BF)
    grad_mixed = jnp.dot(weight, grad_pre, preferred_element_type=F32)
    grad_weight = lax.dot_general(
        mixed, grad_pre, (((1,), (1,)), ((), ())), preferred_element_type=F32
    )
    out[:, :, :width] = grad_mixed.astype(BF).reshape(8, 16, width)
    out[:, :, width : width + 256] = grad_weight.astype(BF).reshape(8, 16, 256)
    out[:, :, width + 256 : 2 * width + 256] = activation[:, :16]
    out[:, :, 2 * width + 256 :] = activation[:, 16:]


def spread_kernel(
    cols_in, counts_in, values, grads, activation, *rest
):
    groups, (total, cols, counts, sems) = rest[:-4], rest[-4:]
    small = start_small((cols_in, counts_in), (cols, counts), sems)
    slots = values.shape[1]
    chunks = grads.shape[0]
    rows = values.shape[0] // chunks
    nodes = total.shape[2]
    width = nodes // chunks

    total[...] = jnp.zeros_like(total)
    weight_part = jnp.zeros((16, 256), F32)
    for j in range(chunks):
        at = slice(j * width, (j + 1) * width)
        activation[:16, at] = grads[j, :, width + 256 : 2 * width + 256]
        activation[16:, at] = grads[j, :, 2 * width + 256 :]
        weight_part += grads[j, :, width : width + 256].astype(F32)

    for copy in small:
        copy.wait()
    for j in range(chunks):
        for i in range(rows):
            r = j * rows + i
            count = counts[r]
            contrib = lax.dot_general(
                grads[j, :, i * BLOCK : (i + 1) * BLOCK],
                values[r].reshape(slots * BLOCK, BLOCK),
                (((1,), (1,)), ((), ())),
                preferred_element_type=F32,
            )
            for s in range(slots):
                group, lane = place_of(cols[s, r])
                group = jnp.where(s < count, group, 16)
                total[group, :, pl.ds(lane, BLOCK)] += contrib[:, s * BLOCK : (s + 1) * BLOCK]

    weight_part = weight_part.astype(BF)
    for server in range(2):
        nears = [node_near(*FARTHEST, server)]
        for steps in (SECOND, THIRD, FIRST):
            nears += pair_near(back(steps), server)
        nears[5:] = [nears[6], nears[5], node_near(0, 0, server)]
        for group in groups[server::2]:
            for k in range(group.shape[0]):
                near = nears.pop(0)
                group[k, :, :nodes] = total[near].astype(BF)
                group[k, :, nodes:] = weight_part


def both(own, other, k):
    return own[k].astype(F32) + other[k].astype(F32)


def pair_kernel(own, other, _, farthest, second, third, first, later):
    farthest[...] = both(own, other, 0).astype(BF)
    for q in range(2):
        second[q] = both(own, other, 1 + q).astype(BF)
        third[q] = both(own, other, 3 + q).astype(BF)
    first[...] = both(own, other, 5).astype(BF)


def merge_kernel(own, other, forwarded, first, stay):
    first[...] = (both(own, other, 0) + forwarded[...].astype(F32)).astype(BF)
    stay[...] = both(own, other, 1).astype(BF)


def hand_kernel(first, second, third, out):
    out[...] = (first[...].astype(F32) + second[1].astype(F32) + third[1].astype(F32)).astype(BF)


def last_kernel(stay, handed, first, second, third, grad_features, grad_weight):
    total = stay[...].astype(F32) + handed[...].astype(F32) + first[...].astype(F32)
    for piece in (second, third):
        total += piece[0].astype(F32)
    nodes = grad_features.shape[1]
    grad_features[...] = total[:, :nodes].astype(BF)
    grad_weight[...] = total[:, nodes:]


def local(features, weight, bias, block_values, block_cols, block_counts, train_mask, cotangent):
    fin, nodes = features.shape
    width = nodes // 8

    block_cols = pltpu.with_memory_space_constraint(block_cols.T, pltpu.HBM)
    block_counts = pltpu.with_memory_space_constraint(block_counts, pltpu.HBM)

    def shape(dims, kind=BF):
        return jax.ShapeDtypeStruct(dims, kind)

    swap = node_pairs(0, 0, 1)
    pieces = [features, lax.ppermute(features, "node", swap)]
    pair = features
    for at, shard in enumerate(pieces):
        pair = pl.pallas_call(
            functools.partial(place_kernel, at),
            in_specs=[ANY] * (1 + at),
            out_specs=ANY,
            out_shape=shape((2, fin, nodes)),
            scratch_shapes=[pltpu.SemaphoreType.DMA],
            input_output_aliases={1: 0} if at else {},
            compiler_params=params(4),
            name="place",
        )(*([shard, pair][: 1 + at]))

    def send(piece, steps):
        return lax.ppermute(piece, "node", shared_pairs(steps))

    first, second, third = (send(pair, steps) for steps in (FIRST, SECOND, THIRD))
    values, loaded = pl.pallas_call(
        load_kernel,
        in_specs=[pl.BlockSpec(memory_space=pltpu.HBM), ANY],
        out_specs=[VMEM, VMEM],
        out_shape=[pltpu.VMEM(block_values.shape, BF), shape((8, 128), F32)],
        scratch_shapes=[pltpu.SemaphoreType.DMA((8,))],
        compiler_params=params(4),
        cost_estimate=pl.CostEstimate(
            flops=0, bytes_accessed=2 * block_values.size * 2, transcendentals=0
        ),
        name="load",
    )(pltpu.with_memory_space_constraint(block_values, pltpu.HBM), pair)
    picked = pl.pallas_call(
        pick_kernel,
        in_specs=[VMEM, ANY],
        out_specs=VMEM,
        out_shape=shape((fin, nodes)),
        compiler_params=params(4),
        name="pick",
    )(first, loaded)
    forwarded = send(picked, FORWARD)
    for piece in (first, second, third, forwarded):
        pieces += [piece, lax.ppermute(piece, "node", swap)]

    index_scratch = [
        pltpu.SMEM(block_cols.shape, jnp.int32),
        pltpu.SMEM(block_counts.shape, jnp.int32),
        pltpu.SemaphoreType.DMA((2,)),
    ]
    mixed = pl.pallas_call(
        mix_kernel,
        in_specs=[HBM, HBM] + [VMEM] * 14,
        out_specs=VMEM,
        out_shape=shape((8, 16, 3 * width + 512)),
        scratch_shapes=[pltpu.VMEM((16, fin, nodes), BF)] + index_scratch,
        compiler_params=params(16),
        name="mix",
    )(block_cols, block_counts, values, cotangent, weight, bias[None, :], *pieces)

    both = lax.all_to_all(mixed, "feat", 0, 0, tiled=True)

    dense = pl.pallas_call(
        dense_kernel,
        in_specs=[VMEM] * 2,
        out_specs=VMEM,
        out_shape=shape((8, 16, 3 * width + 256)),
        compiler_params=params(16),
        name="dense",
    )(both, train_mask[None, :])

    grads = lax.all_to_all(dense, "feat", 0, 0, tiled=True)

    wide = nodes + 256
    activation, own1, other1, own2, other2 = pl.pallas_call(
        spread_kernel,
        in_specs=[HBM, HBM] + [VMEM] * 2,
        out_specs=[VMEM] * 5,
        out_shape=[shape((32, nodes))]
        + [shape((count, 16, wide)) for count in (6, 2) for _ in range(2)],
        scratch_shapes=[pltpu.VMEM((17, fin, nodes), F32)] + index_scratch,
        compiler_params=params(24),
        name="spread",
    )(block_cols, block_counts, values, grads)

    other1 = lax.ppermute(other1, "node", swap)
    farthest, second, third, first, other2 = pl.pallas_call(
        pair_kernel,
        in_specs=[VMEM, VMEM, ANY],
        out_specs=[VMEM] * 4 + [ANY],
        out_shape=[shape((16, wide))]
        + [shape((2, 16, wide))] * 2
        + [shape((16, wide)), shape((2, 16, wide))],
        input_output_aliases={2: 4},
        compiler_params=params(16),
        name="pair",
    )(own1, other1, other2)
    forwarded = send(farthest, back(FORWARD))
    second, third = send(second, back(SECOND)), send(third, back(THIRD))
    first = [send(first, back(FIRST))]
    other2 = lax.ppermute(other2, "node", swap)
    merged, stay = pl.pallas_call(
        merge_kernel,
        in_specs=[VMEM] * 3,
        out_specs=[VMEM] * 2,
        out_shape=[shape((16, wide))] * 2,
        compiler_params=params(16),
        name="merge",
    )(own2, other2, forwarded)
    first.append(send(merged, back(FIRST)))
    handed = pl.pallas_call(
        hand_kernel,
        in_specs=[VMEM] * 3,
        out_specs=VMEM,
        out_shape=shape((16, wide)),
        compiler_params=params(16),
        name="hand",
    )(first[0], second, third)
    handed = lax.ppermute(handed, "node", swap)
    grad_features, grad_weight = pl.pallas_call(
        last_kernel,
        in_specs=[VMEM] * 5,
        out_specs=[VMEM] * 2,
        out_shape=[shape((16, nodes)), shape((16, 256), F32)],
        compiler_params=params(16),
        name="last",
    )(stay, handed, first[1], second, third)
    return activation, grad_features, grad_weight


def solution(mesh):
    placed = (
        P("feat", "node"),
        P("feat", None),
        P("feat"),
        P("node", None, None, None),
        P("node", None),
        P("node"),
        P("node"),
        P("feat", "node"),
    )
    return jax.shard_map(
        local,
        mesh=mesh,
        in_specs=placed,
        out_specs=(P("feat", "node"), P("feat", "node"), P("feat", None)),
        check_vma=False,
    )
```

```python
import functools

import jax
import jax.numpy as jnp
from jax import lax
from jax.experimental import pallas as pl
from jax.experimental.pallas import tpu as pltpu
from jax.sharding import PartitionSpec as P

BF = jnp.bfloat16
F32 = jnp.float32
ANY = pl.BlockSpec(memory_space=pl.ANY)
HBM = pl.BlockSpec(memory_space=pltpu.HBM)
VMEM = pl.BlockSpec(memory_space=pltpu.VMEM)
FIRST = ((1, 0), (0, 2))
SECOND = ((1, 3), (1, 1))
THIRD = ((0, 3), (0, 1))
FORWARD = ((0, 2), (1, 0))
FARTHEST = (1, 2)
BLOCK = 128


def node_at(x, z, core):
    return (x * 4 + z) * 2 + core


def node_pairs(dx, dz, dcore=0):
    return [
        (node_at(x, z, c), node_at(x ^ dx, (z + dz) % 4, c ^ dcore))
        for x in range(2)
        for z in range(4)
        for c in range(2)
    ]


def node_near(dx, dz, dcore):
    me = lax.axis_index("node")
    x, z, c = me >> 3, (me >> 1) & 3, me & 1
    return ((x ^ dx) * 4 + ((z + dz) & 3)) * 2 + (c ^ dcore)


def shared_pairs(steps):
    return [
        (node_at(x, z, c), node_at(x ^ steps[c][0], (z + steps[c][1]) % 4, c))
        for x in range(2)
        for z in range(4)
        for c in range(2)
    ]


def back(steps):
    return tuple((dx, -dz % 4) for dx, dz in steps)


def shared_near(steps, server, dcore):
    core = (lax.axis_index("node") & 1) ^ server
    dx = jnp.where(core == 0, steps[0][0], steps[1][0])
    dz = jnp.where(core == 0, steps[0][1], steps[1][1])
    return node_near(dx, dz, dcore)


def pair_near(steps, server):
    return [shared_near(steps, server, server ^ q) for q in range(2)]


def place_of(column):
    group = lax.shift_right_logical(column * 21846, 20)
    return group, pl.multiple_of((column - group * 48) * BLOCK, BLOCK)


def params(mib):
    return pltpu.CompilerParams(vmem_limit_bytes=mib * 2**20)


def place_kernel(at, shard, *rest):
    out, sem = rest[-2:]
    copy = pltpu.make_async_copy(shard, out.at[at], sem)
    copy.start()
    copy.wait()


def pick_kernel(pair, _, out):
    out[...] = pair[0]


def load_kernel(values, *rest):
    out, loaded, sems = rest[-3:]
    count = sems.shape[0]
    rows = out.shape[0] // count
    copies = [
        pltpu.make_async_copy(
            values.at[pl.ds(i * rows, rows)], out.at[pl.ds(i * rows, rows)], sems.at[i]
        )
        for i in range(count)
    ]
    for copy in copies:
        copy.start()
    for copy in copies:
        copy.wait()
    loaded[...] = jnp.zeros_like(loaded)


def start_small(sources, places, sems):
    copies = [
        pltpu.make_async_copy(source, place, sems.at[at])
        for at, (source, place) in enumerate(zip(sources, places))
    ]
    for copy in copies:
        copy.start()
    return copies


def mix_kernel(cols_in, counts_in, values, cotangent, weight, bias, *rest):
    pieces, (out, held, cols, counts, sems) = rest[:10], rest[10:]
    small = start_small((cols_in, counts_in), (cols, counts), sems)
    slots = values.shape[1]
    chunks, _, _ = out.shape
    width = cotangent.shape[1] // chunks
    rows = values.shape[0] // chunks

    hidden = bias.shape[1]
    high = bias[...].astype(BF).astype(F32)
    middle = (bias[...] - high).astype(BF).astype(F32)
    row = lax.broadcasted_iota(jnp.int32, (16, hidden), 0)
    parts = jnp.where(row == 1, middle, jnp.where(row == 2, bias[...] - high - middle, 0.0))
    parts = jnp.where(row == 0, high, parts).astype(BF)
    place = lax.broadcasted_iota(jnp.int32, (hidden, 256), 1) - lax.axis_index("feat") * hidden
    place = place == lax.broadcasted_iota(jnp.int32, (hidden, 256), 0)
    bias_rows = jnp.dot(
        parts, jnp.where(place, 1.0, 0.0).astype(BF), preferred_element_type=F32
    ).astype(BF)

    first, second, third, farthest = (pieces[at : at + 2] for at in (2, 4, 6, 8))
    for server in range(2):
        held[node_near(0, 0, server)] = pieces[server][...]
        held[node_near(*FARTHEST, server)] = farthest[server][...]
        for shards, steps in ((first, FIRST), (second, SECOND), (third, THIRD)):
            for q, near in enumerate(pair_near(back(steps), server)):
                held[near] = shards[server][q]
    for j in range(chunks):
        out[j, :, width : 2 * width] = cotangent[:16, j * width : (j + 1) * width]
        out[j, :, 2 * width : 3 * width] = cotangent[16:, j * width : (j + 1) * width]
        out[j, :, 3 * width : 3 * width + 256] = weight[...]
        out[j, :, 3 * width + 256 :] = bias_rows

    for copy in small:
        copy.wait()
    for j in range(chunks):
        for i in range(rows):
            r = j * rows + i
            count = counts[r]
            parts = []
            for s in range(slots):
                group, lane = place_of(cols[s, r])
                block = held[group, :, pl.ds(lane, BLOCK)]
                parts.append(jnp.where(s < count, block, jnp.zeros_like(block)))
            total = jnp.dot(
                jnp.concatenate(parts, axis=1),
                values[r].reshape(slots * BLOCK, BLOCK),
                preferred_element_type=F32,
            )
            out[j, :, i * BLOCK : (i + 1) * BLOCK] = total.astype(BF)


def dense_kernel(both, mask, out):
    width = mask.shape[1] // 8
    mixed = both[:, :, :width].reshape(128, width)
    cotangent = jnp.concatenate(
        [both[:, :, width : 2 * width], both[:, :, 2 * width : 3 * width]], axis=1
    ).reshape(256, width)
    weight = both[:, :, 3 * width : 3 * width + 256].reshape(128, 256)
    bias_rows = both[:, :, 3 * width + 256 :].reshape(128, 256)
    kept = mask[:, pl.ds(pl.multiple_of(lax.axis_index("feat") * width, BLOCK), width)]
    preact = lax.dot_general(
        jnp.concatenate([weight, bias_rows], axis=0),
        jnp.concatenate([mixed, jnp.ones_like(mixed)], axis=0),
        (((0,), (0,)), ((), ())),
        preferred_element_type=F32,
    )
    sigma = jax.nn.sigmoid(preact)
    activation = (preact * sigma).astype(BF).reshape(8, 32, width)
    slope = sigma * (1.0 + preact * (1.0 - sigma))
    grad_pre = (cotangent.astype(F32) * kept.astype(F32) * slope).astype(BF)
    grad_mixed = jnp.dot(weight, grad_pre, preferred_element_type=F32)
    grad_weight = lax.dot_general(
        mixed, grad_pre, (((1,), (1,)), ((), ())), preferred_element_type=F32
    )
    out[:, :, :width] = grad_mixed.astype(BF).reshape(8, 16, width)
    out[:, :, width : width + 256] = grad_weight.astype(BF).reshape(8, 16, 256)
    out[:, :, width + 256 : 2 * width + 256] = activation[:, :16]
    out[:, :, 2 * width + 256 :] = activation[:, 16:]


def spread_kernel(
    cols_in, counts_in, values, grads, activation, *rest
):
    groups, (total, cols, counts, sems) = rest[:-4], rest[-4:]
    small = start_small((cols_in, counts_in), (cols, counts), sems)
    slots = values.shape[1]
    chunks = grads.shape[0]
    rows = values.shape[0] // chunks
    nodes = total.shape[2]
    width = nodes // chunks

    total[...] = jnp.zeros_like(total)
    weight_part = jnp.zeros((16, 256), F32)
    for j in range(chunks):
        at = slice(j * width, (j + 1) * width)
        activation[:16, at] = grads[j, :, width + 256 : 2 * width + 256]
        activation[16:, at] = grads[j, :, 2 * width + 256 :]
        weight_part += grads[j, :, width : width + 256].astype(F32)

    for copy in small:
        copy.wait()
    for j in range(chunks):
        for i in range(rows):
            r = j * rows + i
            count = counts[r]
            contrib = lax.dot_general(
                grads[j, :, i * BLOCK : (i + 1) * BLOCK],
                values[r].reshape(slots * BLOCK, BLOCK),
                (((1,), (1,)), ((), ())),
                preferred_element_type=F32,
            )
            for s in range(slots):
                group, lane = place_of(cols[s, r])
                group = jnp.where(s < count, group, 16)
                total[group, :, pl.ds(lane, BLOCK)] += contrib[:, s * BLOCK : (s + 1) * BLOCK]

    weight_part = weight_part.astype(BF)
    for server in range(2):
        nears = [node_near(*FARTHEST, server)]
        for steps in (SECOND, THIRD, FIRST):
            nears += pair_near(back(steps), server)
        nears.append(node_near(0, 0, server))
        for group in groups[server::2]:
            for k in range(group.shape[0]):
                near = nears.pop(0)
                group[k, :, :nodes] = total[near].astype(BF)
                group[k, :, nodes:] = weight_part


def both(own, other, k):
    return own[k].astype(F32) + other[k].astype(F32)


def pair_kernel(own, other, _, farthest, second, third, later):
    farthest[...] = both(own, other, 0).astype(BF)
    for q in range(2):
        second[q] = both(own, other, 1 + q).astype(BF)
        third[q] = both(own, other, 3 + q).astype(BF)


def merge_kernel(own, other, forwarded, first, stay):
    first[0] = (both(own, other, 0) + forwarded[...].astype(F32)).astype(BF)
    first[1] = both(own, other, 1).astype(BF)
    stay[...] = both(own, other, 2).astype(BF)


def hand_kernel(first, second, third, out):
    out[...] = (first[1].astype(F32) + second[1].astype(F32) + third[1].astype(F32)).astype(BF)


def last_kernel(stay, handed, first, second, third, grad_features, grad_weight):
    total = stay[...].astype(F32) + handed[...].astype(F32)
    for piece in (first, second, third):
        total += piece[0].astype(F32)
    nodes = grad_features.shape[1]
    grad_features[...] = total[:, :nodes].astype(BF)
    grad_weight[...] = total[:, nodes:]


def local(features, weight, bias, block_values, block_cols, block_counts, train_mask, cotangent):
    fin, nodes = features.shape
    width = nodes // 8

    block_cols = pltpu.with_memory_space_constraint(block_cols.T, pltpu.HBM)
    block_counts = pltpu.with_memory_space_constraint(block_counts, pltpu.HBM)

    def shape(dims, kind=BF):
        return jax.ShapeDtypeStruct(dims, kind)

    swap = node_pairs(0, 0, 1)
    pieces = [features, lax.ppermute(features, "node", swap)]
    pair = features
    for at, shard in enumerate(pieces):
        pair = pl.pallas_call(
            functools.partial(place_kernel, at),
            in_specs=[ANY] * (1 + at),
            out_specs=ANY,
            out_shape=shape((2, fin, nodes)),
            scratch_shapes=[pltpu.SemaphoreType.DMA],
            input_output_aliases={1: 0} if at else {},
            compiler_params=params(4),
            name="place",
        )(*([shard, pair][: 1 + at]))

    def send(piece, steps):
        return lax.ppermute(piece, "node", shared_pairs(steps))

    first, second, third = (send(pair, steps) for steps in (FIRST, SECOND, THIRD))
    values, loaded = pl.pallas_call(
        load_kernel,
        in_specs=[pl.BlockSpec(memory_space=pltpu.HBM), ANY],
        out_specs=[VMEM, VMEM],
        out_shape=[pltpu.VMEM(block_values.shape, BF), shape((8, 128), F32)],
        scratch_shapes=[pltpu.SemaphoreType.DMA((8,))],
        compiler_params=params(4),
        cost_estimate=pl.CostEstimate(
            flops=0, bytes_accessed=2 * block_values.size * 2, transcendentals=0
        ),
        name="load",
    )(pltpu.with_memory_space_constraint(block_values, pltpu.HBM), pair)
    picked = pl.pallas_call(
        pick_kernel,
        in_specs=[VMEM, ANY],
        out_specs=VMEM,
        out_shape=shape((fin, nodes)),
        compiler_params=params(4),
        name="pick",
    )(first, loaded)
    forwarded = send(picked, FORWARD)
    for piece in (first, second, third, forwarded):
        pieces += [piece, lax.ppermute(piece, "node", swap)]

    index_scratch = [
        pltpu.SMEM(block_cols.shape, jnp.int32),
        pltpu.SMEM(block_counts.shape, jnp.int32),
        pltpu.SemaphoreType.DMA((2,)),
    ]
    mixed = pl.pallas_call(
        mix_kernel,
        in_specs=[HBM, HBM] + [VMEM] * 14,
        out_specs=VMEM,
        out_shape=shape((8, 16, 3 * width + 512)),
        scratch_shapes=[pltpu.VMEM((16, fin, nodes), BF)] + index_scratch,
        compiler_params=params(16),
        name="mix",
    )(block_cols, block_counts, values, cotangent, weight, bias[None, :], *pieces)

    both = lax.all_to_all(mixed, "feat", 0, 0, tiled=True)

    dense = pl.pallas_call(
        dense_kernel,
        in_specs=[VMEM] * 2,
        out_specs=VMEM,
        out_shape=shape((8, 16, 3 * width + 256)),
        compiler_params=params(16),
        name="dense",
    )(both, train_mask[None, :])

    grads = lax.all_to_all(dense, "feat", 0, 0, tiled=True)

    wide = nodes + 256
    activation, own1, other1, own2, other2 = pl.pallas_call(
        spread_kernel,
        in_specs=[HBM, HBM] + [VMEM] * 2,
        out_specs=[VMEM] * 5,
        out_shape=[shape((32, nodes))]
        + [shape((count, 16, wide)) for count in (5, 3) for _ in range(2)],
        scratch_shapes=[pltpu.VMEM((17, fin, nodes), F32)] + index_scratch,
        compiler_params=params(24),
        name="spread",
    )(block_cols, block_counts, values, grads)

    other1 = lax.ppermute(other1, "node", swap)
    farthest, second, third, other2 = pl.pallas_call(
        pair_kernel,
        in_specs=[VMEM, VMEM, ANY],
        out_specs=[VMEM, VMEM, VMEM, ANY],
        out_shape=[shape((16, wide))] + [shape((2, 16, wide))] * 2 + [shape((3, 16, wide))],
        input_output_aliases={2: 3},
        compiler_params=params(16),
        name="pair",
    )(own1, other1, other2)
    forwarded = send(farthest, back(FORWARD))
    second, third = send(second, back(SECOND)), send(third, back(THIRD))
    other2 = lax.ppermute(other2, "node", swap)
    first, stay = pl.pallas_call(
        merge_kernel,
        in_specs=[VMEM] * 3,
        out_specs=[VMEM] * 2,
        out_shape=[shape((2, 16, wide)), shape((16, wide))],
        compiler_params=params(16),
        name="merge",
    )(own2, other2, forwarded)
    first = send(first, back(FIRST))
    handed = pl.pallas_call(
        hand_kernel,
        in_specs=[VMEM] * 3,
        out_specs=VMEM,
        out_shape=shape((16, wide)),
        compiler_params=params(16),
        name="hand",
    )(first, second, third)
    handed = lax.ppermute(handed, "node", swap)
    grad_features, grad_weight = pl.pallas_call(
        last_kernel,
        in_specs=[VMEM] * 5,
        out_specs=[VMEM] * 2,
        out_shape=[shape((16, nodes)), shape((16, 256), F32)],
        compiler_params=params(16),
        name="last",
    )(stay, handed, first, second, third)
    return activation, grad_features, grad_weight


def solution(mesh):
    placed = (
        P("feat", "node"),
        P("feat", None),
        P("feat"),
        P("node", None, None, None),
        P("node", None),
        P("node"),
        P("node"),
        P("feat", "node"),
    )
    return jax.shard_map(
        local,
        mesh=mesh,
        in_specs=placed,
        out_specs=(P("feat", "node"), P("feat", "node"), P("feat", None)),
        check_vma=False,
    )
```

```python
import functools

import jax
import jax.numpy as jnp
from jax import lax
from jax.experimental import pallas as pl
from jax.experimental.pallas import tpu as pltpu
from jax.sharding import PartitionSpec as P

BF = jnp.bfloat16
F32 = jnp.float32
ANY = pl.BlockSpec(memory_space=pl.ANY)
HBM = pl.BlockSpec(memory_space=pltpu.HBM)
VMEM = pl.BlockSpec(memory_space=pltpu.VMEM)
FIRST = ((1, 0), (0, 2))
SECOND = ((1, 3), (1, 1))
THIRD = ((0, 3), (0, 1))
FORWARD = ((0, 2), (1, 0))
FARTHEST = (1, 2)
BLOCK = 128


def node_at(x, z, core):
    return (x * 4 + z) * 2 + core


def node_pairs(dx, dz, dcore=0):
    return [
        (node_at(x, z, c), node_at(x ^ dx, (z + dz) % 4, c ^ dcore))
        for x in range(2)
        for z in range(4)
        for c in range(2)
    ]


def node_near(dx, dz, dcore):
    me = lax.axis_index("node")
    x, z, c = me >> 3, (me >> 1) & 3, me & 1
    return ((x ^ dx) * 4 + ((z + dz) & 3)) * 2 + (c ^ dcore)


def shared_pairs(steps):
    return [
        (node_at(x, z, c), node_at(x ^ steps[c][0], (z + steps[c][1]) % 4, c))
        for x in range(2)
        for z in range(4)
        for c in range(2)
    ]


def back(steps):
    return tuple((dx, -dz % 4) for dx, dz in steps)


def shared_near(steps, server, dcore):
    core = (lax.axis_index("node") & 1) ^ server
    dx = jnp.where(core == 0, steps[0][0], steps[1][0])
    dz = jnp.where(core == 0, steps[0][1], steps[1][1])
    return node_near(dx, dz, dcore)


def pair_near(steps, server):
    return [shared_near(steps, server, server ^ q) for q in range(2)]


def place_of(column):
    group = lax.shift_right_logical(column * 21846, 20)
    return group, pl.multiple_of((column - group * 48) * BLOCK, BLOCK)


def params(mib):
    return pltpu.CompilerParams(vmem_limit_bytes=mib * 2**20)


def place_kernel(at, shard, *rest):
    out, sem = rest[-2:]
    copy = pltpu.make_async_copy(shard, out.at[at], sem)
    copy.start()
    copy.wait()


def pick_kernel(pair, _, out):
    out[...] = pair[0]


def load_kernel(values, *rest):
    out, loaded, sems = rest[-3:]
    count = sems.shape[0]
    rows = out.shape[0] // count
    copies = [
        pltpu.make_async_copy(
            values.at[pl.ds(i * rows, rows)], out.at[pl.ds(i * rows, rows)], sems.at[i]
        )
        for i in range(count)
    ]
    for copy in copies:
        copy.start()
    for copy in copies:
        copy.wait()
    loaded[...] = jnp.zeros_like(loaded)


def start_small(sources, places, sems):
    copies = [
        pltpu.make_async_copy(source, place, sems.at[at])
        for at, (source, place) in enumerate(zip(sources, places))
    ]
    for copy in copies:
        copy.start()
    return copies


def mix_kernel(cols_in, counts_in, values, cotangent, weight, bias, *rest):
    pieces, (out, held, cols, counts, sems) = rest[:10], rest[10:]
    small = start_small((cols_in, counts_in), (cols, counts), sems)
    slots = values.shape[1]
    chunks, _, _ = out.shape
    width = cotangent.shape[1] // chunks
    rows = values.shape[0] // chunks

    hidden = bias.shape[1]
    high = bias[...].astype(BF).astype(F32)
    middle = (bias[...] - high).astype(BF).astype(F32)
    row = lax.broadcasted_iota(jnp.int32, (16, hidden), 0)
    parts = jnp.where(row == 1, middle, jnp.where(row == 2, bias[...] - high - middle, 0.0))
    parts = jnp.where(row == 0, high, parts).astype(BF)
    place = lax.broadcasted_iota(jnp.int32, (hidden, 256), 1) - lax.axis_index("feat") * hidden
    place = place == lax.broadcasted_iota(jnp.int32, (hidden, 256), 0)
    bias_rows = jnp.dot(
        parts, jnp.where(place, 1.0, 0.0).astype(BF), preferred_element_type=F32
    ).astype(BF)

    first, second, third, farthest = (pieces[at : at + 2] for at in (8, 4, 2, 6))
    for server in range(2):
        held[node_near(0, 0, server)] = pieces[server][...]
        held[node_near(*FARTHEST, server)] = farthest[server][...]
        for shards, steps in ((first, FIRST), (second, SECOND), (third, THIRD)):
            for q, near in enumerate(pair_near(back(steps), server)):
                held[near] = shards[server][q]
    for j in range(chunks):
        out[j, :, width : 2 * width] = cotangent[:16, j * width : (j + 1) * width]
        out[j, :, 2 * width : 3 * width] = cotangent[16:, j * width : (j + 1) * width]
        out[j, :, 3 * width : 3 * width + 256] = weight[...]
        out[j, :, 3 * width + 256 :] = bias_rows

    for copy in small:
        copy.wait()
    for j in range(chunks):
        for i in range(rows):
            r = j * rows + i
            count = counts[r]
            parts = []
            for s in range(slots):
                group, lane = place_of(cols[s, r])
                block = held[group, :, pl.ds(lane, BLOCK)]
                parts.append(jnp.where(s < count, block, jnp.zeros_like(block)))
            total = jnp.dot(
                jnp.concatenate(parts, axis=1),
                values[r].reshape(slots * BLOCK, BLOCK),
                preferred_element_type=F32,
            )
            out[j, :, i * BLOCK : (i + 1) * BLOCK] = total.astype(BF)


def dense_kernel(both, mask, out):
    width = mask.shape[1] // 8
    mixed = both[:, :, :width].reshape(128, width)
    cotangent = jnp.concatenate(
        [both[:, :, width : 2 * width], both[:, :, 2 * width : 3 * width]], axis=1
    ).reshape(256, width)
    weight = both[:, :, 3 * width : 3 * width + 256].reshape(128, 256)
    bias_rows = both[:, :, 3 * width + 256 :].reshape(128, 256)
    kept = mask[:, pl.ds(pl.multiple_of(lax.axis_index("feat") * width, BLOCK), width)]
    preact = lax.dot_general(
        jnp.concatenate([weight, bias_rows], axis=0),
        jnp.concatenate([mixed, jnp.ones_like(mixed)], axis=0),
        (((0,), (0,)), ((), ())),
        preferred_element_type=F32,
    )
    sigma = jax.nn.sigmoid(preact)
    activation = (preact * sigma).astype(BF).reshape(8, 32, width)
    slope = sigma * (1.0 + preact * (1.0 - sigma))
    grad_pre = (cotangent.astype(F32) * kept.astype(F32) * slope).astype(BF)
    grad_mixed = jnp.dot(weight, grad_pre, preferred_element_type=F32)
    grad_weight = lax.dot_general(
        mixed, grad_pre, (((1,), (1,)), ((), ())), preferred_element_type=F32
    )
    out[:, :, :width] = grad_mixed.astype(BF).reshape(8, 16, width)
    out[:, :, width : width + 256] = grad_weight.astype(BF).reshape(8, 16, 256)
    out[:, :, width + 256 : 2 * width + 256] = activation[:, :16]
    out[:, :, 2 * width + 256 :] = activation[:, 16:]


def spread_kernel(
    cols_in, counts_in, values, grads, activation, *rest
):
    groups, (total, cols, counts, sems) = rest[:-4], rest[-4:]
    small = start_small((cols_in, counts_in), (cols, counts), sems)
    slots = values.shape[1]
    chunks = grads.shape[0]
    rows = values.shape[0] // chunks
    nodes = total.shape[2]
    width = nodes // chunks

    total[...] = jnp.zeros_like(total)
    weight_part = jnp.zeros((16, 256), F32)
    for j in range(chunks):
        at = slice(j * width, (j + 1) * width)
        activation[:16, at] = grads[j, :, width + 256 : 2 * width + 256]
        activation[16:, at] = grads[j, :, 2 * width + 256 :]
        weight_part += grads[j, :, width : width + 256].astype(F32)

    for copy in small:
        copy.wait()
    for j in range(chunks):
        for i in range(rows):
            r = j * rows + i
            count = counts[r]
            contrib = lax.dot_general(
                grads[j, :, i * BLOCK : (i + 1) * BLOCK],
                values[r].reshape(slots * BLOCK, BLOCK),
                (((1,), (1,)), ((), ())),
                preferred_element_type=F32,
            )
            for s in range(slots):
                group, lane = place_of(cols[s, r])
                group = jnp.where(s < count, group, 16)
                total[group, :, pl.ds(lane, BLOCK)] += contrib[:, s * BLOCK : (s + 1) * BLOCK]

    weight_part = weight_part.astype(BF)
    for server in range(2):
        nears = [node_near(*FARTHEST, server)]
        for steps in (SECOND, THIRD, FIRST):
            nears += pair_near(back(steps), server)
        nears.append(node_near(0, 0, server))
        for group in groups[server::2]:
            for k in range(group.shape[0]):
                near = nears.pop(0)
                group[k, :, :nodes] = total[near].astype(BF)
                group[k, :, nodes:] = weight_part


def both(own, other, k):
    return own[k].astype(F32) + other[k].astype(F32)


def pair_kernel(own, other, _, farthest, second, third, later):
    farthest[...] = both(own, other, 0).astype(BF)
    for q in range(2):
        second[q] = both(own, other, 1 + q).astype(BF)
        third[q] = both(own, other, 3 + q).astype(BF)


def merge_kernel(own, other, forwarded, first, stay):
    first[0] = (both(own, other, 0) + forwarded[...].astype(F32)).astype(BF)
    first[1] = both(own, other, 1).astype(BF)
    stay[...] = both(own, other, 2).astype(BF)


def hand_kernel(first, second, third, out):
    out[...] = (first[1].astype(F32) + second[1].astype(F32) + third[1].astype(F32)).astype(BF)


def last_kernel(stay, handed, first, second, third, grad_features, grad_weight):
    total = stay[...].astype(F32) + handed[...].astype(F32)
    for piece in (first, second, third):
        total += piece[0].astype(F32)
    nodes = grad_features.shape[1]
    grad_features[...] = total[:, :nodes].astype(BF)
    grad_weight[...] = total[:, nodes:]


def local(features, weight, bias, block_values, block_cols, block_counts, train_mask, cotangent):
    fin, nodes = features.shape
    width = nodes // 8

    block_cols = pltpu.with_memory_space_constraint(block_cols.T, pltpu.HBM)
    block_counts = pltpu.with_memory_space_constraint(block_counts, pltpu.HBM)

    def shape(dims, kind=BF):
        return jax.ShapeDtypeStruct(dims, kind)

    swap = node_pairs(0, 0, 1)
    pieces = [features, lax.ppermute(features, "node", swap)]
    pair = features
    for at, shard in enumerate(pieces):
        pair = pl.pallas_call(
            functools.partial(place_kernel, at),
            in_specs=[ANY] * (1 + at),
            out_specs=ANY,
            out_shape=shape((2, fin, nodes)),
            scratch_shapes=[pltpu.SemaphoreType.DMA],
            input_output_aliases={1: 0} if at else {},
            compiler_params=params(4),
            name="place",
        )(*([shard, pair][: 1 + at]))

    def send(piece, steps):
        return lax.ppermute(piece, "node", shared_pairs(steps))

    first, second, third = (send(pair, steps) for steps in (FIRST, SECOND, THIRD))
    values, loaded = pl.pallas_call(
        load_kernel,
        in_specs=[pl.BlockSpec(memory_space=pltpu.HBM), ANY],
        out_specs=[VMEM, VMEM],
        out_shape=[pltpu.VMEM(block_values.shape, BF), shape((8, 128), F32)],
        scratch_shapes=[pltpu.SemaphoreType.DMA((8,))],
        compiler_params=params(4),
        cost_estimate=pl.CostEstimate(
            flops=0, bytes_accessed=2 * block_values.size * 2, transcendentals=0
        ),
        name="load",
    )(pltpu.with_memory_space_constraint(block_values, pltpu.HBM), pair)
    picked = pl.pallas_call(
        pick_kernel,
        in_specs=[VMEM, ANY],
        out_specs=VMEM,
        out_shape=shape((fin, nodes)),
        compiler_params=params(4),
        name="pick",
    )(first, loaded)
    forwarded = send(picked, FORWARD)
    for piece in (third, second, forwarded, first):
        pieces += [piece, lax.ppermute(piece, "node", swap)]

    index_scratch = [
        pltpu.SMEM(block_cols.shape, jnp.int32),
        pltpu.SMEM(block_counts.shape, jnp.int32),
        pltpu.SemaphoreType.DMA((2,)),
    ]
    mixed = pl.pallas_call(
        mix_kernel,
        in_specs=[HBM, HBM] + [VMEM] * 14,
        out_specs=VMEM,
        out_shape=shape((8, 16, 3 * width + 512)),
        scratch_shapes=[pltpu.VMEM((16, fin, nodes), BF)] + index_scratch,
        compiler_params=params(16),
        name="mix",
    )(block_cols, block_counts, values, cotangent, weight, bias[None, :], *pieces)

    both = lax.all_to_all(mixed, "feat", 0, 0, tiled=True)

    dense = pl.pallas_call(
        dense_kernel,
        in_specs=[VMEM] * 2,
        out_specs=VMEM,
        out_shape=shape((8, 16, 3 * width + 256)),
        compiler_params=params(16),
        name="dense",
    )(both, train_mask[None, :])

    grads = lax.all_to_all(dense, "feat", 0, 0, tiled=True)

    wide = nodes + 256
    activation, own1, other1, own2, other2 = pl.pallas_call(
        spread_kernel,
        in_specs=[HBM, HBM] + [VMEM] * 2,
        out_specs=[VMEM] * 5,
        out_shape=[shape((32, nodes))]
        + [shape((count, 16, wide)) for count in (5, 3) for _ in range(2)],
        scratch_shapes=[pltpu.VMEM((17, fin, nodes), F32)] + index_scratch,
        compiler_params=params(24),
        name="spread",
    )(block_cols, block_counts, values, grads)

    other1 = lax.ppermute(other1, "node", swap)
    farthest, second, third, other2 = pl.pallas_call(
        pair_kernel,
        in_specs=[VMEM, VMEM, ANY],
        out_specs=[VMEM, VMEM, VMEM, ANY],
        out_shape=[shape((16, wide))] + [shape((2, 16, wide))] * 2 + [shape((3, 16, wide))],
        input_output_aliases={2: 3},
        compiler_params=params(16),
        name="pair",
    )(own1, other1, other2)
    forwarded = send(farthest, back(FORWARD))
    second, third = send(second, back(SECOND)), send(third, back(THIRD))
    other2 = lax.ppermute(other2, "node", swap)
    first, stay = pl.pallas_call(
        merge_kernel,
        in_specs=[VMEM] * 3,
        out_specs=[VMEM] * 2,
        out_shape=[shape((2, 16, wide)), shape((16, wide))],
        compiler_params=params(16),
        name="merge",
    )(own2, other2, forwarded)
    first = send(first, back(FIRST))
    handed = pl.pallas_call(
        hand_kernel,
        in_specs=[VMEM] * 3,
        out_specs=VMEM,
        out_shape=shape((16, wide)),
        compiler_params=params(16),
        name="hand",
    )(first, second, third)
    handed = lax.ppermute(handed, "node", swap)
    grad_features, grad_weight = pl.pallas_call(
        last_kernel,
        in_specs=[VMEM] * 5,
        out_specs=[VMEM] * 2,
        out_shape=[shape((16, nodes)), shape((16, 256), F32)],
        compiler_params=params(16),
        name="last",
    )(stay, handed, first, second, third)
    return activation, grad_features, grad_weight


def solution(mesh):
    placed = (
        P("feat", "node"),
        P("feat", None),
        P("feat"),
        P("node", None, None, None),
        P("node", None),
        P("node"),
        P("node"),
        P("feat", "node"),
    )
    return jax.shard_map(
        local,
        mesh=mesh,
        in_specs=placed,
        out_specs=(P("feat", "node"), P("feat", "node"), P("feat", None)),
        check_vma=False,
    )
```

```python
import functools

import jax
import jax.numpy as jnp
from jax import lax
from jax.experimental import pallas as pl
from jax.experimental.pallas import tpu as pltpu
from jax.sharding import PartitionSpec as P

BF = jnp.bfloat16
F32 = jnp.float32
ANY = pl.BlockSpec(memory_space=pl.ANY)
HBM = pl.BlockSpec(memory_space=pltpu.HBM)
VMEM = pl.BlockSpec(memory_space=pltpu.VMEM)
FIRST = ((1, 0), (0, 2))
SECOND = ((1, 3), (1, 1))
THIRD = ((0, 3), (0, 1))
FORWARD = ((0, 2), (1, 0))
FARTHEST = (1, 2)
BLOCK = 128


def node_at(x, z, core):
    return (x * 4 + z) * 2 + core


def node_pairs(dx, dz, dcore=0):
    return [
        (node_at(x, z, c), node_at(x ^ dx, (z + dz) % 4, c ^ dcore))
        for x in range(2)
        for z in range(4)
        for c in range(2)
    ]


def node_near(dx, dz, dcore):
    me = lax.axis_index("node")
    x, z, c = me >> 3, (me >> 1) & 3, me & 1
    return ((x ^ dx) * 4 + ((z + dz) & 3)) * 2 + (c ^ dcore)


def shared_pairs(steps):
    return [
        (node_at(x, z, c), node_at(x ^ steps[c][0], (z + steps[c][1]) % 4, c))
        for x in range(2)
        for z in range(4)
        for c in range(2)
    ]


def back(steps):
    return tuple((dx, -dz % 4) for dx, dz in steps)


def shared_near(steps, server, dcore):
    core = (lax.axis_index("node") & 1) ^ server
    dx = jnp.where(core == 0, steps[0][0], steps[1][0])
    dz = jnp.where(core == 0, steps[0][1], steps[1][1])
    return node_near(dx, dz, dcore)


def pair_near(steps, server):
    return [shared_near(steps, server, server ^ q) for q in range(2)]


def place_of(column):
    group = lax.shift_right_logical(column * 21846, 20)
    return group, pl.multiple_of((column - group * 48) * BLOCK, BLOCK)


def params(mib):
    return pltpu.CompilerParams(vmem_limit_bytes=mib * 2**20)


def place_kernel(at, shard, *rest):
    out, sem = rest[-2:]
    copy = pltpu.make_async_copy(shard, out.at[at], sem)
    copy.start()
    copy.wait()


def pick_kernel(pair, _, out):
    out[...] = pair[0]


def load_kernel(values, *rest):
    out, loaded, sems = rest[-3:]
    count = sems.shape[0]
    rows = out.shape[0] // count
    copies = [
        pltpu.make_async_copy(
            values.at[pl.ds(i * rows, rows)], out.at[pl.ds(i * rows, rows)], sems.at[i]
        )
        for i in range(count)
    ]
    for copy in copies:
        copy.start()
    for copy in copies:
        copy.wait()
    loaded[...] = jnp.zeros_like(loaded)


def start_small(sources, places, sems):
    copies = [
        pltpu.make_async_copy(source, place, sems.at[at])
        for at, (source, place) in enumerate(zip(sources, places))
    ]
    for copy in copies:
        copy.start()
    return copies


def mix_kernel(cols_in, counts_in, values, cotangent, weight, bias, *rest):
    pieces, (out, held, cols, counts, sems) = rest[:10], rest[10:]
    small = start_small((cols_in, counts_in), (cols, counts), sems)
    slots = values.shape[1]
    chunks, _, _ = out.shape
    width = cotangent.shape[1] // chunks
    rows = values.shape[0] // chunks

    hidden = bias.shape[1]
    high = bias[...].astype(BF).astype(F32)
    middle = (bias[...] - high).astype(BF).astype(F32)
    row = lax.broadcasted_iota(jnp.int32, (16, hidden), 0)
    parts = jnp.where(row == 1, middle, jnp.where(row == 2, bias[...] - high - middle, 0.0))
    parts = jnp.where(row == 0, high, parts).astype(BF)
    place = lax.broadcasted_iota(jnp.int32, (hidden, 256), 1) - lax.axis_index("feat") * hidden
    place = place == lax.broadcasted_iota(jnp.int32, (hidden, 256), 0)
    bias_rows = jnp.dot(
        parts, jnp.where(place, 1.0, 0.0).astype(BF), preferred_element_type=F32
    ).astype(BF)

    first, second, third, farthest = (pieces[at : at + 2] for at in (8, 2, 4, 6))
    for server in range(2):
        held[node_near(0, 0, server)] = pieces[server][...]
        held[node_near(*FARTHEST, server)] = farthest[server][...]
        for shards, steps in ((first, FIRST), (second, SECOND), (third, THIRD)):
            for q, near in enumerate(pair_near(back(steps), server)):
                held[near] = shards[server][q]
    for j in range(chunks):
        out[j, :, width : 2 * width] = cotangent[:16, j * width : (j + 1) * width]
        out[j, :, 2 * width : 3 * width] = cotangent[16:, j * width : (j + 1) * width]
        out[j, :, 3 * width : 3 * width + 256] = weight[...]
        out[j, :, 3 * width + 256 :] = bias_rows

    for copy in small:
        copy.wait()
    for j in range(chunks):
        for i in range(rows):
            r = j * rows + i
            count = counts[r]
            parts = []
            for s in range(slots):
                group, lane = place_of(cols[s, r])
                block = held[group, :, pl.ds(lane, BLOCK)]
                parts.append(jnp.where(s < count, block, jnp.zeros_like(block)))
            total = jnp.dot(
                jnp.concatenate(parts, axis=1),
                values[r].reshape(slots * BLOCK, BLOCK),
                preferred_element_type=F32,
            )
            out[j, :, i * BLOCK : (i + 1) * BLOCK] = total.astype(BF)


def dense_kernel(both, mask, out):
    width = mask.shape[1] // 8
    mixed = both[:, :, :width].reshape(128, width)
    cotangent = jnp.concatenate(
        [both[:, :, width : 2 * width], both[:, :, 2 * width : 3 * width]], axis=1
    ).reshape(256, width)
    weight = both[:, :, 3 * width : 3 * width + 256].reshape(128, 256)
    bias_rows = both[:, :, 3 * width + 256 :].reshape(128, 256)
    kept = mask[:, pl.ds(pl.multiple_of(lax.axis_index("feat") * width, BLOCK), width)]
    preact = lax.dot_general(
        jnp.concatenate([weight, bias_rows], axis=0),
        jnp.concatenate([mixed, jnp.ones_like(mixed)], axis=0),
        (((0,), (0,)), ((), ())),
        preferred_element_type=F32,
    )
    sigma = jax.nn.sigmoid(preact)
    activation = (preact * sigma).astype(BF).reshape(8, 32, width)
    slope = sigma * (1.0 + preact * (1.0 - sigma))
    grad_pre = (cotangent.astype(F32) * kept.astype(F32) * slope).astype(BF)
    grad_mixed = jnp.dot(weight, grad_pre, preferred_element_type=F32)
    grad_weight = lax.dot_general(
        mixed, grad_pre, (((1,), (1,)), ((), ())), preferred_element_type=F32
    )
    out[:, :, :width] = grad_mixed.astype(BF).reshape(8, 16, width)
    out[:, :, width : width + 256] = grad_weight.astype(BF).reshape(8, 16, 256)
    out[:, :, width + 256 : 2 * width + 256] = activation[:, :16]
    out[:, :, 2 * width + 256 :] = activation[:, 16:]


def spread_kernel(
    cols_in, counts_in, values, grads, activation, *rest
):
    groups, (total, cols, counts, sems) = rest[:-4], rest[-4:]
    small = start_small((cols_in, counts_in), (cols, counts), sems)
    slots = values.shape[1]
    chunks = grads.shape[0]
    rows = values.shape[0] // chunks
    nodes = total.shape[2]
    width = nodes // chunks

    total[...] = jnp.zeros_like(total)
    weight_part = jnp.zeros((16, 256), F32)
    for j in range(chunks):
        at = slice(j * width, (j + 1) * width)
        activation[:16, at] = grads[j, :, width + 256 : 2 * width + 256]
        activation[16:, at] = grads[j, :, 2 * width + 256 :]
        weight_part += grads[j, :, width : width + 256].astype(F32)

    for copy in small:
        copy.wait()
    for j in range(chunks):
        for i in range(rows):
            r = j * rows + i
            count = counts[r]
            contrib = lax.dot_general(
                grads[j, :, i * BLOCK : (i + 1) * BLOCK],
                values[r].reshape(slots * BLOCK, BLOCK),
                (((1,), (1,)), ((), ())),
                preferred_element_type=F32,
            )
            for s in range(slots):
                group, lane = place_of(cols[s, r])
                group = jnp.where(s < count, group, 16)
                total[group, :, pl.ds(lane, BLOCK)] += contrib[:, s * BLOCK : (s + 1) * BLOCK]

    weight_part = weight_part.astype(BF)
    for server in range(2):
        nears = [node_near(*FARTHEST, server)]
        for steps in (SECOND, THIRD, FIRST):
            nears += pair_near(back(steps), server)
        nears.append(node_near(0, 0, server))
        for group in groups[server::2]:
            for k in range(group.shape[0]):
                near = nears.pop(0)
                group[k, :, :nodes] = total[near].astype(BF)
                group[k, :, nodes:] = weight_part


def both(own, other, k):
    return own[k].astype(F32) + other[k].astype(F32)


def pair_kernel(own, other, _, farthest, second, third, later):
    farthest[...] = both(own, other, 0).astype(BF)
    for q in range(2):
        second[q] = both(own, other, 1 + q).astype(BF)
        third[q] = both(own, other, 3 + q).astype(BF)


def merge_kernel(own, other, forwarded, first, stay):
    first[0] = (both(own, other, 0) + forwarded[...].astype(F32)).astype(BF)
    first[1] = both(own, other, 1).astype(BF)
    stay[...] = both(own, other, 2).astype(BF)


def hand_kernel(first, second, third, out):
    out[...] = (first[1].astype(F32) + second[1].astype(F32) + third[1].astype(F32)).astype(BF)


def last_kernel(stay, handed, first, second, third, grad_features, grad_weight):
    total = stay[...].astype(F32) + handed[...].astype(F32)
    for piece in (first, second, third):
        total += piece[0].astype(F32)
    nodes = grad_features.shape[1]
    grad_features[...] = total[:, :nodes].astype(BF)
    grad_weight[...] = total[:, nodes:]


def local(features, weight, bias, block_values, block_cols, block_counts, train_mask, cotangent):
    fin, nodes = features.shape
    width = nodes // 8

    block_cols = pltpu.with_memory_space_constraint(block_cols.T, pltpu.HBM)
    block_counts = pltpu.with_memory_space_constraint(block_counts, pltpu.HBM)

    def shape(dims, kind=BF):
        return jax.ShapeDtypeStruct(dims, kind)

    swap = node_pairs(0, 0, 1)
    pieces = [features, lax.ppermute(features, "node", swap)]
    pair = features
    for at, shard in enumerate(pieces):
        pair = pl.pallas_call(
            functools.partial(place_kernel, at),
            in_specs=[ANY] * (1 + at),
            out_specs=ANY,
            out_shape=shape((2, fin, nodes)),
            scratch_shapes=[pltpu.SemaphoreType.DMA],
            input_output_aliases={1: 0} if at else {},
            compiler_params=params(4),
            name="place",
        )(*([shard, pair][: 1 + at]))

    def send(piece, steps):
        return lax.ppermute(piece, "node", shared_pairs(steps))

    first, second, third = (send(pair, steps) for steps in (FIRST, SECOND, THIRD))
    values, loaded = pl.pallas_call(
        load_kernel,
        in_specs=[pl.BlockSpec(memory_space=pltpu.HBM), ANY],
        out_specs=[VMEM, VMEM],
        out_shape=[pltpu.VMEM(block_values.shape, BF), shape((8, 128), F32)],
        scratch_shapes=[pltpu.SemaphoreType.DMA((8,))],
        compiler_params=params(4),
        cost_estimate=pl.CostEstimate(
            flops=0, bytes_accessed=2 * block_values.size * 2, transcendentals=0
        ),
        name="load",
    )(pltpu.with_memory_space_constraint(block_values, pltpu.HBM), pair)
    picked = pl.pallas_call(
        pick_kernel,
        in_specs=[VMEM, ANY],
        out_specs=VMEM,
        out_shape=shape((fin, nodes)),
        compiler_params=params(4),
        name="pick",
    )(first, loaded)
    forwarded = send(picked, FORWARD)
    for piece in (second, third, forwarded, first):
        pieces += [piece, lax.ppermute(piece, "node", swap)]

    index_scratch = [
        pltpu.SMEM(block_cols.shape, jnp.int32),
        pltpu.SMEM(block_counts.shape, jnp.int32),
        pltpu.SemaphoreType.DMA((2,)),
    ]
    mixed = pl.pallas_call(
        mix_kernel,
        in_specs=[HBM, HBM] + [VMEM] * 14,
        out_specs=VMEM,
        out_shape=shape((8, 16, 3 * width + 512)),
        scratch_shapes=[pltpu.VMEM((16, fin, nodes), BF)] + index_scratch,
        compiler_params=params(16),
        name="mix",
    )(block_cols, block_counts, values, cotangent, weight, bias[None, :], *pieces)

    both = lax.all_to_all(mixed, "feat", 0, 0, tiled=True)

    dense = pl.pallas_call(
        dense_kernel,
        in_specs=[VMEM] * 2,
        out_specs=VMEM,
        out_shape=shape((8, 16, 3 * width + 256)),
        compiler_params=params(16),
        name="dense",
    )(both, train_mask[None, :])

    grads = lax.all_to_all(dense, "feat", 0, 0, tiled=True)

    wide = nodes + 256
    activation, own1, other1, own2, other2 = pl.pallas_call(
        spread_kernel,
        in_specs=[HBM, HBM] + [VMEM] * 2,
        out_specs=[VMEM] * 5,
        out_shape=[shape((32, nodes))]
        + [shape((count, 16, wide)) for count in (5, 3) for _ in range(2)],
        scratch_shapes=[pltpu.VMEM((17, fin, nodes), F32)] + index_scratch,
        compiler_params=params(24),
        name="spread",
    )(block_cols, block_counts, values, grads)

    other1 = lax.ppermute(other1, "node", swap)
    farthest, second, third, other2 = pl.pallas_call(
        pair_kernel,
        in_specs=[VMEM, VMEM, ANY],
        out_specs=[VMEM, VMEM, VMEM, ANY],
        out_shape=[shape((16, wide))] + [shape((2, 16, wide))] * 2 + [shape((3, 16, wide))],
        input_output_aliases={2: 3},
        compiler_params=params(16),
        name="pair",
    )(own1, other1, other2)
    forwarded = send(farthest, back(FORWARD))
    second, third = send(second, back(SECOND)), send(third, back(THIRD))
    other2 = lax.ppermute(other2, "node", swap)
    first, stay = pl.pallas_call(
        merge_kernel,
        in_specs=[VMEM] * 3,
        out_specs=[VMEM] * 2,
        out_shape=[shape((2, 16, wide)), shape((16, wide))],
        compiler_params=params(16),
        name="merge",
    )(own2, other2, forwarded)
    first = send(first, back(FIRST))
    handed = pl.pallas_call(
        hand_kernel,
        in_specs=[VMEM] * 3,
        out_specs=VMEM,
        out_shape=shape((16, wide)),
        compiler_params=params(16),
        name="hand",
    )(first, second, third)
    handed = lax.ppermute(handed, "node", swap)
    grad_features, grad_weight = pl.pallas_call(
        last_kernel,
        in_specs=[VMEM] * 5,
        out_specs=[VMEM] * 2,
        out_shape=[shape((16, nodes)), shape((16, 256), F32)],
        compiler_params=params(16),
        name="last",
    )(stay, handed, first, second, third)
    return activation, grad_features, grad_weight


def solution(mesh):
    placed = (
        P("feat", "node"),
        P("feat", None),
        P("feat"),
        P("node", None, None, None),
        P("node", None),
        P("node"),
        P("node"),
        P("feat", "node"),
    )
    return jax.shard_map(
        local,
        mesh=mesh,
        in_specs=placed,
        out_specs=(P("feat", "node"), P("feat", "node"), P("feat", None)),
        check_vma=False,
    )
```

```python
import functools

import jax
import jax.numpy as jnp
from jax import lax
from jax.experimental import pallas as pl
from jax.experimental.pallas import tpu as pltpu
from jax.sharding import PartitionSpec as P

BF = jnp.bfloat16
F32 = jnp.float32
ANY = pl.BlockSpec(memory_space=pl.ANY)
HBM = pl.BlockSpec(memory_space=pltpu.HBM)
VMEM = pl.BlockSpec(memory_space=pltpu.VMEM)
FIRST = ((1, 0), (0, 2))
SECOND = ((1, 3), (1, 1))
THIRD = ((0, 3), (0, 1))
FORWARD = ((0, 2), (1, 0))
FARTHEST = (1, 2)
BLOCK = 128


def node_at(x, z, core):
    return (x * 4 + z) * 2 + core


def node_pairs(dx, dz, dcore=0):
    return [
        (node_at(x, z, c), node_at(x ^ dx, (z + dz) % 4, c ^ dcore))
        for x in range(2)
        for z in range(4)
        for c in range(2)
    ]


def node_near(dx, dz, dcore):
    me = lax.axis_index("node")
    x, z, c = me >> 3, (me >> 1) & 3, me & 1
    return ((x ^ dx) * 4 + ((z + dz) & 3)) * 2 + (c ^ dcore)


def shared_pairs(steps):
    return [
        (node_at(x, z, c), node_at(x ^ steps[c][0], (z + steps[c][1]) % 4, c))
        for x in range(2)
        for z in range(4)
        for c in range(2)
    ]


def back(steps):
    return tuple((dx, -dz % 4) for dx, dz in steps)


def shared_near(steps, server, dcore):
    core = (lax.axis_index("node") & 1) ^ server
    dx = jnp.where(core == 0, steps[0][0], steps[1][0])
    dz = jnp.where(core == 0, steps[0][1], steps[1][1])
    return node_near(dx, dz, dcore)


def pair_near(steps, server):
    return [shared_near(steps, server, server ^ q) for q in range(2)]


def place_of(column):
    group = lax.shift_right_logical(column * 21846, 20)
    return group, pl.multiple_of((column - group * 48) * BLOCK, BLOCK)


def params(mib):
    return pltpu.CompilerParams(vmem_limit_bytes=mib * 2**20)


def place_kernel(at, shard, *rest):
    out, sem = rest[-2:]
    copy = pltpu.make_async_copy(shard, out.at[at], sem)
    copy.start()
    copy.wait()


def pick_kernel(pair, _, out):
    out[...] = pair[0]


def load_kernel(values, *rest):
    out, loaded, sems = rest[-3:]
    count = sems.shape[0]
    rows = out.shape[0] // count
    copies = [
        pltpu.make_async_copy(
            values.at[pl.ds(i * rows, rows)], out.at[pl.ds(i * rows, rows)], sems.at[i]
        )
        for i in range(count)
    ]
    for copy in copies:
        copy.start()
    for copy in copies:
        copy.wait()
    loaded[...] = jnp.zeros_like(loaded)


def start_small(sources, places, sems):
    copies = [
        pltpu.make_async_copy(source, place, sems.at[at])
        for at, (source, place) in enumerate(zip(sources, places))
    ]
    for copy in copies:
        copy.start()
    return copies


def mix_kernel(cols_in, counts_in, values, cotangent, weight, bias, *rest):
    pieces, (out, held, cols, counts, sems) = rest[:10], rest[10:]
    small = start_small((cols_in, counts_in), (cols, counts), sems)
    slots = values.shape[1]
    chunks, _, _ = out.shape
    width = cotangent.shape[1] // chunks
    rows = values.shape[0] // chunks

    hidden = bias.shape[1]
    high = bias[...].astype(BF).astype(F32)
    middle = (bias[...] - high).astype(BF).astype(F32)
    row = lax.broadcasted_iota(jnp.int32, (16, hidden), 0)
    parts = jnp.where(row == 1, middle, jnp.where(row == 2, bias[...] - high - middle, 0.0))
    parts = jnp.where(row == 0, high, parts).astype(BF)
    place = lax.broadcasted_iota(jnp.int32, (hidden, 256), 1) - lax.axis_index("feat") * hidden
    place = place == lax.broadcasted_iota(jnp.int32, (hidden, 256), 0)
    bias_rows = jnp.dot(
        parts, jnp.where(place, 1.0, 0.0).astype(BF), preferred_element_type=F32
    ).astype(BF)

    first, second, third, farthest = (pieces[at : at + 2] for at in (2, 4, 6, 8))
    for server in range(2):
        held[node_near(0, 0, server)] = pieces[server][...]
        held[node_near(*FARTHEST, server)] = farthest[server][...]
        for shards, steps in ((first, FIRST), (second, SECOND), (third, THIRD)):
            for q, near in enumerate(pair_near(back(steps), server)):
                held[near] = shards[server][q]
    for j in range(chunks):
        out[j, :, width : 2 * width] = cotangent[:16, j * width : (j + 1) * width]
        out[j, :, 2 * width : 3 * width] = cotangent[16:, j * width : (j + 1) * width]
        out[j, :, 3 * width : 3 * width + 256] = weight[...]
        out[j, :, 3 * width + 256 :] = bias_rows

    for copy in small:
        copy.wait()
    for j in range(chunks):
        for i in range(rows):
            r = j * rows + i
            count = counts[r]
            parts = []
            for s in range(slots):
                group, lane = place_of(cols[s, r])
                block = held[group, :, pl.ds(lane, BLOCK)]
                parts.append(jnp.where(s < count, block, jnp.zeros_like(block)))
            total = jnp.dot(
                jnp.concatenate(parts, axis=1),
                values[r].reshape(slots * BLOCK, BLOCK),
                preferred_element_type=F32,
            )
            out[j, :, i * BLOCK : (i + 1) * BLOCK] = total.astype(BF)


def dense_kernel(both, mask, out):
    width = mask.shape[1] // 8
    mixed = both[:, :, :width].reshape(128, width)
    cotangent = jnp.concatenate(
        [both[:, :, width : 2 * width], both[:, :, 2 * width : 3 * width]], axis=1
    ).reshape(256, width)
    weight = both[:, :, 3 * width : 3 * width + 256].reshape(128, 256)
    bias_rows = both[:, :, 3 * width + 256 :].reshape(128, 256)
    kept = mask[:, pl.ds(pl.multiple_of(lax.axis_index("feat") * width, BLOCK), width)]
    preact = lax.dot_general(
        jnp.concatenate([weight, bias_rows], axis=0),
        jnp.concatenate([mixed, jnp.ones_like(mixed)], axis=0),
        (((0,), (0,)), ((), ())),
        preferred_element_type=F32,
    )
    sigma = jax.nn.sigmoid(preact)
    activation = (preact * sigma).astype(BF).reshape(8, 32, width)
    slope = sigma * (1.0 + preact * (1.0 - sigma))
    grad_pre = (cotangent.astype(F32) * kept.astype(F32) * slope).astype(BF)
    grad_mixed = jnp.dot(weight, grad_pre, preferred_element_type=F32)
    grad_weight = lax.dot_general(
        mixed, grad_pre, (((1,), (1,)), ((), ())), preferred_element_type=F32
    )
    out[:, :, :width] = grad_mixed.astype(BF).reshape(8, 16, width)
    out[:, :, width : width + 256] = grad_weight.astype(BF).reshape(8, 16, 256)
    out[:, :, width + 256 : 2 * width + 256] = activation[:, :16]
    out[:, :, 2 * width + 256 :] = activation[:, 16:]


def spread_kernel(
    cols_in, counts_in, values, grads, activation, *rest
):
    groups, (total, cols, counts, sems) = rest[:-4], rest[-4:]
    small = start_small((cols_in, counts_in), (cols, counts), sems)
    slots = values.shape[1]
    chunks = grads.shape[0]
    rows = values.shape[0] // chunks
    nodes = total.shape[2]
    width = nodes // chunks

    total[...] = jnp.zeros_like(total)
    weight_part = jnp.zeros((16, 256), F32)
    for j in range(chunks):
        at = slice(j * width, (j + 1) * width)
        activation[:16, at] = grads[j, :, width + 256 : 2 * width + 256]
        activation[16:, at] = grads[j, :, 2 * width + 256 :]
        weight_part += grads[j, :, width : width + 256].astype(F32)

    for copy in small:
        copy.wait()
    for j in range(chunks):
        for i in range(rows):
            r = j * rows + i
            count = counts[r]
            contrib = lax.dot_general(
                grads[j, :, i * BLOCK : (i + 1) * BLOCK],
                values[r].reshape(slots * BLOCK, BLOCK),
                (((1,), (1,)), ((), ())),
                preferred_element_type=F32,
            )
            for s in range(slots):
                group, lane = place_of(cols[s, r])
                group = jnp.where(s < count, group, 16)
                total[group, :, pl.ds(lane, BLOCK)] += contrib[:, s * BLOCK : (s + 1) * BLOCK]

    weight_part = weight_part.astype(BF)
    for server in range(2):
        nears = [node_near(*FARTHEST, server)]
        for steps in (SECOND, THIRD, FIRST):
            nears += pair_near(back(steps), server)
        nears.append(node_near(0, 0, server))
        for group in groups[server::2]:
            for k in range(group.shape[0]):
                near = nears.pop(0)
                group[k, :, :nodes] = total[near].astype(BF)
                group[k, :, nodes:] = weight_part


def both(own, other, k):
    return own[k].astype(F32) + other[k].astype(F32)


def pair_kernel(own, other, _, farthest, second, third, later):
    farthest[...] = both(own, other, 0).astype(BF)
    for q in range(2):
        second[q] = both(own, other, 1 + q).astype(BF)
        third[q] = both(own, other, 3 + q).astype(BF)


def merge_kernel(own, other, forwarded, first, stay):
    first[0] = (both(own, other, 0) + forwarded[...].astype(F32)).astype(BF)
    first[1] = both(own, other, 1).astype(BF)
    stay[...] = both(own, other, 2).astype(BF)


def hand_kernel(first, third, second, out):
    out[...] = (first[1].astype(F32) + second[1].astype(F32) + third[1].astype(F32)).astype(BF)


def last_kernel(stay, handed, first, second, third, grad_features, grad_weight):
    total = stay[...].astype(F32) + handed[...].astype(F32)
    for piece in (first, second, third):
        total += piece[0].astype(F32)
    nodes = grad_features.shape[1]
    grad_features[...] = total[:, :nodes].astype(BF)
    grad_weight[...] = total[:, nodes:]


def local(features, weight, bias, block_values, block_cols, block_counts, train_mask, cotangent):
    fin, nodes = features.shape
    width = nodes // 8

    block_cols = pltpu.with_memory_space_constraint(block_cols.T, pltpu.HBM)
    block_counts = pltpu.with_memory_space_constraint(block_counts, pltpu.HBM)

    def shape(dims, kind=BF):
        return jax.ShapeDtypeStruct(dims, kind)

    swap = node_pairs(0, 0, 1)
    pieces = [features, lax.ppermute(features, "node", swap)]
    pair = features
    for at, shard in enumerate(pieces):
        pair = pl.pallas_call(
            functools.partial(place_kernel, at),
            in_specs=[ANY] * (1 + at),
            out_specs=ANY,
            out_shape=shape((2, fin, nodes)),
            scratch_shapes=[pltpu.SemaphoreType.DMA],
            input_output_aliases={1: 0} if at else {},
            compiler_params=params(4),
            name="place",
        )(*([shard, pair][: 1 + at]))

    def send(piece, steps):
        return lax.ppermute(piece, "node", shared_pairs(steps))

    first, second, third = (send(pair, steps) for steps in (FIRST, SECOND, THIRD))
    values, loaded = pl.pallas_call(
        load_kernel,
        in_specs=[pl.BlockSpec(memory_space=pltpu.HBM), ANY],
        out_specs=[VMEM, VMEM],
        out_shape=[pltpu.VMEM(block_values.shape, BF), shape((8, 128), F32)],
        scratch_shapes=[pltpu.SemaphoreType.DMA((8,))],
        compiler_params=params(4),
        cost_estimate=pl.CostEstimate(
            flops=0, bytes_accessed=2 * block_values.size * 2, transcendentals=0
        ),
        name="load",
    )(pltpu.with_memory_space_constraint(block_values, pltpu.HBM), pair)
    picked = pl.pallas_call(
        pick_kernel,
        in_specs=[VMEM, ANY],
        out_specs=VMEM,
        out_shape=shape((fin, nodes)),
        compiler_params=params(4),
        name="pick",
    )(first, loaded)
    forwarded = send(picked, FORWARD)
    for piece in (first, second, third, forwarded):
        pieces += [piece, lax.ppermute(piece, "node", swap)]

    index_scratch = [
        pltpu.SMEM(block_cols.shape, jnp.int32),
        pltpu.SMEM(block_counts.shape, jnp.int32),
        pltpu.SemaphoreType.DMA((2,)),
    ]
    mixed = pl.pallas_call(
        mix_kernel,
        in_specs=[HBM, HBM] + [VMEM] * 14,
        out_specs=VMEM,
        out_shape=shape((8, 16, 3 * width + 512)),
        scratch_shapes=[pltpu.VMEM((16, fin, nodes), BF)] + index_scratch,
        compiler_params=params(16),
        name="mix",
    )(block_cols, block_counts, values, cotangent, weight, bias[None, :], *pieces)

    both = lax.all_to_all(mixed, "feat", 0, 0, tiled=True)

    dense = pl.pallas_call(
        dense_kernel,
        in_specs=[VMEM] * 2,
        out_specs=VMEM,
        out_shape=shape((8, 16, 3 * width + 256)),
        compiler_params=params(16),
        name="dense",
    )(both, train_mask[None, :])

    grads = lax.all_to_all(dense, "feat", 0, 0, tiled=True)

    wide = nodes + 256
    activation, own1, other1, own2, other2 = pl.pallas_call(
        spread_kernel,
        in_specs=[HBM, HBM] + [VMEM] * 2,
        out_specs=[VMEM] * 5,
        out_shape=[shape((32, nodes))]
        + [shape((count, 16, wide)) for count in (5, 3) for _ in range(2)],
        scratch_shapes=[pltpu.VMEM((17, fin, nodes), F32)] + index_scratch,
        compiler_params=params(24),
        name="spread",
    )(block_cols, block_counts, values, grads)

    other1 = lax.ppermute(other1, "node", swap)
    farthest, second, third, other2 = pl.pallas_call(
        pair_kernel,
        in_specs=[VMEM, VMEM, ANY],
        out_specs=[VMEM, VMEM, VMEM, ANY],
        out_shape=[shape((16, wide))] + [shape((2, 16, wide))] * 2 + [shape((3, 16, wide))],
        input_output_aliases={2: 3},
        compiler_params=params(16),
        name="pair",
    )(own1, other1, other2)
    forwarded = send(farthest, back(FORWARD))
    second, third = send(second, back(SECOND)), send(third, back(THIRD))
    other2 = lax.ppermute(other2, "node", swap)
    first, stay = pl.pallas_call(
        merge_kernel,
        in_specs=[VMEM] * 3,
        out_specs=[VMEM] * 2,
        out_shape=[shape((2, 16, wide)), shape((16, wide))],
        compiler_params=params(16),
        name="merge",
    )(own2, other2, forwarded)
    first = send(first, back(FIRST))
    handed = pl.pallas_call(
        hand_kernel,
        in_specs=[VMEM] * 3,
        out_specs=VMEM,
        out_shape=shape((16, wide)),
        compiler_params=params(16),
        name="hand",
    )(first, third, second)
    handed = lax.ppermute(handed, "node", swap)
    grad_features, grad_weight = pl.pallas_call(
        last_kernel,
        in_specs=[VMEM] * 5,
        out_specs=[VMEM] * 2,
        out_shape=[shape((16, nodes)), shape((16, 256), F32)],
        compiler_params=params(16),
        name="last",
    )(stay, handed, first, second, third)
    return activation, grad_features, grad_weight


def solution(mesh):
    placed = (
        P("feat", "node"),
        P("feat", None),
        P("feat"),
        P("node", None, None, None),
        P("node", None),
        P("node"),
        P("node"),
        P("feat", "node"),
    )
    return jax.shard_map(
        local,
        mesh=mesh,
        in_specs=placed,
        out_specs=(P("feat", "node"), P("feat", "node"), P("feat", None)),
        check_vma=False,
    )
```
